512 devices in a mesh: ctx: 64 (over x, z), ch: 8 (over y, core).
Axes of the slice: x: 4, y: 4, z: 16, core: 2. Of those that a mesh axis runs over, the one named last changes fastest.
Arguments:
- x_in: bfloat16 [8192, 8192], P('ctx', 'ch'), may hold values from -6 to 6
- gate_in: bfloat16 [8192, 8192], P('ctx', 'ch'), may hold values from -6 to 6
- conv_weight: float32 [4, 8192], P(None, 'ch'), may hold values from -3 to 3
- conv_bias: float32 [8192], P('ch'), may hold values from -3 to 3
- proj_low: bfloat16 [8192, 256], P('ch'), may hold values from -0.0625 to 0.0625
- proj_bc: bfloat16 [8192, 32], P('ch'), may hold values from -0.0625 to 0.0625
- dt_weight: bfloat16 [256, 8192], P(None, 'ch'), may hold values from -0.375 to 0.375
- dt_bias: float32 [8192], P('ch'), may hold values from -5 to -3
- decay_log: float32 [16, 8192], P(None, 'ch'), may hold values from -20 to 1.5
- skip_gain: float32 [8192], P('ch'), may hold values from 0.5 to 1.5
- attn_kv: bfloat16 [8192, 2048], P('ctx', 'ch'), may hold values from -6 to 6
- kept_index: int32 [8, 2048], P('ch', 'ctx'), may hold values from 0 to 8191, as said below
- kept_owner: int32 [8, 2048, 1], P('ch', 'ctx'), may hold values from 0 to 63; in each aligned block of 32 rows (0 to 31, 32 to 63, ..., all dimensions but the last counted through in order) at most 2 rows name the same one
Outputs:
- gated: bfloat16 [8192, 8192], P('ctx', 'ch')
- kept_cache: bfloat16 [8, 8192, 256], P('ch', 'ctx')
The draws below stay inside these ranges and needn't reach their ends.
Inputs may be any that keep to these rules, and one draw needn't show every extreme that they name: `kept_index`: for head h, the block of entries i * 32 to (i + 1) * 32 - 1 holds distinct increasing positions in [i * 128, (i + 1) * 128) and always holds (i + 1) * 128 - 1. `kept_owner`: in each aligned block of 32 entries of a head no owner appears more than 2 times.
All inputs are finite; a program needn't handle non-finite values.
Results may differ from the reference program's by a relative error of at most 0.0062.
Values may be sent and summed in bfloat16 or wider, within the bound.
A program may use at most 64 MiB of HBM per device.

```python
import math
import jax
import jax.numpy as jnp
import numpy as np
from jax import lax

INNER = 8192
STATE = 16
CONV = 4
DT_RANK = 256
HEADS = 8
HEAD_DIM = 128
TOK_DEV = 128
TOKENS = 8192
KEEP_DEV = 32
MOST = 2
KEPT = 2048
N_CTX = 64


def draw_decay_log(key, part):
    key = jax.random.fold_in(key, 5)
    pick_key, slow_key, fast_key = jax.random.split(key, 3)
    slow_share = 0.5
    chooser = jax.random.uniform(pick_key, (1, INNER), jnp.float32)
    slow_log = jax.random.uniform(slow_key, (STATE, INNER), jnp.float32, math.log(0.1), 0.0) - math.log(0.05 * TOKENS)
    fast_log = jax.random.uniform(fast_key, (STATE, INNER), jnp.float32, math.log(0.5), math.log(4.0))
    return jnp.where(chooser < slow_share, slow_log, fast_log).astype(jnp.float32)


def draw_kept_index(key, part):
    key = jax.random.fold_in(key, 11)
    scores = jax.random.randint(key, (HEADS, N_CTX, TOK_DEV), 0, 65536, jnp.int32)
    position = jnp.arange(TOK_DEV, dtype=jnp.int32)
    boost = jnp.where(position == TOK_DEV - 1, 1 << 28, 0).astype(jnp.int32)
    scores = scores * TOK_DEV + position[None, None, :] + boost[None, None, :]
    _, chosen = lax.top_k(scores, KEEP_DEV)
    chosen = jnp.sort(chosen.astype(jnp.int32), axis=-1)
    offsets = jnp.arange(N_CTX, dtype=jnp.int32)[None, :, None] * TOK_DEV
    return (chosen + offsets).reshape(HEADS, N_CTX * KEEP_DEV).astype(jnp.int32)


def shard_levels(stream_key, dims, cuts, smallest, largest):
    level, own = 1.0, jax.random.fold_in(stream_key, 6)
    for dim, blocks in cuts:
        steps = jnp.exp(jax.random.uniform(jax.random.fold_in(own, dim), (blocks,), jnp.float32, smallest / len(cuts), largest / len(cuts)))
        level = level * jnp.repeat(steps, dims[dim] // blocks).reshape([-1 if axis == dim else 1 for axis in range(len(dims))])
    return level


def shared_out(rng, own, number, rows, count, top, most, slope):
    sequence = jax.random.permutation(rng, count)
    crowded, usual = portions_of(count, rows * top, most, slope, True), portions_of(count, rows * top, most, slope, False)
    places = jnp.arange(count)

    def named(lengths, turn):
        used = int((lengths > 0).sum())
        fixed = max(1, used // 4)
        moved = fixed + (places - fixed + turn * (used - fixed)) % max(1, count - fixed)
        return jnp.zeros((count,), jnp.int32).at[sequence[jnp.where(places < fixed, places, moved)]].set(jnp.asarray(lengths, jnp.int32))

    lengths = jnp.where(number % 4 == 0, named(crowded, number // 4), named(usual, number - number // 4 - 1))
    mixed = jax.random.permutation(jax.random.fold_in(own, 3), count)
    source_of, taker = mixed[0:count // 2 * 2:2], mixed[1:count // 2 * 2:2]
    margin = jnp.minimum(lengths[source_of] - 1, most - lengths[taker]) // 2
    margin = jnp.where((source_of == sequence[0]) | (taker == sequence[0]) | (lengths[taker] == 0), 0, jnp.maximum(margin, 0))
    moved = jax.random.randint(jax.random.fold_in(own, 4), (count // 2,), 0, 1 << 20) % (margin + 1)
    lengths = lengths.at[source_of].add(-moved).at[taker].add(moved)
    items = jnp.searchsorted(jnp.cumsum(lengths), jnp.arange(rows * top), side="right").astype(jnp.int32)
    grid = items.reshape(top, rows).T
    grid = grid[jax.random.permutation(jax.random.fold_in(own, 1), rows)]
    turn = jax.random.randint(jax.random.fold_in(own, 2), (rows, 1), 0, top)
    return jnp.take_along_axis(grid, (jnp.arange(top)[None, :] + turn) % top, axis=1)


def portions_of(amount, total, reach, lean, full):
    portions = [(1 << 20) // math.isqrt(grade ** lean) + 1 for grade in range(1, amount + 1)]
    largest = reach if full else min(reach, max(-(-total // amount), total * portions[0] // sum(portions)))
    least = 1 if total - largest >= amount - 1 else 0
    holding, rest = [largest] + [least] * (amount - 1), total - largest - least * (amount - 1)
    while rest > 0:
        free = [i for i in range(1, amount) if holding[i] < largest] or [i for i in range(1, amount) if holding[i] < reach]
        whole, budget = sum([portions[i] for i in free]), rest
        for i in free:
            extra = min(reach - holding[i], max(1, budget * portions[i] // whole), rest)
            holding[i] = holding[i] + extra
            rest = rest - extra
    return np.array(holding)


def centred(rng, extent, scale, most, pieces=(), held_as=jnp.bfloat16):
    level = shard_levels(rng, extent, pieces, -0.22, 0.18) if pieces else 1.0
    drawn = jax.random.normal(rng, extent, jnp.float32) * scale * level
    return jnp.minimum(jnp.maximum(drawn, -most), most).astype(held_as)


def setup_inputs(seed: int = 0) -> dict:
    seeds = jax.random.split(jax.random.key(seed), 14)
    x_in = centred(seeds[0], (TOKENS, INNER), 1.0, 6.0, ((0, 64), (1, 8)))
    gate_in = centred(seeds[1], (TOKENS, INNER), 1.0, 6.0, ((0, 64), (1, 8)))
    conv_weight = centred(seeds[2], (CONV, INNER), CONV ** -0.5, 3.0, ((1, 8),), jnp.float32)
    conv_bias = centred(seeds[3], (INNER,), 0.5, 3.0, ((0, 8),), jnp.float32)
    proj_low = centred(seeds[4], (INNER, DT_RANK), INNER ** -0.5, 0.0625, ((0, 8),))
    proj_bc = centred(seeds[5], (INNER, 2 * STATE), INNER ** -0.5, 0.0625, ((0, 8),))
    dt_weight = centred(seeds[6], (DT_RANK, INNER), DT_RANK ** -0.5, 0.375, ((1, 8),))
    dt_bias = jnp.clip(-5.0 + 2.0 * jax.random.uniform(seeds[7], (INNER,), jnp.float32) ** shard_levels(seeds[7], (INNER,), ((0, 8),), -0.2, 0.2), -5.0, -3.0)
    decay_log = draw_decay_log(jax.random.fold_in(seeds[13], 71), 0)
    skip_gain = jnp.clip(0.5 + 1.0 * jax.random.uniform(seeds[9], (INNER,), jnp.float32) ** shard_levels(seeds[9], (INNER,), ((0, 8),), -0.2, 0.2), 0.5, 1.5)
    attn_kv = centred(seeds[10], (TOKENS, HEADS * 2 * HEAD_DIM), 1.0, 6.0, ((0, 64), (1, 8)))
    kept_index = draw_kept_index(jax.random.fold_in(seeds[13], 71), 0)
    kept_owner_keys = jax.random.split(jax.random.fold_in(seeds[12], 1), HEADS * KEPT // KEEP_DEV)
    kept_owner_turns = jax.random.permutation(jax.random.fold_in(seeds[12], 3), HEADS * KEPT // KEEP_DEV)
    kept_owner = jax.vmap(lambda own, number: shared_out(jax.random.fold_in(seeds[12], 2), own, number, KEEP_DEV, N_CTX, 1, MOST, 2))(kept_owner_keys, kept_owner_turns).reshape((HEADS, KEPT, 1))
    return {"x_in": x_in, "gate_in": gate_in, "conv_weight": conv_weight, "conv_bias": conv_bias, "proj_low": proj_low, "proj_bc": proj_bc, "dt_weight": dt_weight, "dt_bias": dt_bias, "decay_log": decay_log, "skip_gain": skip_gain, "attn_kv": attn_kv, "kept_index": kept_index, "kept_owner": kept_owner}


def scan_tokens(initial, step_size, b_coeff, c_coeff, x_float, decay_rate):
    def advance(carry_state, inputs):
        step_row, b_row, c_row, x_row = inputs
        carry_state = jnp.exp(-step_row[None, :] * decay_rate) * carry_state + (step_row * x_row)[None, :] * b_row[:, None]
        return carry_state, jnp.sum(c_row[:, None] * carry_state, axis=0)
    return lax.scan(advance, initial, (step_size, b_coeff, c_coeff, x_float))


def reference(x_in, gate_in, conv_weight, conv_bias, proj_low, proj_bc, dt_weight, dt_bias, decay_log, skip_gain, attn_kv, kept_index, kept_owner):
    padded = jnp.concatenate([jnp.zeros((CONV - 1, INNER), x_in.dtype), x_in], axis=0)
    conv_sum = jnp.broadcast_to(conv_bias[None, :], (TOKENS, INNER))
    for offset in range(CONV):
        conv_sum = conv_sum + conv_weight[offset][None, :] * padded[offset:offset + TOKENS].astype(jnp.float32)
    conv_act = jax.nn.silu(conv_sum).astype(jnp.bfloat16)
    low_rank = jnp.dot(conv_act, proj_low, preferred_element_type=jnp.float32).astype(jnp.bfloat16)
    state_in = jnp.dot(conv_act, proj_bc, preferred_element_type=jnp.float32).astype(jnp.bfloat16)
    step_size = jax.nn.softplus(jnp.dot(low_rank, dt_weight, preferred_element_type=jnp.float32) + dt_bias[None, :])
    decay_rate = jnp.exp(decay_log)
    b_coeff = state_in[:, :STATE].astype(jnp.float32)
    c_coeff = state_in[:, STATE:].astype(jnp.float32)
    x_float = conv_act.astype(jnp.float32)
    _, outputs = scan_tokens(jnp.zeros((STATE, INNER), jnp.float32), step_size, b_coeff, c_coeff, x_float, decay_rate)
    scanned = outputs + skip_gain[None, :] * x_float
    gated = (scanned * jax.nn.silu(gate_in.astype(jnp.float32))).astype(jnp.bfloat16)

    owners = kept_owner[:, :, 0].reshape(HEADS, N_CTX, KEEP_DEV)
    same_owner = owners[:, :, :, None] == owners[:, :, None, :]
    earlier = jnp.arange(KEEP_DEV)[None, :] < jnp.arange(KEEP_DEV)[:, None]
    slot_rank = jnp.sum(jnp.where(same_owner & earlier[None, None], 1, 0), axis=3).astype(jnp.int32)
    sender = jnp.arange(N_CTX, dtype=jnp.int32)[None, :, None]
    slot_index = (owners * (N_CTX * MOST) + sender * MOST + slot_rank).reshape(HEADS, KEPT).astype(jnp.int32)
    kv_heads = attn_kv.reshape(TOKENS, HEADS, 2 * HEAD_DIM)
    head_ids = jnp.arange(HEADS, dtype=jnp.int32)[:, None]
    picked = kv_heads[kept_index.astype(jnp.int32), head_ids]
    kept_cache = jnp.zeros((HEADS, N_CTX * N_CTX * MOST, 2 * HEAD_DIM), attn_kv.dtype).at[head_ids, slot_index].set(picked)
    return gated, kept_cache
```

```python
import functools
import math

import jax
import jax.numpy as jnp
from jax import lax
from jax.experimental import pallas as pl
from jax.experimental.pallas import tpu as pltpu
from jax.sharding import PartitionSpec as P

MOST = 2
NZ = 16
NX = 4
NC = 8
TOK = 128
CH = 1024
ST = 16
CONV = 4
RANK = 256
LANES = 128
TILES = CH // LANES
KEEP = 32
F32 = jnp.float32
BF16 = jnp.bfloat16
LOG2E = math.log2(math.e)


def dot(a, b):
    return jnp.dot(a, b, preferred_element_type=F32)


def dot_rows(a, b):
    return lax.dot_general(a, b, (((0,), (0,)), ((), ())), preferred_element_type=F32)


def silu(v):
    return v / (1.0 + jnp.exp(-v))


def iota(shape, dim):
    return lax.broadcasted_iota(jnp.int32, shape, dim)


def kernel(
    x_hbm, gate_hbm, cw_hbm, cb_hbm, low_hbm, bc_hbm, dtw_hbm, dtb_hbm, dec_hbm, skip_hbm, kv_hbm, idx_hbm, own_hbm,
    gated_out, kept_out,
    x_v, gate_v, cw_v, cb_v, low_v, bc_v, dtw_v, dtb_v, dec_v, skip_v, kv_v, idx_v, own_v, decs_v,
    halo, xs, act, part, rs_in, ag_out, lr, dtb3, xb3, bcx, a2b, lb, gb, yb, sg,
    s_out, s_in, l_out, l_in, sx_out, sx_in, t_out, t_in, h_out, h_in,
    kz_out, kz_in, kx_out,
    in_sem, send_sem, recv_sem,
):
    kx_in = kept_out.at[0]
    me = lax.axis_index("ctx")
    mc = lax.axis_index("ch")
    mx = me // NZ
    mz = me % NZ
    mj = mz // 2
    mhalf = mz % 2

    loads = [
        (x_hbm, x_v), (cw_hbm, cw_v), (cb_hbm, cb_v), (idx_hbm, idx_v), (own_hbm, own_v), (kv_hbm, kv_v),
        (low_hbm, low_v), (bc_hbm, bc_v), (dec_hbm, dec_v),
        (dec_hbm.at[pl.ds(mhalf * 8, 8), pl.ds(pl.multiple_of(mj * LANES, LANES), LANES)], decs_v),
        (dtw_hbm, dtw_v), (dtb_hbm, dtb_v), (skip_hbm, skip_v), (gate_hbm, gate_v),
    ]
    loads = [pltpu.make_async_copy(s, d, in_sem.at[i]) for i, (s, d) in enumerate(loads)]
    (x_ld, cw_ld, cb_ld, idx_ld, own_ld, kv_ld, low_ld, bc_ld, dec_ld, decs_ld, dtw_ld, dtb_ld, skip_ld, gate_ld) = loads

    for c in loads:
        c.start()

    barrier = pltpu.get_barrier_semaphore()
    for d in range(1, NZ):
        pl.semaphore_signal(barrier, inc=1, device_id={"ctx": mx * NZ + (mz + d) % NZ})
    for d in range(1, NX):
        pl.semaphore_signal(barrier, inc=1, device_id={"ctx": ((mx + d) % NX) * NZ + mz})
    for d in range(1, NC):
        pl.semaphore_signal(barrier, inc=1, device_id={"ch": (mc + d) % NC})
    right = (me + 1) % (NX * NZ)
    left = (me + NX * NZ - 1) % (NX * NZ)

    @pl.when(mz == NZ - 1)
    def _():
        pl.semaphore_signal(barrier, inc=1, device_id={"ctx": right})

    @pl.when(mz == 0)
    def _():
        pl.semaphore_signal(barrier, inc=1, device_id={"ctx": left})

    pl.semaphore_wait(barrier, NZ - 1 + NX - 1 + NC - 1 + jnp.where((mz == 0) | (mz == NZ - 1), 1, 0))

    def remote(src, dst, k, peer):
        return pltpu.make_async_remote_copy(
            src_ref=src, dst_ref=dst, send_sem=send_sem.at[k], recv_sem=recv_sem.at[k], device_id=peer
        )

    def drain(ref, sem):
        pltpu.make_async_copy(ref, ref, sem).wait()

    HALO, RS, AG, KZ, KX, SZ, LZ, SX, TX, HZ = range(10)

    remote(x_hbm.at[pl.ds(TOK - 16, 16), :], halo, HALO, {"ctx": right}).start()

    x_ld.wait()
    cw_ld.wait()
    cb_ld.wait()
    xs[pl.ds(16, TOK), :] = x_v[...].astype(F32)
    for j in range(TILES):
        cols = pl.ds(j * LANES, LANES)
        s = jnp.broadcast_to(cb_v[:, cols], (TOK - 16, LANES))
        for k in range(CONV):
            s = s + cw_v[pl.ds(k, 1), cols] * xs[pl.ds(32 - (CONV - 1) + k, TOK - 16), cols]
        a = silu(s).astype(BF16)
        act[pl.ds(16, TOK - 16), cols] = a
        xb3[pl.ds(16 * TILES + j, TOK - 16, stride=TILES), :] = a.astype(F32)

    idx_ld.wait()
    own_ld.wait()
    kv_ld.wait()
    own_row = own_v[...]
    eye = iota((KEEP, KEEP), 0) == iota((KEEP, KEEP), 1)
    own = jnp.sum(jnp.where(eye, own_row, 0), axis=1, keepdims=True)
    same = (own_row == own) & (iota((KEEP, KEEP), 1) < iota((KEEP, KEEP), 0))
    rank = jnp.sum(jnp.where(same, 1, 0), axis=1, keepdims=True)
    place = (own & (NZ - 1)) * 16 + (own >> 4) * 2 + rank
    src_t = (iota((TOK, KEEP), 0) == idx_v[...] - me * TOK).astype(F32).astype(BF16)
    picked = dot_rows(src_t, kv_v[...]).astype(BF16)
    slots = iota((KEEP, 256), 1)
    kz = dot_rows((slots == place).astype(F32).astype(BF16), picked[:, :LANES])
    kz = kz + dot_rows((slots == place + 8).astype(F32).astype(BF16), picked[:, LANES:])
    kz_out[...] = kz.astype(BF16)

    drain(halo, recv_sem.at[HALO])
    xs[pl.ds(0, 16), :] = jnp.where(me > 0, halo[...].astype(F32), 0.0)
    for j in range(TILES):
        cols = pl.ds(j * LANES, LANES)
        s = jnp.broadcast_to(cb_v[:, cols], (16, LANES))
        for k in range(CONV):
            s = s + cw_v[pl.ds(k, 1), cols] * xs[pl.ds(16 - (CONV - 1) + k, 16), cols]
        a = silu(s).astype(BF16)
        act[pl.ds(0, 16), cols] = a
        xb3[pl.ds(j, 16, stride=TILES), :] = a.astype(F32)

    low_ld.wait()
    bc_ld.wait()
    part[:, pl.ds(RANK, LANES)] = jnp.zeros((TOK, LANES), F32)
    part[:, pl.ds(0, RANK)] = dot(act[...], low_v[...])
    part[:, pl.ds(RANK, 2 * ST)] = lax.dot_general(
        act[...], bc_v[...], (((1,), (1,)), ((), ())), preferred_element_type=F32
    )

    def rows_of(i):
        return pl.ds(pl.multiple_of(i * 16, 16), 16)

    for d in range(1, NC):
        to = (mc + d) % NC
        remote(part.at[rows_of(to), :], rs_in.at[rows_of(mc), :], RS, {"ch": to}).start()
    rs_in[rows_of(mc), :] = part[rows_of(mc), :]
    for d in range(1, NZ):
        to = (mz + d) % NZ
        remote(kz_out.at[rows_of(to), :], kz_in.at[rows_of(mz), :], KZ, {"ctx": mx * NZ + to}).start()
    kz_in[rows_of(mz), :] = kz_out[rows_of(mz), :]

    dec_ld.wait()
    decs_ld.wait()
    gate_ld.wait()
    for j in range(TILES):
        a2b[pl.ds(j, ST, stride=TILES), :] = -LOG2E * jnp.exp(dec_v[:, pl.ds(j * LANES, LANES)])
    a2s = -LOG2E * jnp.exp(decs_v[...])
    sg[...] = silu(gate_v[...].astype(F32))

    drain(rs_in.at[pl.ds(0, TOK - 16), :], recv_sem.at[RS])
    total = rs_in[pl.ds(0, 16), :]
    for i in range(1, NC):
        total = total + rs_in[pl.ds(16 * i, 16), :]
    ag_out[...] = total.astype(BF16)
    for d in range(1, NC):
        to = (mc + d) % NC
        remote(ag_out, lr.at[rows_of(mc), :], AG, {"ch": to}).start()
    lr[rows_of(mc), :] = ag_out[...]

    drain(kz_in.at[pl.ds(0, 240), :], recv_sem.at[KZ])
    row = iota((TOK, 256), 0)
    want = ((row >> 1) & (NZ - 1)) * 16 + (row >> 5) * 2 + (row & 1)
    for half in range(2):
        sel = (iota((TOK, 256), 1) == want + half * 8).astype(F32).astype(BF16)
        kx_out[:, pl.ds(half * LANES, LANES)] = dot(sel, kz_in[...]).astype(BF16)

    def block_of(i):
        return pl.ds(pl.multiple_of(i * 32, 32), 32)

    for d in range(1, NX):
        to = (mx + d) % NX
        remote(kx_out.at[block_of(to), :], kx_in.at[block_of(mx), :], KX, {"ctx": to * NZ + mz}).start()
    kx_in[block_of(mx), :] = kx_out[block_of(mx), :]

    dtw_ld.wait()
    dtb_ld.wait()
    skip_ld.wait()
    drain(lr.at[pl.ds(0, TOK - 16), :], recv_sem.at[AG])

    for j in range(TILES):
        cols = pl.ds(j * LANES, LANES)
        v = dot(lr[:, pl.ds(0, RANK)], dtw_v[:, cols]) + dtb_v[:, cols]
        dtb3[pl.ds(j, TOK, stride=TILES), :] = jnp.maximum(v, 0.0) + jnp.log1p(jnp.exp(-jnp.abs(v)))
    coeff = lr[:, pl.ds(RANK, LANES)][:, : 2 * ST]
    for i in range(8):
        spread = (iota((2 * ST, 4 * LANES), 1) >> 7) + 4 * i == iota((2 * ST, 4 * LANES), 0)
        bcx[:, :, pl.ds(i * 4 * LANES, 4 * LANES)] = dot(coeff, spread.astype(F32).astype(BF16)).reshape(TOK // 8, 8, 4 * LANES)

    def total_step(t, acc):
        for u in range(8):
            acc = acc + dtb3[pl.ds(pl.multiple_of(t * 64, 64) + u * 8, 8), :]
        return acc

    s_total = lax.fori_loop(0, TOK // 8, total_step, jnp.zeros((TILES, LANES), F32))
    for j in range(TILES):
        s_out[j] = s_total[j : j + 1, :]
    for d in range(1, NZ):
        to = (mz + d) % NZ
        remote(s_out.at[to // 2], s_in.at[mz], SZ, {"ctx": mx * NZ + to}).start()
    s_in[mz] = s_out[mj]

    def scan_step(g, state):
        state = list(state)
        for u in range(8):
            dt = dtb3[pl.ds(pl.multiple_of(g * 64, 64) + u * 8, 8), :]
            xt = xb3[pl.ds(pl.multiple_of(g * 64, 64) + u * 8, 8), :]
            dx = dt * xt
            y = [None] * 4
            for n in range(ST):
                b = bcx[g, pl.ds(u, 1), pl.ds(n * LANES, LANES)]
                c = bcx[g, pl.ds(u, 1), pl.ds((ST + n) * LANES, LANES)]
                state[n] = jnp.exp2(dt * a2b[pl.ds(n * 8, 8), :]) * state[n] + dx * b
                term = c * state[n]
                y[n % 4] = term if y[n % 4] is None else y[n % 4] + term
            yb[pl.ds(pl.multiple_of(g * 64, 64) + u * 8, 8), :] = (y[0] + y[1]) + (y[2] + y[3])
        return tuple(state)

    state = lax.fori_loop(0, TOK // 8, scan_step, tuple(jnp.zeros((TILES, LANES), F32) for _ in range(ST)))
    for n in range(ST):
        lb[pl.ds(n * 8, 8), :] = state[n]
    for j in range(TILES):
        l_out[pl.ds(j * ST, ST), :] = lb[pl.ds(j, ST, stride=TILES), :]

    def tile_of(i):
        return pl.ds(pl.multiple_of(i * 8, 8), 8)

    for d in range(1, NZ):
        to = (mz + d) % NZ
        remote(l_out.at[tile_of(to), :], l_in.at[tile_of(mz), :], LZ, {"ctx": mx * NZ + to}).start()
    l_in[tile_of(mz), :] = l_out[tile_of(mz), :]

    drain(s_in.at[pl.ds(0, NZ - 1)], recv_sem.at[SZ])
    run = jnp.zeros((1, LANES), F32)
    decay, reach = [], []
    for z in range(NZ):
        decay.append(jnp.exp2(a2s * s_in[z]))
        reach.append(jnp.exp2(a2s * run))
        run = run + s_in[z]
    sx_out[...] = run
    for d in range(1, NX):
        remote(sx_out, sx_in.at[mx], SX, {"ctx": ((mx + d) % NX) * NZ + mz}).start()
    sx_in[mx] = run

    def reach_step(g, cum):
        for u in range(8):
            cum = cum + dtb3[pl.ds(pl.multiple_of(g * 64, 64) + u * 8, 8), :]
            for n in range(ST):
                c = bcx[g, pl.ds(u, 1), pl.ds((ST + n) * LANES, LANES)]
                gb[pl.ds(pl.multiple_of(g * 1024, 1024) + u * 128 + n * 8, 8), :] = c * jnp.exp2(cum * a2b[pl.ds(n * 8, 8), :])
        return cum

    drain(l_in.at[pl.ds(0, TOK - 8), :], recv_sem.at[LZ])
    before = []
    carry = jnp.zeros((8, LANES), F32)
    for z in range(NZ):
        before.append(carry)
        carry = decay[z] * carry + l_in[pl.ds(z * 8, 8), :]
    t_out[...] = carry
    for d in range(1, NX):
        remote(t_out, t_in.at[mx], TX, {"ctx": ((mx + d) % NX) * NZ + mz}).start()
    t_in[mx] = carry

    lax.fori_loop(0, TOK // 8, reach_step, jnp.zeros((TILES, LANES), F32))

    drain(sx_in.at[pl.ds(0, NX - 1)], recv_sem.at[SX])
    drain(t_in.at[pl.ds(0, NX - 1)], recv_sem.at[TX])
    plane = jnp.zeros((8, LANES), F32)
    for i in range(NX - 1):
        plane = jnp.where(i < mx, jnp.exp2(a2s * sx_in[i]) * plane + t_in[i], plane)
    for z in range(NZ):
        h_out[pl.ds(z * 8, 8), :] = before[z] + reach[z] * plane
    for d in range(1, NZ):
        to = (mz + d) % NZ
        remote(h_out.at[tile_of(to), :], h_in.at[tile_of(mz), :], HZ, {"ctx": mx * NZ + to}).start()
    h_in[tile_of(mz), :] = h_out[tile_of(mz), :]
    drain(h_in.at[pl.ds(0, TOK - 8), :], recv_sem.at[HZ])

    carried = [h_in[pl.ds(n, TILES, stride=ST), :] for n in range(ST)]

    def add_step(g, _):
        for u in range(8):
            at = pl.ds(pl.multiple_of(g * 64, 64) + u * 8, 8)
            y = [yb[at, :], None, None, None]
            for n in range(ST):
                term = gb[pl.ds(pl.multiple_of(g * 1024, 1024) + u * 128 + n * 8, 8), :] * carried[n]
                y[n % 4] = term if y[n % 4] is None else y[n % 4] + term
            yb[at, :] = (y[0] + y[1]) + (y[2] + y[3])
        return 0

    lax.fori_loop(0, TOK // 8, add_step, 0)

    for j in range(TILES):
        cols = pl.ds(j * LANES, LANES)
        y = yb[pl.ds(j, TOK, stride=TILES), :] + skip_v[:, cols] * act[:, cols].astype(F32)
        gated_out[:, cols] = (y * sg[:, cols]).astype(BF16)
    drain(kx_in.at[pl.ds(0, 96), :], recv_sem.at[KX])

    drain(halo, send_sem.at[HALO])
    drain(rs_in.at[pl.ds(0, TOK - 16), :], send_sem.at[RS])
    drain(lr.at[pl.ds(0, TOK - 16), :], send_sem.at[AG])
    drain(kz_in.at[pl.ds(0, 240), :], send_sem.at[KZ])
    drain(kx_in.at[pl.ds(0, 96), :], send_sem.at[KX])
    drain(s_in.at[pl.ds(0, NZ - 1)], send_sem.at[SZ])
    drain(l_in.at[pl.ds(0, TOK - 8), :], send_sem.at[LZ])
    drain(sx_in.at[pl.ds(0, NX - 1)], send_sem.at[SX])
    drain(t_in.at[pl.ds(0, NX - 1)], send_sem.at[TX])
    drain(h_in.at[pl.ds(0, TOK - 8), :], send_sem.at[HZ])


def local(
    x_in, gate_in, conv_weight, conv_bias, proj_low, proj_bc, dt_weight, dt_bias, decay_log, skip_gain, attn_kv,
    kept_index, kept_owner,
):
    V = pltpu.VMEM
    hbm = pl.BlockSpec(memory_space=pltpu.HBM)
    return pl.pallas_call(
        kernel,
        out_shape=(jax.ShapeDtypeStruct((TOK, CH), BF16), jax.ShapeDtypeStruct((1, TOK, 2 * LANES), BF16)),
        in_specs=[hbm] * 13,
        out_specs=(pl.BlockSpec(memory_space=pltpu.VMEM),) * 2,
        scratch_shapes=[
            V((TOK, CH), BF16), V((TOK, CH), BF16), V((CONV, CH), F32), V((1, CH), F32), V((CH, RANK), BF16),
            V((2 * ST, CH), BF16), V((RANK, CH), BF16), V((1, CH), F32), V((ST, CH), F32), V((1, CH), F32),
            V((TOK, 2 * LANES), BF16), V((1, KEEP), jnp.int32), V((1, KEEP), jnp.int32), V((8, LANES), F32),
            V((16, CH), BF16), V((TOK + 16, CH), F32), V((TOK, CH), BF16), V((TOK, RANK + LANES), F32),
            V((TOK, RANK + LANES), F32), V((16, RANK + LANES), BF16), V((TOK, RANK + LANES), BF16),
            V((TOK * TILES, LANES), F32), V((TOK * TILES, LANES), F32), V((TOK // 8, 8, 2 * ST * LANES), F32),
            V((ST * TILES, LANES), F32), V((ST * TILES, LANES), F32), V((TOK * ST * TILES, LANES), F32),
            V((TOK * TILES, LANES), F32), V((TOK, CH), F32),
            V((TILES, 1, LANES), F32), V((NZ, 1, LANES), F32), V((ST * TILES, LANES), F32), V((ST * TILES, LANES), F32),
            V((1, LANES), F32), V((NX, 1, LANES), F32), V((8, LANES), F32), V((NX, 8, LANES), F32),
            V((ST * TILES, LANES), F32), V((ST * TILES, LANES), F32),
            V((256, LANES), BF16), V((256, LANES), BF16), V((TOK, 2 * LANES), BF16),
            pltpu.SemaphoreType.DMA((14,)),
            pltpu.SemaphoreType.DMA((10,)), pltpu.SemaphoreType.DMA((10,)),
        ],
        compiler_params=pltpu.CompilerParams(
            collective_id=0, has_side_effects=True, vmem_limit_bytes=48 * 1024 * 1024
        ),
    )(
        x_in, gate_in, conv_weight, conv_bias.reshape(1, CH), proj_low, proj_bc.T, dt_weight, dt_bias.reshape(1, CH),
        decay_log, skip_gain.reshape(1, CH), attn_kv, kept_index, kept_owner.reshape(1, KEEP),
    )


def solution(mesh):
    return jax.shard_map(
        local,
        mesh=mesh,
        in_specs=(
            P("ctx", "ch"), P("ctx", "ch"), P(None, "ch"), P("ch"), P("ch", None), P("ch", None), P(None, "ch"),
            P("ch"), P(None, "ch"), P("ch"), P("ctx", "ch"), P("ch", "ctx"), P("ch", "ctx", None),
        ),
        out_specs=(P("ctx", "ch"), P("ch", "ctx", None)),
        check_vma=False,
    )
```

```python
import functools
import math

import jax
import jax.numpy as jnp
from jax import lax
from jax.experimental import pallas as pl
from jax.experimental.pallas import tpu as pltpu
from jax.sharding import PartitionSpec as P

MOST = 2
NZ = 16
NX = 4
NC = 8
TOK = 128
CH = 1024
ST = 16
CONV = 4
RANK = 256
LANES = 128
TILES = CH // LANES
KEEP = 32
F32 = jnp.float32
BF16 = jnp.bfloat16
LOG2E = math.log2(math.e)


def dot(a, b):
    return jnp.dot(a, b, preferred_element_type=F32)


def dot_rows(a, b):
    return lax.dot_general(a, b, (((0,), (0,)), ((), ())), preferred_element_type=F32)


def silu(v):
    return v / (1.0 + jnp.exp(-v))


def iota(shape, dim):
    return lax.broadcasted_iota(jnp.int32, shape, dim)


def kernel(
    x_hbm, gate_hbm, cw_hbm, cb_hbm, low_hbm, bc_hbm, dtw_hbm, dtb_hbm, dec_hbm, skip_hbm, kv_hbm, idx_hbm, own_hbm,
    gated_out, kept_out,
    x_v, gate_v, cw_v, cb_v, low_v, bc_v, dtw_v, dtb_v, dec_v, skip_v, kv_v, idx_v, own_v, decs_v,
    halo, xs, act, part, rs_in, ag_out, lr, dtb3, xb3, bcx, a2b, lb, gb, yb, sg,
    s_out, s_in, l_out, l_in, sx_out, sx_in, t_out, t_in, h_out, h_in, hf, decay, reach, before,
    kz_out, kz_in, kx_out,
    in_sem, send_sem, recv_sem, here_sem,
):
    kx_in = kept_out.at[0]
    me = lax.axis_index("ctx")
    mc = lax.axis_index("ch")
    mx = me // NZ
    mz = me % NZ
    mq = mz % 4

    loads = [
        (x_hbm, x_v), (cw_hbm, cw_v), (cb_hbm, cb_v), (idx_hbm, idx_v), (own_hbm, own_v), (kv_hbm, kv_v),
        (low_hbm, low_v), (bc_hbm, bc_v), (dec_hbm, dec_v),
        (dec_hbm.at[:, pl.ds(pl.multiple_of(mq * 2 * LANES, 2 * LANES), 2 * LANES)], decs_v),
        (dtw_hbm, dtw_v), (dtb_hbm, dtb_v), (skip_hbm, skip_v), (gate_hbm, gate_v),
    ]
    loads = [pltpu.make_async_copy(s, d, in_sem.at[i]) for i, (s, d) in enumerate(loads)]
    (x_ld, cw_ld, cb_ld, idx_ld, own_ld, kv_ld, low_ld, bc_ld, dec_ld, decs_ld, dtw_ld, dtb_ld, skip_ld, gate_ld) = loads

    for c in loads:
        c.start()

    def along_z(d):
        return {"ctx": mx * NZ + (mz + d + NZ) % NZ}

    def along_x(d):
        return {"ctx": ((mx + d) % NX) * NZ + mz}

    def along_ch(dy, dc):
        return {"ch": ((mc // 2 + dy) % (NC // 2)) * 2 + (mc + dc) % 2}

    far_z = (8, 7, 9, 6, 10, 5, 11, 4, 12, 3, 13, 2, 14, 1, 15)
    far_x = (2, 1, 3)
    far_ch = ((2, 0), (2, 1), (1, 0), (3, 0), (1, 1), (3, 1), (0, 1))
    right = {"ctx": (me + 1) % (NX * NZ)}
    left = {"ctx": (me + NX * NZ - 1) % (NX * NZ)}
    barrier = pltpu.get_barrier_semaphore()
    for d in far_ch:
        pl.semaphore_signal(barrier, inc=1, device_id=along_ch(*d))
    for d in (-1, 1):
        pl.semaphore_signal(barrier, inc=1, device_id=along_z(d))
    for d in far_x:
        pl.semaphore_signal(barrier, inc=1, device_id=along_x(d))

    @pl.when(mz == NZ - 1)
    def _():
        pl.semaphore_signal(barrier, inc=1, device_id=right)

    @pl.when(mz == 0)
    def _():
        pl.semaphore_signal(barrier, inc=1, device_id=left)

    pl.semaphore_wait(barrier, NC - 1 + NX - 1 + 2 + jnp.where((mz == 0) | (mz == NZ - 1), 1, 0))

    def tell(i):
        for d in (-(1 << i), 1 << i):
            pl.semaphore_signal(here_sem.at[i], inc=1, device_id=along_z(d))

    def hear(i):
        pl.semaphore_wait(here_sem.at[i], 2)

    def remote(src, dst, k, peer):
        return pltpu.make_async_remote_copy(
            src_ref=src, dst_ref=dst, send_sem=send_sem.at[k], recv_sem=recv_sem.at[k], device_id=peer
        )

    def drain(ref, sem):
        pltpu.make_async_copy(ref, ref, sem).wait()

    HALO, RS, AG, KZ, KX, SZ, LZ, SX, TX, HZ = range(10)

    remote(x_hbm.at[pl.ds(TOK - 16, 16), :], halo, HALO, right).start()
    tell(0)

    x_ld.wait()
    cw_ld.wait()
    cb_ld.wait()
    xs[pl.ds(16, TOK), :] = x_v[...].astype(F32)
    for j in range(TILES):
        cols = pl.ds(j * LANES, LANES)
        s = jnp.broadcast_to(cb_v[:, cols], (TOK - 16, LANES))
        for k in range(CONV):
            s = s + cw_v[pl.ds(k, 1), cols] * xs[pl.ds(32 - (CONV - 1) + k, TOK - 16), cols]
        a = silu(s).astype(BF16)
        act[pl.ds(16, TOK - 16), cols] = a
        xb3[pl.ds(16 * TILES + j, TOK - 16, stride=TILES), :] = a.astype(F32)

    idx_ld.wait()
    own_ld.wait()
    kv_ld.wait()
    own_row = own_v[...]
    eye = iota((KEEP, KEEP), 0) == iota((KEEP, KEEP), 1)
    own = jnp.sum(jnp.where(eye, own_row, 0), axis=1, keepdims=True)
    same = (own_row == own) & (iota((KEEP, KEEP), 1) < iota((KEEP, KEEP), 0))
    rank = jnp.sum(jnp.where(same, 1, 0), axis=1, keepdims=True)
    place = (own & (NZ - 1)) * 16 + (own >> 4) * 2 + rank
    src_t = (iota((TOK, KEEP), 0) == idx_v[...] - me * TOK).astype(F32).astype(BF16)
    picked = dot_rows(src_t, kv_v[...]).astype(BF16)
    slots = iota((KEEP, 256), 1)
    kz = dot_rows((slots == place).astype(F32).astype(BF16), picked[:, :LANES])
    kz = kz + dot_rows((slots == place + 8).astype(F32).astype(BF16), picked[:, LANES:])
    kz_out[...] = kz.astype(BF16)

    hear(0)
    tell(1)
    drain(halo, recv_sem.at[HALO])
    xs[pl.ds(0, 16), :] = jnp.where(me > 0, halo[...].astype(F32), 0.0)
    for j in range(TILES):
        cols = pl.ds(j * LANES, LANES)
        s = jnp.broadcast_to(cb_v[:, cols], (16, LANES))
        for k in range(CONV):
            s = s + cw_v[pl.ds(k, 1), cols] * xs[pl.ds(16 - (CONV - 1) + k, 16), cols]
        a = silu(s).astype(BF16)
        act[pl.ds(0, 16), cols] = a
        xb3[pl.ds(j, 16, stride=TILES), :] = a.astype(F32)

    low_ld.wait()
    bc_ld.wait()
    part[:, pl.ds(RANK, LANES)] = jnp.zeros((TOK, LANES), BF16)
    part[:, pl.ds(0, RANK)] = dot(act[...], low_v[...]).astype(BF16)
    part[:, pl.ds(RANK, 2 * ST)] = lax.dot_general(
        act[...], bc_v[...], (((1,), (1,)), ((), ())), preferred_element_type=F32
    ).astype(BF16)

    def rows_of(i):
        return pl.ds(pl.multiple_of(i * 16, 16), 16)

    for d in far_ch:
        to = along_ch(*d)
        remote(part.at[rows_of(to["ch"]), :], rs_in.at[rows_of(mc), :], RS, to).start()
    rs_in[rows_of(mc), :] = part[rows_of(mc), :]
    hear(1)
    tell(2)

    dec_ld.wait()
    decs_ld.wait()
    gate_ld.wait()
    for j in range(TILES):
        a2b[pl.ds(j, ST, stride=TILES), :] = -LOG2E * jnp.exp(dec_v[:, pl.ds(j * LANES, LANES)])
    a2s = [-LOG2E * jnp.exp(decs_v[:, pl.ds(jj * LANES, LANES)]) for jj in range(2)]
    sg[...] = silu(gate_v[...].astype(F32))

    drain(rs_in.at[pl.ds(0, TOK - 16), :], recv_sem.at[RS])
    total = rs_in[pl.ds(0, 16), :].astype(F32)
    for i in range(1, NC):
        total = total + rs_in[pl.ds(16 * i, 16), :].astype(F32)
    ag_out[...] = total.astype(BF16)
    for d in far_ch:
        remote(ag_out, lr.at[rows_of(mc), :], AG, along_ch(*d)).start()
    lr[rows_of(mc), :] = ag_out[...]
    hear(2)
    for d in far_z:
        to = (mz + d) % NZ
        remote(kz_out.at[rows_of(to), :], kz_in.at[rows_of(mz), :], KZ, along_z(d)).start()
    kz_in[rows_of(mz), :] = kz_out[rows_of(mz), :]

    dtw_ld.wait()
    dtb_ld.wait()
    skip_ld.wait()
    drain(lr.at[pl.ds(0, TOK - 16), :], recv_sem.at[AG])

    for j in range(TILES):
        cols = pl.ds(j * LANES, LANES)
        v = dot(lr[:, pl.ds(0, RANK)], dtw_v[:, cols]) + dtb_v[:, cols]
        dtb3[pl.ds(j, TOK, stride=TILES), :] = jnp.maximum(v, 0.0) + jnp.log1p(jnp.exp(-jnp.abs(v)))
    coeff = lr[:, pl.ds(RANK, LANES)][:, : 2 * ST]

    def spread(i):
        rows = (iota((2 * ST, 4 * LANES), 1) >> 7) + 4 * i == iota((2 * ST, 4 * LANES), 0)
        wide = dot(coeff, rows.astype(F32).astype(BF16))
        bcx[:, :, pl.ds(i * 4 * LANES, 4 * LANES)] = wide.reshape(TOK // 8, 8, 4 * LANES)

    for i in range(4):
        spread(i)

    def token(g, u):
        return pl.ds(pl.multiple_of(g * 64, 64) + u * 8, 8)

    def total_step(g, acc):
        for u in range(8):
            acc = acc + dtb3[token(g, u), :]
        return acc

    s_total = lax.fori_loop(0, TOK // 8, total_step, jnp.zeros((TILES, LANES), F32))
    for j in range(TILES):
        s_out[j] = s_total[j : j + 1, :]
    for d in far_z:
        to = (mz + d) % 4
        remote(s_out.at[pl.ds(2 * to, 2)], s_in.at[mz], SZ, along_z(d)).start()
    s_in[mz] = s_out[pl.ds(2 * mq, 2)]

    def end_step(g, state):
        state = list(state)
        for u in range(8):
            dt = dtb3[token(g, u), :]
            dx = dt * xb3[token(g, u), :]
            for n in range(ST):
                b = bcx[g, pl.ds(u, 1), pl.ds(n * LANES, LANES)]
                state[n] = jnp.exp2(dt * a2b[pl.ds(n * 8, 8), :]) * state[n] + dx * b
        return tuple(state)

    empty = tuple(jnp.zeros((TILES, LANES), F32) for _ in range(ST))
    state = lax.fori_loop(0, TOK // 8, end_step, empty)
    for n in range(ST):
        lb[pl.ds(n * 8, 8), :] = state[n]
    for j in range(TILES):
        l_out[pl.ds(j * ST, ST), :] = lb[pl.ds(j, ST, stride=TILES), :].astype(BF16)

    def block_of(i):
        return pl.ds(pl.multiple_of(i * 32, 32), 32)

    for d in far_z:
        to = (mz + d) % 4
        remote(l_out.at[block_of(to), :], l_in.at[block_of(mz), :], LZ, along_z(d)).start()
    l_in[block_of(mz), :] = l_out[block_of(mq), :]

    for i in range(4, 8):
        spread(i)

    def scan_step(g, state):
        state = list(state)
        for u in range(8):
            dt = dtb3[token(g, u), :]
            dx = dt * xb3[token(g, u), :]
            y = [None] * 4
            for n in range(ST):
                b = bcx[g, pl.ds(u, 1), pl.ds(n * LANES, LANES)]
                c = bcx[g, pl.ds(u, 1), pl.ds((ST + n) * LANES, LANES)]
                state[n] = jnp.exp2(dt * a2b[pl.ds(n * 8, 8), :]) * state[n] + dx * b
                term = c * state[n]
                y[n % 4] = term if y[n % 4] is None else y[n % 4] + term
            yb[token(g, u), :] = (y[0] + y[1]) + (y[2] + y[3])
        return tuple(state)

    lax.fori_loop(0, TOK // 8, scan_step, empty)

    def reach_step(g, cum):
        for u in range(8):
            cum = cum + dtb3[token(g, u), :]
            for n in range(ST):
                c = bcx[g, pl.ds(u, 1), pl.ds((ST + n) * LANES, LANES)]
                gb[pl.ds(pl.multiple_of(g * 1024, 1024) + u * 128 + n * 8, 8), :] = c * jnp.exp2(cum * a2b[pl.ds(n * 8, 8), :])
        return cum

    lax.fori_loop(0, TOK // 8, reach_step, jnp.zeros((TILES, LANES), F32))

    drain(kz_in.at[pl.ds(0, 240), :], recv_sem.at[KZ])
    row = iota((TOK, 256), 0)
    want = ((row >> 1) & (NZ - 1)) * 16 + (row >> 5) * 2 + (row & 1)
    for half in range(2):
        sel = (iota((TOK, 256), 1) == want + half * 8).astype(F32).astype(BF16)
        kx_out[:, pl.ds(half * LANES, LANES)] = dot(sel, kz_in[...]).astype(BF16)

    for d in far_x:
        to = (mx + d) % NX
        remote(kx_out.at[block_of(to), :], kx_in.at[block_of(mx), :], KX, along_x(d)).start()
    kx_in[block_of(mx), :] = kx_out[block_of(mx), :]

    drain(s_in.at[pl.ds(0, NZ - 1)], recv_sem.at[SZ])
    for jj in range(2):
        run = jnp.zeros((1, LANES), F32)
        for z in range(NZ):
            rows = pl.ds(z * 32 + jj * ST, ST)
            decay[rows, :] = jnp.exp2(a2s[jj] * s_in[z, jj])
            reach[rows, :] = jnp.exp2(a2s[jj] * run)
            run = run + s_in[z, jj]
        sx_out[jj] = run
    for d in far_x:
        remote(sx_out, sx_in.at[mx], SX, along_x(d)).start()
    sx_in[mx] = sx_out[...]

    drain(l_in.at[pl.ds(0, 480), :], recv_sem.at[LZ])
    for jj in range(2):
        carry = jnp.zeros((ST, LANES), F32)
        for z in range(NZ):
            rows = pl.ds(z * 32 + jj * ST, ST)
            before[rows, :] = carry
            carry = decay[rows, :] * carry + l_in[rows, :].astype(F32)
        t_out[pl.ds(jj * ST, ST), :] = carry.astype(BF16)
    for d in far_x:
        remote(t_out, t_in.at[mx], TX, along_x(d)).start()
    t_in[mx] = t_out[...]
    drain(sx_in.at[pl.ds(0, NX - 1)], recv_sem.at[SX])
    drain(t_in.at[pl.ds(0, NX - 1)], recv_sem.at[TX])
    plane = []
    for jj in range(2):
        p = jnp.zeros((ST, LANES), F32)
        for i in range(NX - 1):
            later = jnp.exp2(a2s[jj] * sx_in[i, jj]) * p + t_in[i, pl.ds(jj * ST, ST), :].astype(F32)
            p = jnp.where(i < mx, later, p)
        plane.append(p)

    for k, d in enumerate((-2, -1, 1, 0)):
        z = (mz + d + NZ) % NZ
        for jj in range(2):
            rows = pl.ds(pl.multiple_of(z * 32, 32) + jj * ST, ST)
            h_out[pl.ds(k * 32 + jj * ST, ST), :] = (before[rows, :] + reach[rows, :] * plane[jj]).astype(BF16)
        if d:
            remote(h_out.at[pl.ds(k * 32, 32), :], h_in.at[block_of(mq), :], HZ, along_z(d)).start()
    h_in[block_of(mq), :] = h_out[pl.ds(96, 32), :]
    drain(h_in.at[pl.ds(0, 96), :], recv_sem.at[HZ])
    hf[...] = h_in[...].astype(F32)

    carried = [hf[pl.ds(n, TILES, stride=ST), :] for n in range(ST)]

    def add_step(g, _):
        for u in range(8):
            at = token(g, u)
            y = [yb[at, :], None, None, None]
            for n in range(ST):
                term = gb[pl.ds(pl.multiple_of(g * 1024, 1024) + u * 128 + n * 8, 8), :] * carried[n]
                y[n % 4] = term if y[n % 4] is None else y[n % 4] + term
            yb[at, :] = (y[0] + y[1]) + (y[2] + y[3])
        return 0

    lax.fori_loop(0, TOK // 8, add_step, 0)

    for j in range(TILES):
        cols = pl.ds(j * LANES, LANES)
        y = yb[pl.ds(j, TOK, stride=TILES), :] + skip_v[:, cols] * act[:, cols].astype(F32)
        gated_out[:, cols] = (y * sg[:, cols]).astype(BF16)
    drain(kx_in.at[pl.ds(0, 96), :], recv_sem.at[KX])

    drain(halo, send_sem.at[HALO])
    drain(rs_in.at[pl.ds(0, TOK - 16), :], send_sem.at[RS])
    drain(lr.at[pl.ds(0, TOK - 16), :], send_sem.at[AG])
    drain(kz_in.at[pl.ds(0, 240), :], send_sem.at[KZ])
    drain(kx_in.at[pl.ds(0, 96), :], send_sem.at[KX])
    drain(s_in.at[pl.ds(0, NZ - 1)], send_sem.at[SZ])
    drain(l_in.at[pl.ds(0, 480), :], send_sem.at[LZ])
    drain(sx_in.at[pl.ds(0, NX - 1)], send_sem.at[SX])
    drain(t_in.at[pl.ds(0, NX - 1)], send_sem.at[TX])
    drain(h_in.at[pl.ds(0, 96), :], send_sem.at[HZ])


def local(
    x_in, gate_in, conv_weight, conv_bias, proj_low, proj_bc, dt_weight, dt_bias, decay_log, skip_gain, attn_kv,
    kept_index, kept_owner,
):
    V = pltpu.VMEM
    hbm = pl.BlockSpec(memory_space=pltpu.HBM)
    return pl.pallas_call(
        kernel,
        out_shape=(jax.ShapeDtypeStruct((TOK, CH), BF16), jax.ShapeDtypeStruct((1, TOK, 2 * LANES), BF16)),
        in_specs=[hbm] * 13,
        out_specs=(pl.BlockSpec(memory_space=pltpu.VMEM),) * 2,
        scratch_shapes=[
            V((TOK, CH), BF16), V((TOK, CH), BF16), V((CONV, CH), F32), V((1, CH), F32), V((CH, RANK), BF16),
            V((2 * ST, CH), BF16), V((RANK, CH), BF16), V((1, CH), F32), V((ST, CH), F32), V((1, CH), F32),
            V((TOK, 2 * LANES), BF16), V((1, KEEP), jnp.int32), V((1, KEEP), jnp.int32), V((ST, 2 * LANES), F32),
            V((16, CH), BF16), V((TOK + 16, CH), F32), V((TOK, CH), BF16), V((TOK, RANK + LANES), BF16),
            V((TOK, RANK + LANES), BF16), V((16, RANK + LANES), BF16), V((TOK, RANK + LANES), BF16),
            V((TOK * TILES, LANES), F32), V((TOK * TILES, LANES), F32), V((TOK // 8, 8, 2 * ST * LANES), F32),
            V((ST * TILES, LANES), F32), V((ST * TILES, LANES), F32), V((TOK * ST * TILES, LANES), F32),
            V((TOK * TILES, LANES), F32), V((TOK, CH), F32),
            V((TILES, 1, LANES), F32), V((NZ, 2, 1, LANES), F32), V((ST * TILES, LANES), BF16), V((NZ * 32, LANES), BF16),
            V((2, 1, LANES), F32), V((NX, 2, 1, LANES), F32), V((32, LANES), BF16), V((NX, 32, LANES), BF16),
            V((ST * TILES, LANES), BF16), V((ST * TILES, LANES), BF16), V((ST * TILES, LANES), F32),
            V((NZ * 32, LANES), F32), V((NZ * 32, LANES), F32), V((NZ * 32, LANES), F32),
            V((256, LANES), BF16), V((256, LANES), BF16), V((TOK, 2 * LANES), BF16),
            pltpu.SemaphoreType.DMA((14,)),
            pltpu.SemaphoreType.DMA((10,)), pltpu.SemaphoreType.DMA((10,)),
            pltpu.SemaphoreType.REGULAR((3,)),
        ],
        compiler_params=pltpu.CompilerParams(
            collective_id=0, has_side_effects=True, vmem_limit_bytes=62_000_000
        ),
    )(
        x_in, gate_in, conv_weight, conv_bias.reshape(1, CH), proj_low, proj_bc.T, dt_weight, dt_bias.reshape(1, CH),
        decay_log, skip_gain.reshape(1, CH), attn_kv, kept_index, kept_owner.reshape(1, KEEP),
    )


def solution(mesh):
    return jax.shard_map(
        local,
        mesh=mesh,
        in_specs=(
            P("ctx", "ch"), P("ctx", "ch"), P(None, "ch"), P("ch"), P("ch", None), P("ch", None), P(None, "ch"),
            P("ch"), P(None, "ch"), P("ch"), P("ctx", "ch"), P("ch", "ctx"), P("ch", "ctx", None),
        ),
        out_specs=(P("ctx", "ch"), P("ch", "ctx", None)),
        check_vma=False,
    )
```

```python
import functools
import math

import jax
import jax.numpy as jnp
from jax import lax
from jax.experimental import pallas as pl
from jax.experimental.pallas import tpu as pltpu
from jax.sharding import PartitionSpec as P

MOST = 2
NZ = 16
NX = 4
NC = 8
TOK = 128
CH = 1024
ST = 16
CONV = 4
RANK = 256
LANES = 128
TILES = CH // LANES
KEEP = 32
F32 = jnp.float32
BF16 = jnp.bfloat16
LOG2E = math.log2(math.e)


def dot(a, b):
    return jnp.dot(a, b, preferred_element_type=F32)


def dot_rows(a, b):
    return lax.dot_general(a, b, (((0,), (0,)), ((), ())), preferred_element_type=F32)


def silu(v):
    return v / (1.0 + jnp.exp(-v))


def iota(shape, dim):
    return lax.broadcasted_iota(jnp.int32, shape, dim)


def kernel(
    x_hbm, gate_hbm, cw_hbm, cb_hbm, low_hbm, bc_hbm, dtw_hbm, dtb_hbm, dec_hbm, skip_hbm, kv_hbm, idx_hbm, own_hbm,
    gated_out, kept_out,
    x_v, gate_v, cw_v, cb_v, low_v, bc_v, dtw_v, dtb_v, dec_v, skip_v, kv_v, idx_v, own_v, decs_v,
    halo, halo_out, halo_f, xs, act, part, rs_in, r0_in, ag_out, lr, dtb3, xb3, bcx, a2b, lb, gb, yb, sg,
    s_out, s_in, l_out, l_in, sx_out, sx_in, t_out, t_in, h_out, h_in, hf, decay, reach, before,
    kz_out, kz_in, kx_out,
    in_sem, send_sem, recv_sem, here_sem,
):
    kx_in = kept_out.at[0]
    me = lax.axis_index("ctx")
    mc = lax.axis_index("ch")
    mx = me // NZ
    mz = me % NZ
    mq = mz % 4

    loads = [
        (x_hbm, x_v), (cw_hbm, cw_v), (cb_hbm, cb_v), (idx_hbm, idx_v), (own_hbm, own_v), (kv_hbm, kv_v),
        (low_hbm, low_v), (bc_hbm, bc_v.at[pl.ds(0, 2 * ST), :]), (bc_hbm, bc_v.at[pl.ds(2 * ST, 2 * ST), :]),
        (dec_hbm, dec_v),
        (dec_hbm.at[:, pl.ds(pl.multiple_of(mq * 2 * LANES, 2 * LANES), 2 * LANES)], decs_v),
        (dtw_hbm, dtw_v), (dtb_hbm, dtb_v), (skip_hbm, skip_v), (gate_hbm, gate_v),
    ]
    loads = [pltpu.make_async_copy(s, d, in_sem.at[i]) for i, (s, d) in enumerate(loads)]
    (x_ld, cw_ld, cb_ld, idx_ld, own_ld, kv_ld, low_ld, bc_ld, bc2_ld, dec_ld, decs_ld, dtw_ld, dtb_ld, skip_ld, gate_ld) = loads

    for c in loads:
        c.start()

    def along_z(d):
        return {"ctx": mx * NZ + (mz + d + NZ) % NZ}

    def along_x(d):
        return {"ctx": ((mx + d) % NX) * NZ + mz}

    def along_ch(dy, dc):
        return {"ch": ((mc // 2 + dy) % (NC // 2)) * 2 + (mc + dc) % 2}

    far_z = (8, 7, 9, 6, 10, 5, 11, 4, 12, 3, 13, 2, 14, 1, 15)
    far_x = (2, 1, 3)
    far_ch = ((2, 0), (2, 1), (1, 0), (3, 0), (1, 1), (3, 1), (0, 1))
    right = {"ctx": (me + 1) % (NX * NZ)}
    left = {"ctx": (me + NX * NZ - 1) % (NX * NZ)}
    barrier = pltpu.get_barrier_semaphore()
    for d in far_ch:
        pl.semaphore_signal(barrier, inc=1, device_id=along_ch(*d))
    for d in (-1, 1):
        pl.semaphore_signal(barrier, inc=1, device_id=along_z(d))
    for d in far_x:
        pl.semaphore_signal(barrier, inc=1, device_id=along_x(d))

    @pl.when(mz == NZ - 1)
    def _():
        pl.semaphore_signal(barrier, inc=1, device_id=right)

    @pl.when(mz == 0)
    def _():
        pl.semaphore_signal(barrier, inc=1, device_id=left)

    def tell(i):
        for d in (-(1 << i), 1 << i):
            pl.semaphore_signal(here_sem.at[i], inc=1, device_id=along_z(d))

    def hear(i):
        pl.semaphore_wait(here_sem.at[i], 2)

    def remote(src, dst, k, peer):
        return pltpu.make_async_remote_copy(
            src_ref=src, dst_ref=dst, send_sem=send_sem.at[k], recv_sem=recv_sem.at[k], device_id=peer
        )

    def drain(ref, sem):
        pltpu.make_async_copy(ref, ref, sem).wait()

    HALO, RS, AG, KZ, KX, SZ, LZ, SX, TX, HZ, R0 = range(11)

    bc_v[pl.ds(4 * ST, LANES - 4 * ST), :] = jnp.zeros((LANES - 4 * ST, CH), BF16)

    x_ld.wait()
    for j in range(TILES):
        halo_f[pl.ds(4 * j, 4), :] = x_v[pl.ds(TOK - 16, 16), pl.ds(j * LANES, LANES)].astype(F32)[12:, :]
    halo_out[...] = halo_f[...].astype(BF16)
    pl.semaphore_wait(barrier, NC - 1 + NX - 1 + 2 + jnp.where((mz == 0) | (mz == NZ - 1), 1, 0))

    remote(halo_out, halo, HALO, right).start()
    tell(0)

    def conv(first, rows):
        for j in range(TILES):
            cols = pl.ds(j * LANES, LANES)
            s = jnp.broadcast_to(cb_v[:, cols], (rows, LANES))
            for k in range(CONV):
                s = s + cw_v[pl.ds(k, 1), cols] * xs[pl.ds(first + 16 - (CONV - 1) + k, rows), cols]
            a = silu(s).astype(BF16)
            act[pl.ds(first, rows), cols] = a
            xb3[pl.ds(first * TILES + j, rows, stride=TILES), :] = a.astype(F32)

    def project(first, rows):
        a = act[pl.ds(first, rows), :]
        part[pl.ds(first, rows), pl.ds(0, RANK)] = dot(a, low_v[...]).astype(BF16)
        wide = lax.dot_general(a, bc_v[...], (((1,), (1,)), ((), ())), preferred_element_type=F32)
        high = wide.astype(BF16).astype(F32)
        low = jnp.where(iota((rows, LANES), 1) < 2 * ST, high, wide - high)
        part[pl.ds(first, rows), pl.ds(RANK, LANES)] = low.astype(BF16)

    def summed(ref):
        total = ref[pl.ds(0, 16), :].astype(F32)
        for i in range(1, NC):
            total = total + ref[pl.ds(16 * i, 16), :].astype(F32)
        wide = total[:, RANK:]
        return total[:, :RANK].astype(BF16), (wide + pltpu.roll(wide, LANES - 2 * ST, 1)).astype(BF16)

    def rows_of(i):
        return pl.ds(pl.multiple_of(i * 16, 16), 16)

    cw_ld.wait()
    cb_ld.wait()
    xs[pl.ds(16, TOK), :] = x_v[...].astype(F32)
    conv(16, TOK - 16)
    low_ld.wait()
    bc_ld.wait()
    bc2_ld.wait()
    project(16, TOK - 16)

    for d in far_ch:
        to = along_ch(*d)

        @pl.when(to["ch"] > 0)
        def _():
            remote(part.at[rows_of(to["ch"]), :], rs_in.at[rows_of(mc), :], RS, to).start()

    hear(0)
    tell(1)
    drain(halo, recv_sem.at[HALO])
    halo_f[...] = halo[...].astype(F32)
    for j in range(TILES):
        xs[pl.ds(12, 4), pl.ds(j * LANES, LANES)] = jnp.where(me > 0, halo_f[pl.ds(4 * j, 4), :], 0.0)
    conv(0, 16)
    project(0, 16)
    for d in far_ch:
        remote(part.at[pl.ds(0, 16), :], r0_in.at[rows_of(mc), :], R0, along_ch(*d)).start()
    r0_in[rows_of(mc), :] = part[pl.ds(0, 16), :]

    idx_ld.wait()
    own_ld.wait()
    kv_ld.wait()
    own_row = own_v[...]
    eye = iota((KEEP, KEEP), 0) == iota((KEEP, KEEP), 1)
    own = jnp.sum(jnp.where(eye, own_row, 0), axis=1, keepdims=True)
    same = (own_row == own) & (iota((KEEP, KEEP), 1) < iota((KEEP, KEEP), 0))
    rank = jnp.sum(jnp.where(same, 1, 0), axis=1, keepdims=True)
    place = (own & (NZ - 1)) * 16 + (own >> 4) * 2 + rank
    src_t = (iota((TOK, KEEP), 0) == idx_v[...] - me * TOK).astype(F32).astype(BF16)
    picked = dot_rows(src_t, kv_v[...]).astype(BF16)
    slots = iota((KEEP, 256), 1)
    kz = dot_rows((slots == place).astype(F32).astype(BF16), picked[:, :LANES])
    kz = kz + dot_rows((slots == place + 8).astype(F32).astype(BF16), picked[:, LANES:])
    kz_out[...] = kz.astype(BF16)

    hear(1)
    tell(2)

    dec_ld.wait()
    decs_ld.wait()
    gate_ld.wait()
    for j in range(TILES):
        a2b[pl.ds(j, ST, stride=TILES), :] = -LOG2E * jnp.exp(dec_v[:, pl.ds(j * LANES, LANES)])
    a2s = [-LOG2E * jnp.exp(decs_v[:, pl.ds(jj * LANES, LANES)]) for jj in range(2)]
    sg[...] = silu(gate_v[...].astype(F32))

    @pl.when(mc > 0)
    def _():
        rs_in[rows_of(mc), :] = part[rows_of(mc), :]
        drain(rs_in.at[pl.ds(0, TOK - 16), :], recv_sem.at[RS])
        low, coeff = summed(rs_in)
        ag_out[:, pl.ds(0, RANK)] = low
        ag_out[:, pl.ds(RANK, LANES)] = coeff
        for d in far_ch:
            remote(ag_out, lr.at[rows_of(mc), :], AG, along_ch(*d)).start()
        lr[rows_of(mc), :] = ag_out[...]

    hear(2)
    for d in far_z:
        to = (mz + d) % NZ
        remote(kz_out.at[rows_of(to), :], kz_in.at[rows_of(mz), :], KZ, along_z(d)).start()
    kz_in[rows_of(mz), :] = kz_out[rows_of(mz), :]

    dtw_ld.wait()
    dtb_ld.wait()
    skip_ld.wait()
    drain(r0_in.at[pl.ds(0, TOK - 16), :], recv_sem.at[R0])
    low, coeff = summed(r0_in)
    lr[pl.ds(0, 16), pl.ds(0, RANK)] = low
    lr[pl.ds(0, 16), pl.ds(RANK, LANES)] = coeff

    @pl.when(mc > 0)
    def _():
        drain(lr.at[pl.ds(0, TOK - 32), :], recv_sem.at[AG])

    @pl.when(mc == 0)
    def _():
        drain(lr.at[pl.ds(0, TOK - 16), :], recv_sem.at[AG])

    for j in range(TILES):
        cols = pl.ds(j * LANES, LANES)
        v = dot(lr[:, pl.ds(0, RANK)], dtw_v[:, cols]) + dtb_v[:, cols]
        dtb3[pl.ds(j, TOK, stride=TILES), :] = jnp.maximum(v, 0.0) + jnp.log1p(jnp.exp(-jnp.abs(v)))
    coeff = lr[:, pl.ds(RANK, LANES)]

    def spread(i):
        rows = (iota((LANES, 4 * LANES), 1) >> 7) + 4 * i == iota((LANES, 4 * LANES), 0)
        wide = dot(coeff, rows.astype(F32).astype(BF16))
        bcx[:, :, pl.ds(i * 4 * LANES, 4 * LANES)] = wide.reshape(TOK // 8, 8, 4 * LANES)

    for i in range(4):
        spread(i)

    def token(g, u):
        return pl.ds(pl.multiple_of(g * 64, 64) + u * 8, 8)

    def total_step(g, acc):
        for u in range(8):
            acc = acc + dtb3[token(g, u), :]
        return acc

    s_total = lax.fori_loop(0, TOK // 8, total_step, jnp.zeros((TILES, LANES), F32))
    for j in range(TILES):
        s_out[j] = s_total[j : j + 1, :]
    for d in far_z:
        to = (mz + d) % 4
        remote(s_out.at[pl.ds(2 * to, 2)], s_in.at[mz], SZ, along_z(d)).start()
    s_in[mz] = s_out[pl.ds(2 * mq, 2)]

    def end_step(g, state):
        state = list(state)
        for u in range(8):
            dt = dtb3[token(g, u), :]
            dx = dt * xb3[token(g, u), :]
            for n in range(ST):
                b = bcx[g, pl.ds(u, 1), pl.ds(n * LANES, LANES)]
                state[n] = jnp.exp2(dt * a2b[pl.ds(n * 8, 8), :]) * state[n] + dx * b
        return tuple(state)

    empty = tuple(jnp.zeros((TILES, LANES), F32) for _ in range(ST))
    state = lax.fori_loop(0, TOK // 8, end_step, empty)
    for n in range(ST):
        lb[pl.ds(n * 8, 8), :] = state[n]
    for j in range(TILES):
        l_out[pl.ds(j * ST, ST), :] = lb[pl.ds(j, ST, stride=TILES), :].astype(BF16)

    def block_of(i):
        return pl.ds(pl.multiple_of(i * 32, 32), 32)

    for d in far_z:
        to = (mz + d) % 4
        remote(l_out.at[block_of(to), :], l_in.at[block_of(mz), :], LZ, along_z(d)).start()
    l_in[block_of(mz), :] = l_out[block_of(mq), :]

    for i in range(4, 8):
        spread(i)

    def scan_step(g, state):
        state = list(state)
        for u in range(8):
            dt = dtb3[token(g, u), :]
            dx = dt * xb3[token(g, u), :]
            y = [None] * 4
            for n in range(ST):
                b = bcx[g, pl.ds(u, 1), pl.ds(n * LANES, LANES)]
                c = bcx[g, pl.ds(u, 1), pl.ds((ST + n) * LANES, LANES)]
                state[n] = jnp.exp2(dt * a2b[pl.ds(n * 8, 8), :]) * state[n] + dx * b
                term = c * state[n]
                y[n % 4] = term if y[n % 4] is None else y[n % 4] + term
            yb[token(g, u), :] = (y[0] + y[1]) + (y[2] + y[3])
        return tuple(state)

    lax.fori_loop(0, TOK // 8, scan_step, empty)

    def reach_step(g, cum):
        for u in range(8):
            cum = cum + dtb3[token(g, u), :]
            for n in range(ST):
                c = bcx[g, pl.ds(u, 1), pl.ds((ST + n) * LANES, LANES)]
                gb[pl.ds(pl.multiple_of(g * 1024, 1024) + u * 128 + n * 8, 8), :] = c * jnp.exp2(cum * a2b[pl.ds(n * 8, 8), :])
        return cum

    lax.fori_loop(0, TOK // 8, reach_step, jnp.zeros((TILES, LANES), F32))

    drain(kz_in.at[pl.ds(0, 240), :], recv_sem.at[KZ])
    row = iota((TOK, 256), 0)
    want = ((row >> 1) & (NZ - 1)) * 16 + (row >> 5) * 2 + (row & 1)
    for half in range(2):
        sel = (iota((TOK, 256), 1) == want + half * 8).astype(F32).astype(BF16)
        kx_out[:, pl.ds(half * LANES, LANES)] = dot(sel, kz_in[...]).astype(BF16)

    for d in far_x:
        to = (mx + d) % NX
        remote(kx_out.at[block_of(to), :], kx_in.at[block_of(mx), :], KX, along_x(d)).start()
    kx_in[block_of(mx), :] = kx_out[block_of(mx), :]

    drain(s_in.at[pl.ds(0, NZ - 1)], recv_sem.at[SZ])
    for jj in range(2):
        run = jnp.zeros((1, LANES), F32)
        for z in range(NZ):
            rows = pl.ds(z * 32 + jj * ST, ST)
            decay[rows, :] = jnp.exp2(a2s[jj] * s_in[z, jj])
            reach[rows, :] = jnp.exp2(a2s[jj] * run)
            run = run + s_in[z, jj]
        sx_out[jj] = run
    for d in far_x:
        remote(sx_out, sx_in.at[mx], SX, along_x(d)).start()
    sx_in[mx] = sx_out[...]

    drain(l_in.at[pl.ds(0, 480), :], recv_sem.at[LZ])
    for jj in range(2):
        carry = jnp.zeros((ST, LANES), F32)
        for z in range(NZ):
            rows = pl.ds(z * 32 + jj * ST, ST)
            before[rows, :] = carry
            carry = decay[rows, :] * carry + l_in[rows, :].astype(F32)
        t_out[pl.ds(jj * ST, ST), :] = carry.astype(BF16)
    for d in far_x:
        remote(t_out, t_in.at[mx], TX, along_x(d)).start()
    t_in[mx] = t_out[...]
    drain(sx_in.at[pl.ds(0, NX - 1)], recv_sem.at[SX])
    drain(t_in.at[pl.ds(0, NX - 1)], recv_sem.at[TX])
    plane = []
    for jj in range(2):
        p = jnp.zeros((ST, LANES), F32)
        for i in range(NX - 1):
            later = jnp.exp2(a2s[jj] * sx_in[i, jj]) * p + t_in[i, pl.ds(jj * ST, ST), :].astype(F32)
            p = jnp.where(i < mx, later, p)
        plane.append(p)

    for k, d in enumerate((-2, -1, 1, 0)):
        z = (mz + d + NZ) % NZ
        for jj in range(2):
            rows = pl.ds(pl.multiple_of(z * 32, 32) + jj * ST, ST)
            h_out[pl.ds(k * 32 + jj * ST, ST), :] = (before[rows, :] + reach[rows, :] * plane[jj]).astype(BF16)
        if d:
            remote(h_out.at[pl.ds(k * 32, 32), :], h_in.at[block_of(mq), :], HZ, along_z(d)).start()
    h_in[block_of(mq), :] = h_out[pl.ds(96, 32), :]
    drain(h_in.at[pl.ds(0, 96), :], recv_sem.at[HZ])
    hf[...] = h_in[...].astype(F32)

    carried = [hf[pl.ds(n, TILES, stride=ST), :] for n in range(ST)]

    def add_step(g, _):
        for u in range(8):
            at = token(g, u)
            y = [yb[at, :], None, None, None]
            for n in range(ST):
                term = gb[pl.ds(pl.multiple_of(g * 1024, 1024) + u * 128 + n * 8, 8), :] * carried[n]
                y[n % 4] = term if y[n % 4] is None else y[n % 4] + term
            yb[at, :] = (y[0] + y[1]) + (y[2] + y[3])
        return 0

    lax.fori_loop(0, TOK // 8, add_step, 0)

    for j in range(TILES):
        cols = pl.ds(j * LANES, LANES)
        y = yb[pl.ds(j, TOK, stride=TILES), :] + skip_v[:, cols] * act[:, cols].astype(F32)
        gated_out[:, cols] = (y * sg[:, cols]).astype(BF16)
    drain(kx_in.at[pl.ds(0, 96), :], recv_sem.at[KX])

    drain(halo, send_sem.at[HALO])
    drain(r0_in.at[pl.ds(0, TOK - 16), :], send_sem.at[R0])

    @pl.when(mc > 0)
    def _():
        drain(rs_in.at[pl.ds(0, TOK - 32), :], send_sem.at[RS])
        drain(lr.at[pl.ds(0, TOK - 16), :], send_sem.at[AG])

    @pl.when(mc == 0)
    def _():
        drain(rs_in.at[pl.ds(0, TOK - 16), :], send_sem.at[RS])

    drain(kz_in.at[pl.ds(0, 240), :], send_sem.at[KZ])
    drain(kx_in.at[pl.ds(0, 96), :], send_sem.at[KX])
    drain(s_in.at[pl.ds(0, NZ - 1)], send_sem.at[SZ])
    drain(l_in.at[pl.ds(0, 480), :], send_sem.at[LZ])
    drain(sx_in.at[pl.ds(0, NX - 1)], send_sem.at[SX])
    drain(t_in.at[pl.ds(0, NX - 1)], send_sem.at[TX])
    drain(h_in.at[pl.ds(0, 96), :], send_sem.at[HZ])


def local(
    x_in, gate_in, conv_weight, conv_bias, proj_low, proj_bc, dt_weight, dt_bias, decay_log, skip_gain, attn_kv,
    kept_index, kept_owner,
):
    V = pltpu.VMEM
    hbm = pl.BlockSpec(memory_space=pltpu.HBM)
    return pl.pallas_call(
        kernel,
        out_shape=(pltpu.VMEM((TOK, CH), BF16), pltpu.VMEM((1, TOK, 2 * LANES), BF16)),
        in_specs=[hbm] * 13,
        out_specs=(pl.BlockSpec(memory_space=pltpu.VMEM),) * 2,
        scratch_shapes=[
            V((TOK, CH), BF16), V((TOK, CH), BF16), V((CONV, CH), F32), V((1, CH), F32), V((CH, RANK), BF16),
            V((LANES, CH), BF16), V((RANK, CH), BF16), V((1, CH), F32), V((ST, CH), F32), V((1, CH), F32),
            V((TOK, 2 * LANES), BF16), V((1, KEEP), jnp.int32), V((1, KEEP), jnp.int32), V((ST, 2 * LANES), F32),
            V((32, LANES), BF16), V((32, LANES), BF16), V((32, LANES), F32), V((TOK + 16, CH), F32), V((TOK, CH), BF16),
            V((TOK, RANK + LANES), BF16), V((TOK, RANK + LANES), BF16), V((TOK, RANK + LANES), BF16), V((16, RANK + LANES), BF16), V((TOK, RANK + LANES), BF16),
            V((TOK * TILES, LANES), F32), V((TOK * TILES, LANES), F32), V((TOK // 8, 8, 2 * ST * LANES), F32),
            V((ST * TILES, LANES), F32), V((ST * TILES, LANES), F32), V((TOK * ST * TILES, LANES), F32),
            V((TOK * TILES, LANES), F32), V((TOK, CH), F32),
            V((TILES, 1, LANES), F32), V((NZ, 2, 1, LANES), F32), V((ST * TILES, LANES), BF16), V((NZ * 32, LANES), BF16),
            V((2, 1, LANES), F32), V((NX, 2, 1, LANES), F32), V((32, LANES), BF16), V((NX, 32, LANES), BF16),
            V((ST * TILES, LANES), BF16), V((ST * TILES, LANES), BF16), V((ST * TILES, LANES), F32),
            V((NZ * 32, LANES), F32), V((NZ * 32, LANES), F32), V((NZ * 32, LANES), F32),
            V((256, LANES), BF16), V((256, LANES), BF16), V((TOK, 2 * LANES), BF16),
            pltpu.SemaphoreType.DMA((15,)),
            pltpu.SemaphoreType.DMA((11,)), pltpu.SemaphoreType.DMA((11,)),
            pltpu.SemaphoreType.REGULAR((3,)),
        ],
        compiler_params=pltpu.CompilerParams(
            collective_id=0, has_side_effects=True, vmem_limit_bytes=62_000_000
        ),
    )(
        x_in, gate_in, conv_weight, conv_bias.reshape(1, CH), proj_low, proj_bc.T, dt_weight, dt_bias.reshape(1, CH),
        decay_log, skip_gain.reshape(1, CH), attn_kv, kept_index, kept_owner.reshape(1, KEEP),
    )


def solution(mesh):
    return jax.shard_map(
        local,
        mesh=mesh,
        in_specs=(
            P("ctx", "ch"), P("ctx", "ch"), P(None, "ch"), P("ch"), P("ch", None), P("ch", None), P(None, "ch"),
            P("ch"), P(None, "ch"), P("ch"), P("ctx", "ch"), P("ch", "ctx"), P("ch", "ctx", None),
        ),
        out_specs=(P("ctx", "ch"), P("ch", "ctx", None)),
        check_vma=False,
    )
```

```python
import functools
import math

import jax
import jax.numpy as jnp
from jax import lax
from jax.experimental import pallas as pl
from jax.experimental.pallas import tpu as pltpu
from jax.sharding import PartitionSpec as P

MOST = 2
NZ = 16
NX = 4
NC = 8
TOK = 128
CH = 1024
ST = 16
CONV = 4
RANK = 256
LANES = 128
TILES = CH // LANES
KEEP = 32
F32 = jnp.float32
BF16 = jnp.bfloat16
LOG2E = math.log2(math.e)


def dot(a, b):
    return jnp.dot(a, b, preferred_element_type=F32)


def dot_rows(a, b):
    return lax.dot_general(a, b, (((0,), (0,)), ((), ())), preferred_element_type=F32)


def silu(v):
    return v / (1.0 + jnp.exp(-v))


def iota(shape, dim):
    return lax.broadcasted_iota(jnp.int32, shape, dim)


def kernel(
    x_hbm, gate_hbm, cw_hbm, cb_hbm, low_hbm, bc_hbm, dtw_hbm, dtb_hbm, dec_hbm, skip_hbm, kv_hbm, idx_hbm, own_hbm,
    gated_out, kept_out,
    x_v, gate_v, cw_v, cb_v, low_v, bc_v, dtw_v, dtb_v, dec_v, skip_v, kv_v, idx_v, own_v, decs_v,
    halo, halo_out, halo_f, xs, act, part, rs_in, r0_in, ag_out, lr, dtb3, xb3, bcx, a2b, a2n, lb, gb, yb, sgb, skip_b,
    s_out, s_in, l_out, l_in, sx_out, sx_in, cum_out, cum_in, t_out, t_in, before, h_in, hf, decay, reach,
    plane, carry_x,
    kz_out, kz_in, kx_out,
    in_sem, send_sem, recv_sem, here_sem,
):
    kx_in = kept_out.at[0]
    me = lax.axis_index("ctx")
    mc = lax.axis_index("ch")
    mx = me // NZ
    mz = me % NZ
    mq = mz % 4

    loads = [
        (x_hbm, x_v), (cw_hbm, cw_v), (cb_hbm, cb_v), (idx_hbm, idx_v), (own_hbm, own_v), (kv_hbm, kv_v),
        (low_hbm, low_v), (bc_hbm, bc_v.at[pl.ds(0, 2 * ST), :]), (bc_hbm, bc_v.at[pl.ds(2 * ST, 2 * ST), :]),
        (dec_hbm, dec_v),
        (dec_hbm.at[:, pl.ds(pl.multiple_of(mq * 2 * LANES, 2 * LANES), 2 * LANES)], decs_v),
        (dtw_hbm, dtw_v), (dtb_hbm, dtb_v), (skip_hbm, skip_v), (gate_hbm, gate_v),
    ]
    loads = [pltpu.make_async_copy(s, d, in_sem.at[i]) for i, (s, d) in enumerate(loads)]
    (x_ld, cw_ld, cb_ld, idx_ld, own_ld, kv_ld, low_ld, bc_ld, bc2_ld, dec_ld, decs_ld, dtw_ld, dtb_ld, skip_ld, gate_ld) = loads

    for c in loads:
        c.start()

    def along_z(d):
        return {"ctx": mx * NZ + (mz + d + NZ) % NZ}

    def along_x(d):
        return {"ctx": ((mx + d) % NX) * NZ + mz}

    def along_xz(dx, dz):
        return {"ctx": ((mx + dx) % NX) * NZ + (mz + dz + NZ) % NZ}

    def along_ch(dy, dc):
        return {"ch": ((mc // 2 + dy) % (NC // 2)) * 2 + (mc + dc) % 2}

    far_z = (8, 7, 9, 6, 10, 5, 11, 4, 12, 3, 13, 2, 14, 1, 15)
    far_x = (2, 1, 3)
    far_ch = ((2, 0), (2, 1), (1, 0), (3, 0), (1, 1), (3, 1), (0, 1))
    right = {"ctx": (me + 1) % (NX * NZ)}
    left = {"ctx": (me + NX * NZ - 1) % (NX * NZ)}
    barrier = pltpu.get_barrier_semaphore()
    for d in far_ch:
        pl.semaphore_signal(barrier, inc=1, device_id=along_ch(*d))
    for d in (-1, 1):
        pl.semaphore_signal(barrier, inc=1, device_id=along_z(d))
    for d in far_x:
        pl.semaphore_signal(barrier, inc=1, device_id=along_x(d))

    @pl.when(mz == NZ - 1)
    def _():
        pl.semaphore_signal(barrier, inc=1, device_id=right)

    @pl.when(mz == 0)
    def _():
        pl.semaphore_signal(barrier, inc=1, device_id=left)

    def tell(i):
        for d in (-(1 << i), 1 << i):
            pl.semaphore_signal(here_sem.at[i], inc=1, device_id=along_z(d))

    def hear(i):
        pl.semaphore_wait(here_sem.at[i], 2)

    def tell_x():
        for d in far_x:
            pl.semaphore_signal(here_sem.at[3], inc=1, device_id=along_x(d))

    def hear_x():
        pl.semaphore_wait(here_sem.at[3], NX - 1)

    def remote(src, dst, k, peer):
        return pltpu.make_async_remote_copy(
            src_ref=src, dst_ref=dst, send_sem=send_sem.at[k], recv_sem=recv_sem.at[k], device_id=peer
        )

    def drain(ref, sem):
        pltpu.make_async_copy(ref, ref, sem).wait()

    HALO, RS, AG, KZ, KX, SZ, LZ, CZ, HZ, R0, CX, TX = (0, 1, 2, 3, 4, 5, 6, 7, 8, 9, 10, 13)

    bc_v[pl.ds(4 * ST, LANES - 4 * ST), :] = jnp.zeros((LANES - 4 * ST, CH), BF16)

    x_ld.wait()
    for j in range(TILES):
        halo_f[pl.ds(4 * j, 4), :] = x_v[pl.ds(TOK - 16, 16), pl.ds(j * LANES, LANES)].astype(F32)[12:, :]
    halo_out[...] = halo_f[...].astype(BF16)
    pl.semaphore_wait(barrier, NC - 1 + NX - 1 + 2 + jnp.where((mz == 0) | (mz == NZ - 1), 1, 0))

    remote(halo_out, halo, HALO, right).start()
    tell(0)

    def conv(first, rows):
        for j in range(TILES):
            cols = pl.ds(j * LANES, LANES)
            s = jnp.broadcast_to(cb_v[:, cols], (rows, LANES))
            for k in range(CONV):
                s = s + cw_v[pl.ds(k, 1), cols] * xs[pl.ds(first + 16 - (CONV - 1) + k, rows), cols]
            a = silu(s).astype(BF16)
            act[pl.ds(first, rows), cols] = a
            xb3[pl.ds(first * TILES + j, rows, stride=TILES), :] = a.astype(F32)

    def project(first, rows):
        a = act[pl.ds(first, rows), :]
        part[pl.ds(first, rows), pl.ds(0, RANK)] = dot(a, low_v[...]).astype(BF16)
        wide = lax.dot_general(a, bc_v[...], (((1,), (1,)), ((), ())), preferred_element_type=F32)
        high = wide.astype(BF16).astype(F32)
        low = jnp.where(iota((rows, LANES), 1) < 2 * ST, high, wide - high)
        part[pl.ds(first, rows), pl.ds(RANK, LANES)] = low.astype(BF16)

    def summed(ref):
        total = ref[pl.ds(0, 16), :].astype(F32)
        for i in range(1, NC):
            total = total + ref[pl.ds(16 * i, 16), :].astype(F32)
        wide = total[:, RANK:]
        return total[:, :RANK].astype(BF16), (wide + pltpu.roll(wide, LANES - 2 * ST, 1)).astype(BF16)

    def rows_of(i):
        return pl.ds(pl.multiple_of(i * 16, 16), 16)

    cw_ld.wait()
    cb_ld.wait()
    xs[pl.ds(16, TOK), :] = x_v[...].astype(F32)
    conv(16, TOK - 16)
    low_ld.wait()
    bc_ld.wait()
    bc2_ld.wait()
    project(16, TOK - 16)

    for d in far_ch:
        to = along_ch(*d)

        @pl.when(to["ch"] > 0)
        def _():
            remote(part.at[rows_of(to["ch"]), :], rs_in.at[rows_of(mc), :], RS, to).start()

    hear(0)
    tell(1)
    tell_x()
    drain(halo, recv_sem.at[HALO])
    halo_f[...] = halo[...].astype(F32)
    for j in range(TILES):
        xs[pl.ds(12, 4), pl.ds(j * LANES, LANES)] = jnp.where(me > 0, halo_f[pl.ds(4 * j, 4), :], 0.0)
    conv(0, 16)
    project(0, 16)
    for d in far_ch:
        remote(part.at[pl.ds(0, 16), :], r0_in.at[rows_of(mc), :], R0, along_ch(*d)).start()
    r0_in[rows_of(mc), :] = part[pl.ds(0, 16), :]

    idx_ld.wait()
    own_ld.wait()
    kv_ld.wait()
    own_row = own_v[...]
    eye = iota((KEEP, KEEP), 0) == iota((KEEP, KEEP), 1)
    own = jnp.sum(jnp.where(eye, own_row, 0), axis=1, keepdims=True)
    same = (own_row == own) & (iota((KEEP, KEEP), 1) < iota((KEEP, KEEP), 0))
    rank = jnp.sum(jnp.where(same, 1, 0), axis=1, keepdims=True)
    place = (own & (NZ - 1)) * 16 + (own >> 4) * 2 + rank
    src_t = (iota((TOK, KEEP), 0) == idx_v[...] - me * TOK).astype(F32).astype(BF16)
    picked = dot_rows(src_t, kv_v[...]).astype(BF16)
    slots = iota((KEEP, 256), 1)
    kz = dot_rows((slots == place).astype(F32).astype(BF16), picked[:, :LANES])
    kz = kz + dot_rows((slots == place + 8).astype(F32).astype(BF16), picked[:, LANES:])
    kz_out[...] = kz.astype(BF16)

    hear(1)
    tell(2)

    dec_ld.wait()
    decs_ld.wait()
    gate_ld.wait()
    for j in range(TILES):
        rate = -LOG2E * jnp.exp(dec_v[:, pl.ds(j * LANES, LANES)])
        a2n[pl.ds(j * ST, ST), :] = rate
        a2b[pl.ds(j, ST, stride=TILES), :] = rate
    a2s = [-LOG2E * jnp.exp(decs_v[:, pl.ds(jj * LANES, LANES)]) for jj in range(2)]
    skip_ld.wait()
    for j in range(TILES):
        cols = pl.ds(j * LANES, LANES)
        sgb[pl.ds(j, TOK, stride=TILES), :] = silu(gate_v[:, cols].astype(F32))
        skip_b[pl.ds(j, 1), :] = skip_v[:, cols]

    @pl.when(mc > 0)
    def _():
        rs_in[rows_of(mc), :] = part[rows_of(mc), :]
        drain(rs_in.at[pl.ds(0, TOK - 16), :], recv_sem.at[RS])
        low, coeff = summed(rs_in)
        ag_out[:, pl.ds(0, RANK)] = low
        ag_out[:, pl.ds(RANK, LANES)] = coeff
        for d in far_ch:
            remote(ag_out, lr.at[rows_of(mc), :], AG, along_ch(*d)).start()
        lr[rows_of(mc), :] = ag_out[...]

    hear(2)
    hear_x()
    for d in far_z:
        to = (mz + d) % NZ
        remote(kz_out.at[rows_of(to), :], kz_in.at[rows_of(mz), :], KZ, along_z(d)).start()
    kz_in[rows_of(mz), :] = kz_out[rows_of(mz), :]

    dtw_ld.wait()
    dtb_ld.wait()
    drain(r0_in.at[pl.ds(0, TOK - 16), :], recv_sem.at[R0])
    low, coeff = summed(r0_in)
    lr[pl.ds(0, 16), pl.ds(0, RANK)] = low
    lr[pl.ds(0, 16), pl.ds(RANK, LANES)] = coeff

    @pl.when(mc > 0)
    def _():
        drain(lr.at[pl.ds(0, TOK - 32), :], recv_sem.at[AG])

    @pl.when(mc == 0)
    def _():
        drain(lr.at[pl.ds(0, TOK - 16), :], recv_sem.at[AG])

    for j in range(TILES):
        cols = pl.ds(j * LANES, LANES)
        v = dot(lr[:, pl.ds(0, RANK)], dtw_v[:, cols]) + dtb_v[:, cols]
        dtb3[pl.ds(j, TOK, stride=TILES), :] = jnp.maximum(v, 0.0) + jnp.log1p(jnp.exp(-jnp.abs(v)))
    coeff = lr[:, pl.ds(RANK, LANES)]

    def spread(i):
        rows = (iota((LANES, 4 * LANES), 1) >> 7) + 4 * i == iota((LANES, 4 * LANES), 0)
        wide = dot(coeff, rows.astype(F32).astype(BF16))
        bcx[:, :, pl.ds(i * 4 * LANES, 4 * LANES)] = wide.reshape(TOK // 8, 8, 4 * LANES)

    for i in range(4):
        spread(i)

    def token(g, u):
        return pl.ds(pl.multiple_of(g * 64, 64) + u * 8, 8)

    def total_step(g, acc):
        for u in range(8):
            acc = acc + dtb3[token(g, u), :]
        return acc

    s_total = lax.fori_loop(0, TOK // 8, total_step, jnp.zeros((TILES, LANES), F32))
    for j in range(TILES):
        s_out[j] = s_total[j : j + 1, :]
    for d in far_z:
        to = (mz + d) % 4
        remote(s_out.at[pl.ds(2 * to, 2)], s_in.at[mz], SZ, along_z(d)).start()
    s_in[mz] = s_out[pl.ds(2 * mq, 2)]

    def end_step(g, state):
        state = list(state)
        for u in range(8):
            dt = dtb3[token(g, u), :]
            dx = dt * xb3[token(g, u), :]
            for n in range(ST):
                b = bcx[g, pl.ds(u, 1), pl.ds(n * LANES, LANES)]
                state[n] = jnp.exp2(dt * a2b[pl.ds(n * 8, 8), :]) * state[n] + dx * b
        return tuple(state)

    empty = tuple(jnp.zeros((TILES, LANES), F32) for _ in range(ST))
    state = lax.fori_loop(0, TOK // 8, end_step, empty)
    for n in range(ST):
        lb[pl.ds(n * 8, 8), :] = state[n]
    for j in range(TILES):
        l_out[pl.ds(j * ST, ST), :] = lb[pl.ds(j, ST, stride=TILES), :].astype(BF16)

    def block_of(i):
        return pl.ds(pl.multiple_of(i * 32, 32), 32)

    for d in far_z:
        to = (mz + d) % 4
        remote(l_out.at[block_of(to), :], l_in.at[block_of(mz), :], LZ, along_z(d)).start()
    l_in[block_of(mz), :] = l_out[block_of(mq), :]

    for i in range(4, 8):
        spread(i)

    def scan_step(g, state):
        state = list(state)
        for u in range(8):
            dt = dtb3[token(g, u), :]
            xt = xb3[token(g, u), :]
            dx = dt * xt
            y = [skip_b[...] * xt, None, None, None]
            for n in range(ST):
                b = bcx[g, pl.ds(u, 1), pl.ds(n * LANES, LANES)]
                c = bcx[g, pl.ds(u, 1), pl.ds((ST + n) * LANES, LANES)]
                state[n] = jnp.exp2(dt * a2b[pl.ds(n * 8, 8), :]) * state[n] + dx * b
                term = c * state[n]
                y[n % 4] = term if y[n % 4] is None else y[n % 4] + term
            yb[token(g, u), :] = ((y[0] + y[1]) + (y[2] + y[3])) * sgb[token(g, u), :]
        return tuple(state)

    lax.fori_loop(0, TOK // 8, scan_step, empty)

    def reach_step(g, cum):
        for u in range(8):
            cum = cum + dtb3[token(g, u), :]
            sgt = sgb[token(g, u), :]
            for n in range(ST):
                c = bcx[g, pl.ds(u, 1), pl.ds((ST + n) * LANES, LANES)]
                gb[pl.ds(pl.multiple_of(g * 1024, 1024) + u * 128 + n * 8, 8), :] = (c * sgt) * jnp.exp2(cum * a2b[pl.ds(n * 8, 8), :])
        return cum

    lax.fori_loop(0, TOK // 8, reach_step, jnp.zeros((TILES, LANES), F32))

    drain(kz_in.at[pl.ds(0, 240), :], recv_sem.at[KZ])
    row = iota((TOK, 256), 0)
    want = ((row >> 1) & (NZ - 1)) * 16 + (row >> 5) * 2 + (row & 1)
    for half in range(2):
        sel = (iota((TOK, 256), 1) == want + half * 8).astype(F32).astype(BF16)
        kx_out[:, pl.ds(half * LANES, LANES)] = dot(sel, kz_in[...]).astype(BF16)

    for d in far_x:
        to = (mx + d) % NX
        remote(kx_out.at[block_of(to), :], kx_in.at[block_of(mx), :], KX, along_x(d)).start()
    kx_in[block_of(mx), :] = kx_out[block_of(mx), :]

    drain(s_in.at[pl.ds(0, NZ - 1)], recv_sem.at[SZ])
    for jj in range(2):
        run = jnp.zeros((1, LANES), F32)
        for z in range(NZ):
            decay[pl.ds(z * 32 + jj * ST, ST), :] = jnp.exp2(a2s[jj] * s_in[z, jj])
            cum_out[z, jj] = run
            run = run + s_in[z, jj]
        sx_out[jj] = run

    def pair_of(i):
        return pl.ds(2 * i, 2)

    def to_planes(src, dst, k):
        for dx in (3, 2, 1):

            @pl.when(mx + dx < NX)
            def _():
                for dz in (-2, -1, 1, 0):
                    pltpu.make_async_remote_copy(
                        src_ref=src, dst_ref=dst, send_sem=send_sem.at[k + dx - 1], recv_sem=recv_sem.at[k + mx],
                        device_id=along_xz(dx, dz),
                    ).start()

    @pl.when(mx < NX - 1)
    def _():
        to_planes(sx_out, sx_in.at[mx, pair_of(mq)], CX)

    for dz in (-2, -1, 1):
        remote(cum_out.at[(mz + dz + NZ) % NZ], cum_in.at[pair_of(mq)], CZ, along_z(dz)).start()
    cum_in[pair_of(mq)] = cum_out[mz]

    drain(l_in.at[pl.ds(0, 480), :], recv_sem.at[LZ])
    for jj in range(2):
        carry = jnp.zeros((ST, LANES), F32)
        for z in range(NZ):
            rows = pl.ds(z * 32 + jj * ST, ST)
            before[rows, :] = carry.astype(BF16)
            carry = decay[rows, :] * carry + l_in[rows, :].astype(F32)
        t_out[pl.ds(jj * ST, ST), :] = carry.astype(BF16)

    @pl.when(mx < NX - 1)
    def _():
        to_planes(t_out, t_in.at[mx, block_of(mq)], TX)

    for dz in (-2, -1, 1):
        remote(before.at[block_of((mz + dz + NZ) % NZ), :], h_in.at[block_of(mq), :], HZ, along_z(dz)).start()
    h_in[block_of(mq), :] = before[block_of(mz), :]

    carry_x[...] = jnp.zeros_like(carry_x)
    for i in range(NX - 1):

        @pl.when(i < mx)
        def _():
            drain(sx_in.at[i], recv_sem.at[CX + i])
            for j in range(TILES):
                rows = pl.ds(j * ST, ST)
                plane[pl.ds(i * 128 + j * ST, ST), :] = jnp.exp2(a2n[rows, :] * sx_in[i, j])

    drain(cum_in.at[pl.ds(0, 6)], recv_sem.at[CZ])
    for j in range(TILES):
        rows = pl.ds(j * ST, ST)
        reach[rows, :] = jnp.exp2(a2n[rows, :] * cum_in[j])
    for i in range(NX - 1):

        @pl.when(i < mx)
        def _():
            drain(t_in.at[i], recv_sem.at[TX + i])
            carry_x[...] = plane[pl.ds(i * 128, 128), :] * carry_x[...] + t_in[i].astype(F32)

    drain(h_in.at[pl.ds(0, 96), :], recv_sem.at[HZ])
    hf[...] = h_in[...].astype(F32) + reach[...] * carry_x[...]

    carried = [hf[pl.ds(n, TILES, stride=ST), :] for n in range(ST)]

    def add_step(g, _):
        for u in range(8):
            at = token(g, u)
            y = [yb[at, :], None, None, None]
            for n in range(ST):
                term = gb[pl.ds(pl.multiple_of(g * 1024, 1024) + u * 128 + n * 8, 8), :] * carried[n]
                y[n % 4] = term if y[n % 4] is None else y[n % 4] + term
            yb[at, :] = (y[0] + y[1]) + (y[2] + y[3])
        return 0

    lax.fori_loop(0, TOK // 8, add_step, 0)

    for j in range(TILES):
        cols = pl.ds(j * LANES, LANES)
        gated_out[:, cols] = yb[pl.ds(j, TOK, stride=TILES), :].astype(BF16)
    drain(kx_in.at[pl.ds(0, 96), :], recv_sem.at[KX])

    drain(halo, send_sem.at[HALO])
    drain(r0_in.at[pl.ds(0, TOK - 16), :], send_sem.at[R0])

    @pl.when(mc > 0)
    def _():
        drain(rs_in.at[pl.ds(0, TOK - 32), :], send_sem.at[RS])
        drain(lr.at[pl.ds(0, TOK - 16), :], send_sem.at[AG])

    @pl.when(mc == 0)
    def _():
        drain(rs_in.at[pl.ds(0, TOK - 16), :], send_sem.at[RS])

    drain(kz_in.at[pl.ds(0, 240), :], send_sem.at[KZ])
    drain(kx_in.at[pl.ds(0, 96), :], send_sem.at[KX])
    drain(s_in.at[pl.ds(0, NZ - 1)], send_sem.at[SZ])
    drain(l_in.at[pl.ds(0, 480), :], send_sem.at[LZ])
    for dx in (1, 2, 3):

        @pl.when(mx + dx < NX)
        def _():
            drain(sx_in.at[0], send_sem.at[CX + dx - 1])
            drain(t_in.at[0], send_sem.at[TX + dx - 1])

    drain(cum_in.at[pl.ds(0, 6)], send_sem.at[CZ])
    drain(h_in.at[pl.ds(0, 96), :], send_sem.at[HZ])


def local(
    x_in, gate_in, conv_weight, conv_bias, proj_low, proj_bc, dt_weight, dt_bias, decay_log, skip_gain, attn_kv,
    kept_index, kept_owner,
):
    V = pltpu.VMEM
    hbm = pl.BlockSpec(memory_space=pltpu.HBM)
    return pl.pallas_call(
        kernel,
        out_shape=(pltpu.VMEM((TOK, CH), BF16), pltpu.VMEM((1, TOK, 2 * LANES), BF16)),
        in_specs=[hbm] * 13,
        out_specs=(pl.BlockSpec(memory_space=pltpu.VMEM),) * 2,
        scratch_shapes=[
            V((TOK, CH), BF16), V((TOK, CH), BF16), V((CONV, CH), F32), V((1, CH), F32), V((CH, RANK), BF16),
            V((LANES, CH), BF16), V((RANK, CH), BF16), V((1, CH), F32), V((ST, CH), F32), V((1, CH), F32),
            V((TOK, 2 * LANES), BF16), V((1, KEEP), jnp.int32), V((1, KEEP), jnp.int32), V((ST, 2 * LANES), F32),
            V((32, LANES), BF16), V((32, LANES), BF16), V((32, LANES), F32), V((TOK + 16, CH), F32), V((TOK, CH), BF16),
            V((TOK, RANK + LANES), BF16), V((TOK, RANK + LANES), BF16), V((TOK, RANK + LANES), BF16), V((16, RANK + LANES), BF16), V((TOK, RANK + LANES), BF16),
            V((TOK * TILES, LANES), F32), V((TOK * TILES, LANES), F32), V((TOK // 8, 8, 2 * ST * LANES), F32),
            V((ST * TILES, LANES), F32), V((ST * TILES, LANES), F32), V((ST * TILES, LANES), F32),
            V((TOK * ST * TILES, LANES), F32), V((TOK * TILES, LANES), F32), V((TOK * TILES, LANES), F32), V((TILES, LANES), F32),
            V((TILES, 1, LANES), F32), V((NZ, 2, 1, LANES), F32), V((ST * TILES, LANES), BF16), V((NZ * 32, LANES), BF16),
            V((2, 1, LANES), F32), V((NX - 1, TILES, 1, LANES), F32), V((NZ, 2, 1, LANES), F32), V((TILES, 1, LANES), F32),
            V((32, LANES), BF16), V((NX - 1, 128, LANES), BF16), V((NZ * 32, LANES), BF16), V((128, LANES), BF16),
            V((128, LANES), F32), V((NZ * 32, LANES), F32), V((128, LANES), F32), V(((NX - 1) * 128, LANES), F32),
            V((128, LANES), F32),
            V((256, LANES), BF16), V((256, LANES), BF16), V((TOK, 2 * LANES), BF16),
            pltpu.SemaphoreType.DMA((15,)),
            pltpu.SemaphoreType.DMA((16,)), pltpu.SemaphoreType.DMA((16,)),
            pltpu.SemaphoreType.REGULAR((4,)),
        ],
        compiler_params=pltpu.CompilerParams(
            collective_id=0, has_side_effects=True, vmem_limit_bytes=62_000_000
        ),
    )(
        x_in, gate_in, conv_weight, conv_bias.reshape(1, CH), proj_low, proj_bc.T, dt_weight, dt_bias.reshape(1, CH),
        decay_log, skip_gain.reshape(1, CH), attn_kv, kept_index, kept_owner.reshape(1, KEEP),
    )


def solution(mesh):
    return jax.shard_map(
        local,
        mesh=mesh,
        in_specs=(
            P("ctx", "ch"), P("ctx", "ch"), P(None, "ch"), P("ch"), P("ch", None), P("ch", None), P(None, "ch"),
            P("ch"), P(None, "ch"), P("ch"), P("ctx", "ch"), P("ch", "ctx"), P("ch", "ctx", None),
        ),
        out_specs=(P("ctx", "ch"), P("ch", "ctx", None)),
        check_vma=False,
    )
```

```python
import functools
import math

import jax
import jax.numpy as jnp
from jax import lax
from jax.experimental import pallas as pl
from jax.experimental.pallas import tpu as pltpu
from jax.sharding import PartitionSpec as P

MOST = 2
NZ = 16
NX = 4
NC = 8
TOK = 128
CH = 1024
ST = 16
CONV = 4
RANK = 256
LANES = 128
TILES = CH // LANES
KEEP = 32
F32 = jnp.float32
BF16 = jnp.bfloat16
LOG2E = math.log2(math.e)


def dot(a, b):
    return jnp.dot(a, b, preferred_element_type=F32)


def dot_rows(a, b):
    return lax.dot_general(a, b, (((0,), (0,)), ((), ())), preferred_element_type=F32)


def silu(v):
    return v / (1.0 + jnp.exp(-v))


def iota(shape, dim):
    return lax.broadcasted_iota(jnp.int32, shape, dim)


def kernel(
    x_hbm, gate_hbm, cw_hbm, cb_hbm, low_hbm, bc_hbm, dtw_hbm, dtb_hbm, dec_hbm, skip_hbm, kv_hbm, idx_hbm, own_hbm,
    gated_out, kept_out,
    x_v, gate_v, cw_v, cb_v, low_v, bc_v, dtw_v, dtb_v, dec_v, skip_v, kv_v, idx_v, own_v, decs_v,
    halo, halo_out, halo_f, xs, act, part, rs_in, r0_in, ag_out, lr, dtb3, xb3, bcx, a2b, a2n, lb, gb, yb, sgb, skip_b,
    s_out, s_in, l_out, l_in, sx_out, sx_in, cum_out, cum_in, t_out, t_in, before, h_in, hf, decay, reach,
    plane, carry_x,
    kz_out, kz_in, kx_out,
    in_sem, send_sem, recv_sem, here_sem,
):
    kx_in = kept_out.at[0]
    me = lax.axis_index("ctx")
    mc = lax.axis_index("ch")
    mx = me // NZ
    mz = me % NZ
    mq = mz % 4

    loads = [
        (x_hbm, x_v), (cw_hbm, cw_v), (cb_hbm, cb_v), (idx_hbm, idx_v), (own_hbm, own_v), (kv_hbm, kv_v),
        (low_hbm, low_v), (bc_hbm, bc_v.at[pl.ds(0, 2 * ST), :]), (bc_hbm, bc_v.at[pl.ds(2 * ST, 2 * ST), :]),
        (dec_hbm, dec_v),
        (dec_hbm.at[:, pl.ds(pl.multiple_of(mq * 2 * LANES, 2 * LANES), 2 * LANES)], decs_v),
        (dtw_hbm, dtw_v), (dtb_hbm, dtb_v), (skip_hbm, skip_v), (gate_hbm, gate_v),
    ]
    loads = [pltpu.make_async_copy(s, d, in_sem.at[i]) for i, (s, d) in enumerate(loads)]
    (x_ld, cw_ld, cb_ld, idx_ld, own_ld, kv_ld, low_ld, bc_ld, bc2_ld, dec_ld, decs_ld, dtw_ld, dtb_ld, skip_ld, gate_ld) = loads

    for c in loads[:3]:
        c.start()

    def along_z(d):
        return {"ctx": mx * NZ + (mz + d + NZ) % NZ}

    def along_x(d):
        return {"ctx": ((mx + d) % NX) * NZ + mz}

    def along_xz(dx, dz):
        return {"ctx": ((mx + dx) % NX) * NZ + (mz + dz + NZ) % NZ}

    def along_ch(dy, dc):
        return {"ch": ((mc // 2 + dy) % (NC // 2)) * 2 + (mc + dc) % 2}

    far_z = (8, 7, 9, 6, 10, 5, 11, 4, 12, 3, 13, 2, 14, 1, 15)
    far_x = (2, 1, 3)
    far_ch = ((2, 0), (2, 1), (1, 0), (3, 0), (1, 1), (3, 1), (0, 1))
    right = {"ctx": (me + 1) % (NX * NZ)}
    left = {"ctx": (me + NX * NZ - 1) % (NX * NZ)}
    barrier = pltpu.get_barrier_semaphore()
    for d in far_ch:
        pl.semaphore_signal(barrier, inc=1, device_id=along_ch(*d))
    for d in (-1, 1):
        pl.semaphore_signal(barrier, inc=1, device_id=along_z(d))
    for d in far_x:
        pl.semaphore_signal(barrier, inc=1, device_id=along_x(d))

    @pl.when(mz == NZ - 1)
    def _():
        pl.semaphore_signal(barrier, inc=1, device_id=right)

    @pl.when(mz == 0)
    def _():
        pl.semaphore_signal(barrier, inc=1, device_id=left)

    for c in loads[3:]:
        c.start()

    def tell(i):
        for d in (-(1 << i), 1 << i):
            pl.semaphore_signal(here_sem.at[i], inc=1, device_id=along_z(d))

    def hear(i):
        pl.semaphore_wait(here_sem.at[i], 2)

    def tell_x():
        for d in far_x:
            pl.semaphore_signal(here_sem.at[3], inc=1, device_id=along_x(d))

    def hear_x():
        pl.semaphore_wait(here_sem.at[3], NX - 1)

    def remote(src, dst, k, peer):
        return pltpu.make_async_remote_copy(
            src_ref=src, dst_ref=dst, send_sem=send_sem.at[k], recv_sem=recv_sem.at[k], device_id=peer
        )

    def drain(ref, sem):
        pltpu.make_async_copy(ref, ref, sem).wait()

    HALO, RS, AG, KZ, KX, SZ, R0, CZ, LZ, HZ, CX, TX = (0, 1, 2, 3, 4, 5, 6, 7, 8, 10, 12, 15)

    bc_v[pl.ds(4 * ST, LANES - 4 * ST), :] = jnp.zeros((LANES - 4 * ST, CH), BF16)

    x_ld.wait()
    for j in range(TILES):
        halo_f[pl.ds(4 * j, 4), :] = x_v[pl.ds(TOK - 16, 16), pl.ds(j * LANES, LANES)].astype(F32)[12:, :]
    halo_out[...] = halo_f[...].astype(BF16)
    pl.semaphore_wait(barrier, NC - 1 + NX - 1 + 2 + jnp.where((mz == 0) | (mz == NZ - 1), 1, 0))

    remote(halo_out, halo, HALO, right).start()
    tell(0)

    def conv(first, rows):
        for j in range(TILES):
            cols = pl.ds(j * LANES, LANES)
            s = jnp.broadcast_to(cb_v[:, cols], (rows, LANES))
            for k in range(CONV):
                s = s + cw_v[pl.ds(k, 1), cols] * xs[pl.ds(first + 16 - (CONV - 1) + k, rows), cols]
            a = silu(s).astype(BF16)
            act[pl.ds(first, rows), cols] = a
            xb3[pl.ds(first * TILES + j, rows, stride=TILES), :] = a.astype(F32)

    def project(first, rows):
        a = act[pl.ds(first, rows), :]
        part[pl.ds(first, rows), pl.ds(0, RANK)] = dot(a, low_v[...]).astype(BF16)
        wide = lax.dot_general(a, bc_v[...], (((1,), (1,)), ((), ())), preferred_element_type=F32)
        high = wide.astype(BF16).astype(F32)
        low = jnp.where(iota((rows, LANES), 1) < 2 * ST, high, wide - high)
        part[pl.ds(first, rows), pl.ds(RANK, LANES)] = low.astype(BF16)

    def summed(ref):
        total = ref[pl.ds(0, 16), :].astype(F32)
        for i in range(1, NC):
            total = total + ref[pl.ds(16 * i, 16), :].astype(F32)
        wide = total[:, RANK:]
        return total[:, :RANK].astype(BF16), (wide + pltpu.roll(wide, LANES - 2 * ST, 1)).astype(BF16)

    def rows_of(i):
        return pl.ds(pl.multiple_of(i * 16, 16), 16)

    cw_ld.wait()
    cb_ld.wait()
    xs[pl.ds(16, TOK), :] = x_v[...].astype(F32)
    conv(16, TOK - 16)
    low_ld.wait()
    bc_ld.wait()
    bc2_ld.wait()
    project(16, TOK - 16)

    for d in far_ch:
        to = along_ch(*d)

        @pl.when(to["ch"] > 0)
        def _():
            remote(part.at[rows_of(to["ch"]), :], rs_in.at[rows_of(mc), :], RS, to).start()

    hear(0)
    tell(1)
    tell_x()
    drain(halo, recv_sem.at[HALO])
    halo_f[...] = halo[...].astype(F32)
    for j in range(TILES):
        xs[pl.ds(12, 4), pl.ds(j * LANES, LANES)] = jnp.where(me > 0, halo_f[pl.ds(4 * j, 4), :], 0.0)
    conv(0, 16)
    project(0, 16)
    for d in far_ch:
        remote(part.at[pl.ds(0, 16), :], r0_in.at[rows_of(mc), :], R0, along_ch(*d)).start()
    r0_in[rows_of(mc), :] = part[pl.ds(0, 16), :]

    idx_ld.wait()
    own_ld.wait()
    kv_ld.wait()
    own_row = own_v[...]
    eye = iota((KEEP, KEEP), 0) == iota((KEEP, KEEP), 1)
    own = jnp.sum(jnp.where(eye, own_row, 0), axis=1, keepdims=True)
    same = (own_row == own) & (iota((KEEP, KEEP), 1) < iota((KEEP, KEEP), 0))
    rank = jnp.sum(jnp.where(same, 1, 0), axis=1, keepdims=True)
    place = (own & (NZ - 1)) * 16 + (own >> 4) * 2 + rank
    src_t = (iota((TOK, KEEP), 0) == idx_v[...] - me * TOK).astype(F32).astype(BF16)
    picked = dot_rows(src_t, kv_v[...]).astype(BF16)
    slots = iota((KEEP, 256), 1)
    kz = dot_rows((slots == place).astype(F32).astype(BF16), picked[:, :LANES])
    kz = kz + dot_rows((slots == place + 8).astype(F32).astype(BF16), picked[:, LANES:])
    kz_out[...] = kz.astype(BF16)

    hear(1)
    tell(2)

    dec_ld.wait()
    decs_ld.wait()
    gate_ld.wait()
    for j in range(TILES):
        rate = -LOG2E * jnp.exp(dec_v[:, pl.ds(j * LANES, LANES)])
        for half in range(2):
            a2n[pl.ds(half * 64 + j * 8, 8), :] = rate[half * 8 : half * 8 + 8, :]
        a2b[pl.ds(j, ST, stride=TILES), :] = rate
    a2s = [
        [-LOG2E * jnp.exp(decs_v[pl.ds(half * 8, 8), pl.ds(jj * LANES, LANES)]) for jj in range(2)] for half in range(2)
    ]
    skip_ld.wait()
    for j in range(TILES):
        cols = pl.ds(j * LANES, LANES)
        sgb[pl.ds(j, TOK, stride=TILES), :] = silu(gate_v[:, cols].astype(F32))
        skip_b[pl.ds(j, 1), :] = skip_v[:, cols]

    @pl.when(mc > 0)
    def _():
        rs_in[rows_of(mc), :] = part[rows_of(mc), :]
        drain(rs_in.at[pl.ds(0, TOK - 16), :], recv_sem.at[RS])
        low, coeff = summed(rs_in)
        ag_out[:, pl.ds(0, RANK)] = low
        ag_out[:, pl.ds(RANK, LANES)] = coeff
        for d in far_ch:
            remote(ag_out, lr.at[rows_of(mc), :], AG, along_ch(*d)).start()
        lr[rows_of(mc), :] = ag_out[...]

    hear(2)
    hear_x()
    for d in far_z:
        to = (mz + d) % NZ
        remote(kz_out.at[rows_of(to), :], kz_in.at[rows_of(mz), :], KZ, along_z(d)).start()
    kz_in[rows_of(mz), :] = kz_out[rows_of(mz), :]

    dtw_ld.wait()
    dtb_ld.wait()
    drain(r0_in.at[pl.ds(0, TOK - 16), :], recv_sem.at[R0])
    low, coeff = summed(r0_in)
    lr[pl.ds(0, 16), pl.ds(0, RANK)] = low
    lr[pl.ds(0, 16), pl.ds(RANK, LANES)] = coeff

    @pl.when(mc > 0)
    def _():
        drain(lr.at[pl.ds(0, TOK - 32), :], recv_sem.at[AG])

    @pl.when(mc == 0)
    def _():
        drain(lr.at[pl.ds(0, TOK - 16), :], recv_sem.at[AG])

    for j in range(TILES):
        cols = pl.ds(j * LANES, LANES)
        v = dot(lr[:, pl.ds(0, RANK)], dtw_v[:, cols]) + dtb_v[:, cols]
        v = jnp.maximum(v, 0.0) + jnp.log1p(jnp.exp(-jnp.abs(v)))
        dtb3[pl.ds(j, TOK, stride=TILES), :] = v
        s_out[j] = jnp.sum(v, axis=0, keepdims=True)
    coeff = lr[:, pl.ds(RANK, LANES)]

    def spread(i):
        rows = (iota((LANES, 4 * LANES), 1) >> 7) + 4 * i == iota((LANES, 4 * LANES), 0)
        wide = dot(coeff, rows.astype(F32).astype(BF16))
        bcx[:, :, pl.ds(i * 4 * LANES, 4 * LANES)] = wide.reshape(TOK // 8, 8, 4 * LANES)

    for i in range(4):
        spread(i)

    def token(g, u):
        return pl.ds(pl.multiple_of(g * 64, 64) + u * 8, 8)

    for d in far_z:
        to = (mz + d) % 4
        remote(s_out.at[pl.ds(2 * to, 2)], s_in.at[mz], SZ, along_z(d)).start()
    s_in[mz] = s_out[pl.ds(2 * mq, 2)]

    def quarter_of(i):
        return pl.ds(pl.multiple_of(i * 16, 16), 16)

    def block_of(i):
        return pl.ds(pl.multiple_of(i * 32, 32), 32)

    empty = tuple(jnp.zeros((TILES, LANES), F32) for _ in range(ST))

    def half_block(half, i):
        return pl.ds(half * 64 + pl.multiple_of(i * 16, 16), 16)

    for half in range(2):

        def end_step(g, state):
            state = list(state)
            for u in range(8):
                dt = dtb3[token(g, u), :]
                dx = dt * xb3[token(g, u), :]
                for i in range(8):
                    n = half * 8 + i
                    b = bcx[g, pl.ds(u, 1), pl.ds(n * LANES, LANES)]
                    state[i] = jnp.exp2(dt * a2b[pl.ds(n * 8, 8), :]) * state[i] + dx * b
            return tuple(state)

        state = lax.fori_loop(0, TOK // 8, end_step, tuple(jnp.zeros((TILES, LANES), F32) for _ in range(8)))
        for i in range(8):
            lb[pl.ds(half * 64 + i * 8, 8), :] = state[i]
        for j in range(0, TILES, 2):
            two = [lb[pl.ds(half * 64 + j + i, 8, stride=TILES), :] for i in range(2)]
            l_out[pl.ds(half * 64 + j * 8, 16), :] = jnp.concatenate(two, axis=0).astype(BF16)
        for d in far_z:
            to = (mz + d) % 4
            remote(l_out.at[half_block(half, to), :], l_in.at[half, quarter_of(mz), :], LZ + half, along_z(d)).start()
        l_in[half, quarter_of(mz), :] = l_out[half_block(half, mq), :]

    for i in range(4, 8):
        spread(i)

    def scan_step(g, state):
        state = list(state)
        for u in range(8):
            dt = dtb3[token(g, u), :]
            xt = xb3[token(g, u), :]
            dx = dt * xt
            y = [skip_b[...] * xt, None, None, None]
            for n in range(ST):
                b = bcx[g, pl.ds(u, 1), pl.ds(n * LANES, LANES)]
                c = bcx[g, pl.ds(u, 1), pl.ds((ST + n) * LANES, LANES)]
                state[n] = jnp.exp2(dt * a2b[pl.ds(n * 8, 8), :]) * state[n] + dx * b
                term = c * state[n]
                y[n % 4] = term if y[n % 4] is None else y[n % 4] + term
            yb[token(g, u), :] = ((y[0] + y[1]) + (y[2] + y[3])) * sgb[token(g, u), :]
        return tuple(state)

    lax.fori_loop(0, TOK // 8, scan_step, empty)

    def reach_step(g, cum):
        for u in range(8):
            cum = cum + dtb3[token(g, u), :]
            sgt = sgb[token(g, u), :]
            for n in range(ST):
                c = bcx[g, pl.ds(u, 1), pl.ds((ST + n) * LANES, LANES)]
                gb[pl.ds(pl.multiple_of(g * 1024, 1024) + u * 128 + n * 8, 8), :] = (c * sgt) * jnp.exp2(cum * a2b[pl.ds(n * 8, 8), :])
        return cum

    lax.fori_loop(0, TOK // 8, reach_step, jnp.zeros((TILES, LANES), F32))

    drain(kz_in.at[pl.ds(0, 240), :], recv_sem.at[KZ])
    row = iota((TOK, 256), 0)
    want = ((row >> 1) & (NZ - 1)) * 16 + (row >> 5) * 2 + (row & 1)
    for half in range(2):
        sel = (iota((TOK, 256), 1) == want + half * 8).astype(F32).astype(BF16)
        kx_out[:, pl.ds(half * LANES, LANES)] = dot(sel, kz_in[...]).astype(BF16)

    for d in far_x:
        to = (mx + d) % NX
        remote(kx_out.at[block_of(to), :], kx_in.at[block_of(mx), :], KX, along_x(d)).start()
    kx_in[block_of(mx), :] = kx_out[block_of(mx), :]

    drain(s_in.at[pl.ds(0, NZ - 1)], recv_sem.at[SZ])
    for jj in range(2):
        run = jnp.zeros((1, LANES), F32)
        for z in range(NZ):
            for half in range(2):
                decay[half, pl.ds(z * 16 + jj * 8, 8), :] = jnp.exp2(a2s[half][jj] * s_in[z, jj])
            cum_out[z, jj] = run
            run = run + s_in[z, jj]
        sx_out[jj] = run

    def pair_of(i):
        return pl.ds(2 * i, 2)

    def to_planes(src, dst, k):
        for dx in (3, 2, 1):

            @pl.when(mx + dx < NX)
            def _():
                for dz in (-2, -1, 1, 0):
                    pltpu.make_async_remote_copy(
                        src_ref=src, dst_ref=dst, send_sem=send_sem.at[k + dx - 1], recv_sem=recv_sem.at[k + mx],
                        device_id=along_xz(dx, dz),
                    ).start()

    @pl.when(mx < NX - 1)
    def _():
        to_planes(sx_out, sx_in.at[mx, pair_of(mq)], CX)

    for dz in (-2, -1, 1):
        remote(cum_out.at[(mz + dz + NZ) % NZ], cum_in.at[pair_of(mq)], CZ, along_z(dz)).start()
    cum_in[pair_of(mq)] = cum_out[mz]

    for half in range(2):
        drain(l_in.at[half, pl.ds(0, 240), :], recv_sem.at[LZ + half])
        carry = jnp.zeros((16, LANES), F32)
        for z in range(NZ):
            rows = pl.ds(z * 16, 16)
            before[half, rows, :] = carry.astype(BF16)
            carry = decay[half, rows, :] * carry + l_in[half, rows, :].astype(F32)
        t_out[half] = carry.astype(BF16)

        @pl.when(mx < NX - 1)
        def _():
            to_planes(t_out.at[half], t_in.at[half, mx, quarter_of(mq)], TX + 3 * half)

        for dz in (-2, -1, 1):
            to = (mz + dz + NZ) % NZ
            remote(before.at[half, quarter_of(to), :], h_in.at[half, quarter_of(mq), :], HZ + half, along_z(dz)).start()
        h_in[half, quarter_of(mq), :] = before[half, quarter_of(mz), :]

    carry_x[...] = jnp.zeros_like(carry_x)
    for i in range(NX - 1):

        @pl.when(i < mx)
        def _():
            drain(sx_in.at[i], recv_sem.at[CX + i])
            for j in range(TILES):
                for half in range(2):
                    rows = pl.ds(half * 64 + j * 8, 8)
                    plane[i, rows, :] = jnp.exp2(a2n[rows, :] * sx_in[i, j])

    drain(cum_in.at[pl.ds(0, 6)], recv_sem.at[CZ])
    for j in range(TILES):
        for half in range(2):
            rows = pl.ds(half * 64 + j * 8, 8)
            reach[rows, :] = jnp.exp2(a2n[rows, :] * cum_in[j])
    for half in range(2):
        rows = pl.ds(half * 64, 64)
        for i in range(NX - 1):

            @pl.when(i < mx)
            def _():
                drain(t_in.at[half, i], recv_sem.at[TX + 3 * half + i])
                carry_x[rows, :] = plane[i, rows, :] * carry_x[rows, :] + t_in[half, i].astype(F32)

        drain(h_in.at[half, pl.ds(0, 48), :], recv_sem.at[HZ + half])
        hf[rows, :] = h_in[half].astype(F32) + reach[rows, :] * carry_x[rows, :]

    carried = [hf[pl.ds((n // 8) * 64 + n % 8, TILES, stride=8), :] for n in range(ST)]

    def add_step(g, _):
        for u in range(8):
            at = token(g, u)
            y = [yb[at, :], None, None, None]
            for n in range(ST):
                term = gb[pl.ds(pl.multiple_of(g * 1024, 1024) + u * 128 + n * 8, 8), :] * carried[n]
                y[n % 4] = term if y[n % 4] is None else y[n % 4] + term
            yb[at, :] = (y[0] + y[1]) + (y[2] + y[3])
        return 0

    lax.fori_loop(0, TOK // 8, add_step, 0)

    for j in range(TILES):
        cols = pl.ds(j * LANES, LANES)
        gated_out[:, cols] = yb[pl.ds(j, TOK, stride=TILES), :].astype(BF16)
    drain(kx_in.at[pl.ds(0, 96), :], recv_sem.at[KX])

    drain(halo, send_sem.at[HALO])
    drain(r0_in.at[pl.ds(0, TOK - 16), :], send_sem.at[R0])

    @pl.when(mc > 0)
    def _():
        drain(rs_in.at[pl.ds(0, TOK - 32), :], send_sem.at[RS])
        drain(lr.at[pl.ds(0, TOK - 16), :], send_sem.at[AG])

    @pl.when(mc == 0)
    def _():
        drain(rs_in.at[pl.ds(0, TOK - 16), :], send_sem.at[RS])

    drain(kz_in.at[pl.ds(0, 240), :], send_sem.at[KZ])
    drain(kx_in.at[pl.ds(0, 96), :], send_sem.at[KX])
    drain(s_in.at[pl.ds(0, NZ - 1)], send_sem.at[SZ])
    for half in range(2):
        drain(l_in.at[half, pl.ds(0, 240), :], send_sem.at[LZ + half])
        drain(h_in.at[half, pl.ds(0, 48), :], send_sem.at[HZ + half])
    for dx in (1, 2, 3):

        @pl.when(mx + dx < NX)
        def _():
            drain(sx_in.at[0], send_sem.at[CX + dx - 1])
            for half in range(2):
                drain(t_in.at[half, 0], send_sem.at[TX + 3 * half + dx - 1])

    drain(cum_in.at[pl.ds(0, 6)], send_sem.at[CZ])


def local(
    x_in, gate_in, conv_weight, conv_bias, proj_low, proj_bc, dt_weight, dt_bias, decay_log, skip_gain, attn_kv,
    kept_index, kept_owner,
):
    V = pltpu.VMEM
    hbm = pl.BlockSpec(memory_space=pltpu.HBM)
    return pl.pallas_call(
        kernel,
        out_shape=(pltpu.VMEM((TOK, CH), BF16), pltpu.VMEM((1, TOK, 2 * LANES), BF16)),
        in_specs=[hbm] * 13,
        out_specs=(pl.BlockSpec(memory_space=pltpu.VMEM),) * 2,
        scratch_shapes=[
            V((TOK, CH), BF16), V((TOK, CH), BF16), V((CONV, CH), F32), V((1, CH), F32), V((CH, RANK), BF16),
            V((LANES, CH), BF16), V((RANK, CH), BF16), V((1, CH), F32), V((ST, CH), F32), V((1, CH), F32),
            V((TOK, 2 * LANES), BF16), V((1, KEEP), jnp.int32), V((1, KEEP), jnp.int32), V((ST, 2 * LANES), F32),
            V((32, LANES), BF16), V((32, LANES), BF16), V((32, LANES), F32), V((TOK + 16, CH), F32), V((TOK, CH), BF16),
            V((TOK, RANK + LANES), BF16), V((TOK, RANK + LANES), BF16), V((TOK, RANK + LANES), BF16), V((16, RANK + LANES), BF16), V((TOK, RANK + LANES), BF16),
            V((TOK * TILES, LANES), F32), V((TOK * TILES, LANES), F32), V((TOK // 8, 8, 2 * ST * LANES), F32),
            V((ST * TILES, LANES), F32), V((ST * TILES, LANES), F32), V((ST * TILES, LANES), F32),
            V((TOK * ST * TILES, LANES), F32), V((TOK * TILES, LANES), F32), V((TOK * TILES, LANES), F32), V((TILES, LANES), F32),
            V((TILES, 1, LANES), F32), V((NZ, 2, 1, LANES), F32), V((128, LANES), BF16), V((2, NZ * 16, LANES), BF16),
            V((2, 1, LANES), F32), V((NX - 1, TILES, 1, LANES), F32), V((NZ, 2, 1, LANES), F32), V((TILES, 1, LANES), F32),
            V((2, 16, LANES), BF16), V((2, NX - 1, 64, LANES), BF16), V((2, NZ * 16, LANES), BF16), V((2, 64, LANES), BF16),
            V((128, LANES), F32), V((2, NZ * 16, LANES), F32), V((128, LANES), F32), V((NX - 1, 128, LANES), F32),
            V((128, LANES), F32),
            V((256, LANES), BF16), V((256, LANES), BF16), V((TOK, 2 * LANES), BF16),
            pltpu.SemaphoreType.DMA((15,)),
            pltpu.SemaphoreType.DMA((21,)), pltpu.SemaphoreType.DMA((21,)),
            pltpu.SemaphoreType.REGULAR((4,)),
        ],
        compiler_params=pltpu.CompilerParams(
            collective_id=0, has_side_effects=True, vmem_limit_bytes=62_000_000
        ),
    )(
        x_in, gate_in, conv_weight, conv_bias.reshape(1, CH), proj_low, proj_bc.T, dt_weight, dt_bias.reshape(1, CH),
        decay_log, skip_gain.reshape(1, CH), attn_kv, kept_index, kept_owner.reshape(1, KEEP),
    )


def solution(mesh):
    return jax.shard_map(
        local,
        mesh=mesh,
        in_specs=(
            P("ctx", "ch"), P("ctx", "ch"), P(None, "ch"), P("ch"), P("ch", None), P("ch", None), P(None, "ch"),
            P("ch"), P(None, "ch"), P("ch"), P("ctx", "ch"), P("ch", "ctx"), P("ch", "ctx", None),
        ),
        out_specs=(P("ctx", "ch"), P("ch", "ctx", None)),
        check_vma=False,
    )
```

```python
import functools
import math

import jax
import jax.numpy as jnp
from jax import lax
from jax.experimental import pallas as pl
from jax.experimental.pallas import tpu as pltpu
from jax.sharding import PartitionSpec as P

MOST = 2
PARTS = 4
NZ = 16
NX = 4
NC = 8
TOK = 128
CH = 1024
ST = 16
CONV = 4
RANK = 256
LANES = 128
TILES = CH // LANES
KEEP = 32
F32 = jnp.float32
BF16 = jnp.bfloat16
LOG2E = math.log2(math.e)


def dot(a, b):
    return jnp.dot(a, b, preferred_element_type=F32)


def dot_rows(a, b):
    return lax.dot_general(a, b, (((0,), (0,)), ((), ())), preferred_element_type=F32)


def silu(v):
    return v / (1.0 + jnp.exp(-v))


def iota(shape, dim):
    return lax.broadcasted_iota(jnp.int32, shape, dim)


def kernel(
    x_hbm, gate_hbm, cw_hbm, cb_hbm, low_hbm, bc_hbm, dtw_hbm, dtb_hbm, dec_hbm, skip_hbm, kv_hbm, idx_hbm, own_hbm,
    gb, yb, hf, kept_out,
    x_v, gate_v, cw_v, cb_v, low_v, bc_v, dtw_v, dtb_v, dec_v, skip_v, kv_v, idx_v, own_v, decs_v,
    halo, halo_out, halo_f, xs, act, part, rs_in, r0_in, ag_out, lr, dtb3, xb3, bcx, a2b, a2n, lb, sgb, skip_b,
    s_out, s_in, l_out, l_in, sx_out, sx_in, cum_out, cum_in, t_out, t_in, before, h_in, decay, reach,
    plane, carry_x,
    kz_out, kz_in, kx_out,
    in_sem, send_sem, recv_sem, here_sem,
):
    kx_in = kept_out
    me = lax.axis_index("ctx")
    mc = lax.axis_index("ch")
    mx = me // NZ
    mz = me % NZ
    mq = mz % 4

    loads = [
        (x_hbm, x_v), (cw_hbm, cw_v), (cb_hbm, cb_v), (idx_hbm, idx_v), (own_hbm, own_v), (kv_hbm, kv_v),
        (low_hbm, low_v), (bc_hbm, bc_v.at[pl.ds(0, 2 * ST), :]), (bc_hbm, bc_v.at[pl.ds(2 * ST, 2 * ST), :]),
        (dec_hbm, dec_v),
        (dec_hbm.at[:, pl.ds(pl.multiple_of(mq * 2 * LANES, 2 * LANES), 2 * LANES)], decs_v),
        (dtw_hbm, dtw_v), (dtb_hbm, dtb_v), (skip_hbm, skip_v), (gate_hbm, gate_v),
    ]
    loads = [pltpu.make_async_copy(s, d, in_sem.at[i]) for i, (s, d) in enumerate(loads)]
    (x_ld, cw_ld, cb_ld, idx_ld, own_ld, kv_ld, low_ld, bc_ld, bc2_ld, dec_ld, decs_ld, dtw_ld, dtb_ld, skip_ld, gate_ld) = loads

    for c in loads[:3]:
        c.start()

    def along_z(d):
        return {"ctx": mx * NZ + (mz + d + NZ) % NZ}

    def along_x(d):
        return {"ctx": ((mx + d) % NX) * NZ + mz}

    def along_xz(dx, dz):
        return {"ctx": ((mx + dx) % NX) * NZ + (mz + dz + NZ) % NZ}

    def along_ch(dy, dc):
        return {"ch": ((mc // 2 + dy) % (NC // 2)) * 2 + (mc + dc) % 2}

    far_z = (8, 7, 9, 6, 10, 5, 11, 4, 12, 3, 13, 2, 14, 1, 15)
    far_x = (2, 1, 3)
    far_ch = ((2, 0), (2, 1), (1, 0), (3, 0), (1, 1), (3, 1), (0, 1))
    right = {"ctx": (me + 1) % (NX * NZ)}
    left = {"ctx": (me + NX * NZ - 1) % (NX * NZ)}
    barrier = pltpu.get_barrier_semaphore()
    for d in far_ch:
        pl.semaphore_signal(barrier, inc=1, device_id=along_ch(*d))
    for d in (-1, 1):
        pl.semaphore_signal(barrier, inc=1, device_id=along_z(d))
    for d in far_x:
        pl.semaphore_signal(barrier, inc=1, device_id=along_x(d))

    @pl.when(mz == NZ - 1)
    def _():
        pl.semaphore_signal(barrier, inc=1, device_id=right)

    @pl.when(mz == 0)
    def _():
        pl.semaphore_signal(barrier, inc=1, device_id=left)

    for c in loads[3:]:
        c.start()

    def tell(i):
        for d in (-(1 << i), 1 << i):
            pl.semaphore_signal(here_sem.at[i], inc=1, device_id=along_z(d))

    def hear(i):
        pl.semaphore_wait(here_sem.at[i], 2)

    def tell_x():
        for d in far_x:
            pl.semaphore_signal(here_sem.at[3], inc=1, device_id=along_x(d))

    def hear_x():
        pl.semaphore_wait(here_sem.at[3], NX - 1)

    def remote(src, dst, k, peer):
        return pltpu.make_async_remote_copy(
            src_ref=src, dst_ref=dst, send_sem=send_sem.at[k], recv_sem=recv_sem.at[k], device_id=peer
        )

    def drain(ref, sem):
        pltpu.make_async_copy(ref, ref, sem).wait()

    HALO, RS, AG, KZ, KX, SZ, R0, CZ, LZ, HZ, CX, TX = (0, 1, 2, 3, 4, 5, 6, 7, 8, 10, 12, 15)

    bc_v[pl.ds(4 * ST, LANES - 4 * ST), :] = jnp.zeros((LANES - 4 * ST, CH), BF16)

    x_ld.wait()
    for j in range(TILES):
        halo_f[pl.ds(4 * j, 4), :] = x_v[pl.ds(TOK - 16, 16), pl.ds(j * LANES, LANES)].astype(F32)[12:, :]
    halo_out[...] = halo_f[...].astype(BF16)
    pl.semaphore_wait(barrier, NC - 1 + NX - 1 + 2 + jnp.where((mz == 0) | (mz == NZ - 1), 1, 0))

    remote(halo_out, halo, HALO, right).start()
    tell(0)

    def conv(first, rows):
        for j in range(TILES):
            cols = pl.ds(j * LANES, LANES)
            s = jnp.broadcast_to(cb_v[:, cols], (rows, LANES))
            for k in range(CONV):
                s = s + cw_v[pl.ds(k, 1), cols] * xs[pl.ds(first + 16 - (CONV - 1) + k, rows), cols]
            a = silu(s).astype(BF16)
            act[pl.ds(first, rows), cols] = a
            xb3[pl.ds(first * TILES + j, rows, stride=TILES), :] = a.astype(F32)

    def project(first, rows):
        a = act[pl.ds(first, rows), :]
        part[pl.ds(first, rows), pl.ds(0, RANK)] = dot(a, low_v[...]).astype(BF16)
        wide = lax.dot_general(a, bc_v[...], (((1,), (1,)), ((), ())), preferred_element_type=F32)
        high = wide.astype(BF16).astype(F32)
        low = jnp.where(iota((rows, LANES), 1) < 2 * ST, high, wide - high)
        part[pl.ds(first, rows), pl.ds(RANK, LANES)] = low.astype(BF16)

    def summed(ref):
        total = ref[pl.ds(0, 16), :].astype(F32)
        for i in range(1, NC):
            total = total + ref[pl.ds(16 * i, 16), :].astype(F32)
        wide = total[:, RANK:]
        return total[:, :RANK].astype(BF16), (wide + pltpu.roll(wide, LANES - 2 * ST, 1)).astype(BF16)

    def rows_of(i):
        return pl.ds(pl.multiple_of(i * 16, 16), 16)

    cw_ld.wait()
    cb_ld.wait()
    xs[pl.ds(16, TOK), :] = x_v[...].astype(F32)
    conv(16, TOK - 16)
    low_ld.wait()
    bc_ld.wait()
    bc2_ld.wait()
    project(16, TOK - 16)

    for d in far_ch:
        to = along_ch(*d)

        @pl.when(to["ch"] > 0)
        def _():
            remote(part.at[rows_of(to["ch"]), :], rs_in.at[rows_of(mc), :], RS, to).start()

    hear(0)
    tell(1)
    tell_x()
    drain(halo, recv_sem.at[HALO])
    halo_f[...] = halo[...].astype(F32)
    for j in range(TILES):
        xs[pl.ds(12, 4), pl.ds(j * LANES, LANES)] = jnp.where(me > 0, halo_f[pl.ds(4 * j, 4), :], 0.0)
    conv(0, 16)
    project(0, 16)
    for d in far_ch:
        remote(part.at[pl.ds(0, 16), :], r0_in.at[rows_of(mc), :], R0, along_ch(*d)).start()
    r0_in[rows_of(mc), :] = part[pl.ds(0, 16), :]

    idx_ld.wait()
    own_ld.wait()
    kv_ld.wait()
    own_row = own_v[...]
    eye = iota((KEEP, KEEP), 0) == iota((KEEP, KEEP), 1)
    own = jnp.sum(jnp.where(eye, own_row, 0), axis=1, keepdims=True)
    same = (own_row == own) & (iota((KEEP, KEEP), 1) < iota((KEEP, KEEP), 0))
    rank = jnp.sum(jnp.where(same, 1, 0), axis=1, keepdims=True)
    place = (own & (NZ - 1)) * 16 + (own >> 4) * 2 + rank
    src_t = (iota((TOK, KEEP), 0) == idx_v[...] - me * TOK).astype(F32).astype(BF16)
    picked = dot_rows(src_t, kv_v[...]).astype(BF16)
    slots = iota((KEEP, 256), 1)
    kz = dot_rows((slots == place).astype(F32).astype(BF16), picked[:, :LANES])
    kz = kz + dot_rows((slots == place + 8).astype(F32).astype(BF16), picked[:, LANES:])
    kz_out[...] = kz.astype(BF16)

    hear(1)
    tell(2)

    dec_ld.wait()
    decs_ld.wait()
    gate_ld.wait()
    for j in range(TILES):
        rate = -LOG2E * jnp.exp(dec_v[:, pl.ds(j * LANES, LANES)])
        for half in range(2):
            a2n[pl.ds(half * 64 + j * 8, 8), :] = rate[half * 8 : half * 8 + 8, :]
        a2b[pl.ds(j, ST, stride=TILES), :] = rate
    a2s = [
        [-LOG2E * jnp.exp(decs_v[pl.ds(half * 8, 8), pl.ds(jj * LANES, LANES)]) for jj in range(2)] for half in range(2)
    ]
    skip_ld.wait()
    for j in range(TILES):
        cols = pl.ds(j * LANES, LANES)
        sgb[pl.ds(j, TOK, stride=TILES), :] = silu(gate_v[:, cols].astype(F32))
        skip_b[pl.ds(j, 1), :] = skip_v[:, cols]

    @pl.when(mc > 0)
    def _():
        rs_in[rows_of(mc), :] = part[rows_of(mc), :]
        drain(rs_in.at[pl.ds(0, TOK - 16), :], recv_sem.at[RS])
        low, coeff = summed(rs_in)
        ag_out[:, pl.ds(0, RANK)] = low
        ag_out[:, pl.ds(RANK, LANES)] = coeff
        for d in far_ch:
            remote(ag_out, lr.at[rows_of(mc), :], AG, along_ch(*d)).start()
        lr[rows_of(mc), :] = ag_out[...]

    hear(2)
    hear_x()
    for d in far_z:
        to = (mz + d) % NZ
        remote(kz_out.at[rows_of(to), :], kz_in.at[rows_of(mz), :], KZ, along_z(d)).start()
    kz_in[rows_of(mz), :] = kz_out[rows_of(mz), :]

    dtw_ld.wait()
    dtb_ld.wait()
    drain(r0_in.at[pl.ds(0, TOK - 16), :], recv_sem.at[R0])
    low, coeff = summed(r0_in)
    lr[pl.ds(0, 16), pl.ds(0, RANK)] = low
    lr[pl.ds(0, 16), pl.ds(RANK, LANES)] = coeff

    @pl.when(mc > 0)
    def _():
        drain(lr.at[pl.ds(0, TOK - 32), :], recv_sem.at[AG])

    @pl.when(mc == 0)
    def _():
        drain(lr.at[pl.ds(0, TOK - 16), :], recv_sem.at[AG])

    for j in range(TILES):
        cols = pl.ds(j * LANES, LANES)
        v = dot(lr[:, pl.ds(0, RANK)], dtw_v[:, cols]) + dtb_v[:, cols]
        v = jnp.maximum(v, 0.0) + jnp.log1p(jnp.exp(-jnp.abs(v)))
        dtb3[pl.ds(j, TOK, stride=TILES), :] = v
        s_out[j] = jnp.sum(v, axis=0, keepdims=True)
    coeff = lr[:, pl.ds(RANK, LANES)]

    def spread(i):
        rows = (iota((LANES, 4 * LANES), 1) >> 7) + 4 * i == iota((LANES, 4 * LANES), 0)
        wide = dot(coeff, rows.astype(F32).astype(BF16))
        bcx[:, :, pl.ds(i * 4 * LANES, 4 * LANES)] = wide.reshape(TOK // 8, 8, 4 * LANES)

    for i in range(4):
        spread(i)

    def token(g, u):
        return pl.ds(pl.multiple_of(g * 64, 64) + u * 8, 8)

    for d in far_z:
        to = (mz + d) % 4
        remote(s_out.at[pl.ds(2 * to, 2)], s_in.at[mz], SZ, along_z(d)).start()
    s_in[mz] = s_out[pl.ds(2 * mq, 2)]

    def quarter_of(i):
        return pl.ds(pl.multiple_of(i * 16, 16), 16)

    def block_of(i):
        return pl.ds(pl.multiple_of(i * 32, 32), 32)

    empty = tuple(jnp.zeros((TILES, LANES), F32) for _ in range(ST))

    def half_block(half, i):
        return pl.ds(half * 64 + pl.multiple_of(i * 16, 16), 16)

    for half in range(2):

        def end_step(g, state):
            state = list(state)
            for u in range(8):
                dt = dtb3[token(g, u), :]
                dx = dt * xb3[token(g, u), :]
                for i in range(8):
                    n = half * 8 + i
                    b = bcx[g, pl.ds(u, 1), pl.ds(n * LANES, LANES)]
                    state[i] = jnp.exp2(dt * a2b[pl.ds(n * 8, 8), :]) * state[i] + dx * b
            return tuple(state)

        state = lax.fori_loop(0, TOK // 8, end_step, tuple(jnp.zeros((TILES, LANES), F32) for _ in range(8)))
        for i in range(8):
            lb[pl.ds(half * 64 + i * 8, 8), :] = state[i]
        for j in range(0, TILES, 2):
            two = [lb[pl.ds(half * 64 + j + i, 8, stride=TILES), :] for i in range(2)]
            l_out[pl.ds(half * 64 + j * 8, 16), :] = jnp.concatenate(two, axis=0).astype(BF16)
        for d in far_z:
            to = (mz + d) % 4
            remote(l_out.at[half_block(half, to), :], l_in.at[half, quarter_of(mz), :], LZ + half, along_z(d)).start()
        l_in[half, quarter_of(mz), :] = l_out[half_block(half, mq), :]

    for i in range(4, 8):
        spread(i)

    def scan_step(g, state):
        state = list(state)
        for u in range(8):
            dt = dtb3[token(g, u), :]
            xt = xb3[token(g, u), :]
            dx = dt * xt
            y = [skip_b[...] * xt, None, None, None]
            for n in range(ST):
                b = bcx[g, pl.ds(u, 1), pl.ds(n * LANES, LANES)]
                c = bcx[g, pl.ds(u, 1), pl.ds((ST + n) * LANES, LANES)]
                state[n] = jnp.exp2(dt * a2b[pl.ds(n * 8, 8), :]) * state[n] + dx * b
                term = c * state[n]
                y[n % 4] = term if y[n % 4] is None else y[n % 4] + term
            yb[token(g, u), :] = ((y[0] + y[1]) + (y[2] + y[3])) * sgb[token(g, u), :]
        return tuple(state)

    lax.fori_loop(0, TOK // 8, scan_step, empty)

    def reach_step(g, cum):
        for u in range(8):
            cum = cum + dtb3[token(g, u), :]
            sgt = sgb[token(g, u), :]
            for n in range(ST):
                c = bcx[g, pl.ds(u, 1), pl.ds((ST + n) * LANES, LANES)]
                gb[pl.ds(pl.multiple_of(g * 1024, 1024) + u * 128 + n * 8, 8), :] = (c * sgt) * jnp.exp2(cum * a2b[pl.ds(n * 8, 8), :])
        return cum

    lax.fori_loop(0, TOK // 8, reach_step, jnp.zeros((TILES, LANES), F32))

    drain(kz_in.at[pl.ds(0, 240), :], recv_sem.at[KZ])
    row = iota((TOK, 256), 0)
    want = ((row >> 1) & (NZ - 1)) * 16 + (row >> 5) * 2 + (row & 1)
    for half in range(2):
        sel = (iota((TOK, 256), 1) == want + half * 8).astype(F32).astype(BF16)
        kx_out[:, pl.ds(half * LANES, LANES)] = dot(sel, kz_in[...]).astype(BF16)

    for d in far_x:
        to = (mx + d) % NX
        remote(kx_out.at[block_of(to), :], kx_in.at[block_of(mx), :], KX, along_x(d)).start()
    kx_in[block_of(mx), :] = kx_out[block_of(mx), :]

    drain(s_in.at[pl.ds(0, NZ - 1)], recv_sem.at[SZ])
    for jj in range(2):
        run = jnp.zeros((1, LANES), F32)
        for z in range(NZ):
            for half in range(2):
                decay[half, pl.ds(z * 16 + jj * 8, 8), :] = jnp.exp2(a2s[half][jj] * s_in[z, jj])
            cum_out[z, jj] = run
            run = run + s_in[z, jj]
        sx_out[jj] = run

    def pair_of(i):
        return pl.ds(2 * i, 2)

    def to_planes(src, dst, k):
        for dx in (3, 2, 1):

            @pl.when(mx + dx < NX)
            def _():
                for dz in (-2, -1, 1, 0):
                    pltpu.make_async_remote_copy(
                        src_ref=src, dst_ref=dst, send_sem=send_sem.at[k + dx - 1], recv_sem=recv_sem.at[k + mx],
                        device_id=along_xz(dx, dz),
                    ).start()

    @pl.when(mx < NX - 1)
    def _():
        to_planes(sx_out, sx_in.at[mx, pair_of(mq)], CX)

    for dz in (-2, -1, 1):
        remote(cum_out.at[(mz + dz + NZ) % NZ], cum_in.at[pair_of(mq)], CZ, along_z(dz)).start()
    cum_in[pair_of(mq)] = cum_out[mz]

    for half in range(2):
        drain(l_in.at[half, pl.ds(0, 240), :], recv_sem.at[LZ + half])
        carry = jnp.zeros((16, LANES), F32)
        for z in range(NZ):
            rows = pl.ds(z * 16, 16)
            before[half, rows, :] = carry.astype(BF16)
            carry = decay[half, rows, :] * carry + l_in[half, rows, :].astype(F32)
        t_out[half] = carry.astype(BF16)

        @pl.when(mx < NX - 1)
        def _():
            to_planes(t_out.at[half], t_in.at[half, mx, quarter_of(mq)], TX + 3 * half)

        for dz in (-2, -1, 1):
            to = (mz + dz + NZ) % NZ
            remote(before.at[half, quarter_of(to), :], h_in.at[half, quarter_of(mq), :], HZ + half, along_z(dz)).start()
        h_in[half, quarter_of(mq), :] = before[half, quarter_of(mz), :]

    carry_x[...] = jnp.zeros_like(carry_x)
    for i in range(NX - 1):

        @pl.when(i < mx)
        def _():
            drain(sx_in.at[i], recv_sem.at[CX + i])
            for j in range(TILES):
                for half in range(2):
                    rows = pl.ds(half * 64 + j * 8, 8)
                    plane[i, rows, :] = jnp.exp2(a2n[rows, :] * sx_in[i, j])

    drain(cum_in.at[pl.ds(0, 6)], recv_sem.at[CZ])
    for j in range(TILES):
        for half in range(2):
            rows = pl.ds(half * 64 + j * 8, 8)
            reach[rows, :] = jnp.exp2(a2n[rows, :] * cum_in[j])
    for half in range(2):
        rows = pl.ds(half * 64, 64)
        for i in range(NX - 1):

            @pl.when(i < mx)
            def _():
                drain(t_in.at[half, i], recv_sem.at[TX + 3 * half + i])
                carry_x[rows, :] = plane[i, rows, :] * carry_x[rows, :] + t_in[half, i].astype(F32)

        drain(h_in.at[half, pl.ds(0, 48), :], recv_sem.at[HZ + half])
        hf[rows, :] = h_in[half].astype(F32) + reach[rows, :] * carry_x[rows, :]

    drain(kx_in.at[pl.ds(0, 96), :], recv_sem.at[KX])

    drain(halo, send_sem.at[HALO])
    drain(r0_in.at[pl.ds(0, TOK - 16), :], send_sem.at[R0])

    @pl.when(mc > 0)
    def _():
        drain(rs_in.at[pl.ds(0, TOK - 32), :], send_sem.at[RS])
        drain(lr.at[pl.ds(0, TOK - 16), :], send_sem.at[AG])

    @pl.when(mc == 0)
    def _():
        drain(rs_in.at[pl.ds(0, TOK - 16), :], send_sem.at[RS])

    drain(kz_in.at[pl.ds(0, 240), :], send_sem.at[KZ])
    drain(kx_in.at[pl.ds(0, 96), :], send_sem.at[KX])
    drain(s_in.at[pl.ds(0, NZ - 1)], send_sem.at[SZ])
    for half in range(2):
        drain(l_in.at[half, pl.ds(0, 240), :], send_sem.at[LZ + half])
        drain(h_in.at[half, pl.ds(0, 48), :], send_sem.at[HZ + half])
    for dx in (1, 2, 3):

        @pl.when(mx + dx < NX)
        def _():
            drain(sx_in.at[0], send_sem.at[CX + dx - 1])
            for half in range(2):
                drain(t_in.at[half, 0], send_sem.at[TX + 3 * half + dx - 1])

    drain(cum_in.at[pl.ds(0, 6)], send_sem.at[CZ])


def finish(gb, yb, hf, kept, gated_hbm, kept_hbm, ys, gated_v, sem):
    kept_copy = pltpu.make_async_copy(kept, kept_hbm.at[0], sem.at[PARTS])
    kept_copy.start()
    carried = [hf[pl.ds((n // 8) * 64 + n % 8, TILES, stride=8), :] for n in range(ST)]
    rows = TOK // PARTS
    copies = []
    for part in range(PARTS):

        def add_step(g, _):
            for u in range(8):
                at = pl.ds(pl.multiple_of(g * 64, 64) + u * 8, 8)
                y = [yb[at, :], None, None, None]
                for n in range(ST):
                    term = gb[pl.ds(pl.multiple_of(g * 1024, 1024) + u * 128 + n * 8, 8), :] * carried[n]
                    y[n % 4] = term if y[n % 4] is None else y[n % 4] + term
                ys[at, :] = (y[0] + y[1]) + (y[2] + y[3])
            return 0

        lax.fori_loop(part * rows // 8, (part + 1) * rows // 8, add_step, 0)
        here = pl.ds(part * rows, rows)
        for j in range(TILES):
            y = ys[pl.ds(part * rows * TILES + j, rows, stride=TILES), :]
            gated_v[here, pl.ds(j * LANES, LANES)] = y.astype(BF16)
        copies.append(pltpu.make_async_copy(gated_v.at[here, :], gated_hbm.at[here, :], sem.at[part]))
        copies[-1].start()
    for c in copies:
        c.wait()
    kept_copy.wait()


def local(
    x_in, gate_in, conv_weight, conv_bias, proj_low, proj_bc, dt_weight, dt_bias, decay_log, skip_gain, attn_kv,
    kept_index, kept_owner,
):
    V = pltpu.VMEM
    hbm = pl.BlockSpec(memory_space=pltpu.HBM)
    vmem = pl.BlockSpec(memory_space=pltpu.VMEM)
    pin = functools.partial(pltpu.with_memory_space_constraint, memory_space=pltpu.HBM)
    parts = pl.pallas_call(
        kernel,
        out_shape=(
            V((TOK * ST * TILES, LANES), F32), V((TOK * TILES, LANES), F32), V((128, LANES), F32), V((TOK, 2 * LANES), BF16),
        ),
        in_specs=[hbm] * 13,
        out_specs=(vmem,) * 4,
        scratch_shapes=[
            V((TOK, CH), BF16), V((TOK, CH), BF16), V((CONV, CH), F32), V((1, CH), F32), V((CH, RANK), BF16),
            V((LANES, CH), BF16), V((RANK, CH), BF16), V((1, CH), F32), V((ST, CH), F32), V((1, CH), F32),
            V((TOK, 2 * LANES), BF16), V((1, KEEP), jnp.int32), V((1, KEEP), jnp.int32), V((ST, 2 * LANES), F32),
            V((32, LANES), BF16), V((32, LANES), BF16), V((32, LANES), F32), V((TOK + 16, CH), F32), V((TOK, CH), BF16),
            V((TOK, RANK + LANES), BF16), V((TOK, RANK + LANES), BF16), V((TOK, RANK + LANES), BF16), V((16, RANK + LANES), BF16), V((TOK, RANK + LANES), BF16),
            V((TOK * TILES, LANES), F32), V((TOK * TILES, LANES), F32), V((TOK // 8, 8, 2 * ST * LANES), F32),
            V((ST * TILES, LANES), F32), V((ST * TILES, LANES), F32), V((ST * TILES, LANES), F32),
            V((TOK * TILES, LANES), F32), V((TILES, LANES), F32),
            V((TILES, 1, LANES), F32), V((NZ, 2, 1, LANES), F32), V((128, LANES), BF16), V((2, NZ * 16, LANES), BF16),
            V((2, 1, LANES), F32), V((NX - 1, TILES, 1, LANES), F32), V((NZ, 2, 1, LANES), F32), V((TILES, 1, LANES), F32),
            V((2, 16, LANES), BF16), V((2, NX - 1, 64, LANES), BF16), V((2, NZ * 16, LANES), BF16), V((2, 64, LANES), BF16),
            V((2, NZ * 16, LANES), F32), V((128, LANES), F32), V((NX - 1, 128, LANES), F32),
            V((128, LANES), F32),
            V((256, LANES), BF16), V((256, LANES), BF16), V((TOK, 2 * LANES), BF16),
            pltpu.SemaphoreType.DMA((15,)),
            pltpu.SemaphoreType.DMA((21,)), pltpu.SemaphoreType.DMA((21,)),
            pltpu.SemaphoreType.REGULAR((4,)),
        ],
        compiler_params=pltpu.CompilerParams(
            collective_id=0, has_side_effects=True, vmem_limit_bytes=40_000_000
        ),
    )(*map(pin, (
        x_in, gate_in, conv_weight, conv_bias.reshape(1, CH), proj_low, proj_bc.T, dt_weight, dt_bias.reshape(1, CH),
        decay_log, skip_gain.reshape(1, CH), attn_kv, kept_index, kept_owner.reshape(1, KEEP),
    )))
    return pl.pallas_call(
        finish,
        out_shape=(jax.ShapeDtypeStruct((TOK, CH), BF16), jax.ShapeDtypeStruct((1, TOK, 2 * LANES), BF16)),
        in_specs=[vmem] * 4,
        out_specs=(hbm, hbm),
        scratch_shapes=[
            V((TOK * TILES, LANES), F32), V((TOK, CH), BF16), pltpu.SemaphoreType.DMA((PARTS + 1,)),
        ],
        compiler_params=pltpu.CompilerParams(vmem_limit_bytes=20_000_000),
    )(*parts)


def solution(mesh):
    return jax.shard_map(
        local,
        mesh=mesh,
        in_specs=(
            P("ctx", "ch"), P("ctx", "ch"), P(None, "ch"), P("ch"), P("ch", None), P("ch", None), P(None, "ch"),
            P("ch"), P(None, "ch"), P("ch"), P("ctx", "ch"), P("ch", "ctx"), P("ch", "ctx", None),
        ),
        out_specs=(P("ctx", "ch"), P("ch", "ctx", None)),
        check_vma=False,
    )
```

```python
import functools
import math

import jax
import jax.numpy as jnp
from jax import lax
from jax.experimental import pallas as pl
from jax.experimental.pallas import tpu as pltpu
from jax.sharding import PartitionSpec as P

MOST = 2
PARTS = 4
NZ = 16
NX = 4
NC = 8
TOK = 128
CH = 1024
ST = 16
CONV = 4
RANK = 256
LANES = 128
TILES = CH // LANES
KEEP = 32
F32 = jnp.float32
BF16 = jnp.bfloat16
LOG2E = math.log2(math.e)


def dot(a, b):
    return jnp.dot(a, b, preferred_element_type=F32)


def dot_rows(a, b):
    return lax.dot_general(a, b, (((0,), (0,)), ((), ())), preferred_element_type=F32)


def silu(v):
    return v / (1.0 + jnp.exp(-v))


def iota(shape, dim):
    return lax.broadcasted_iota(jnp.int32, shape, dim)


def kernel(
    x_hbm, gate_hbm, cw_hbm, cb_hbm, low_hbm, bc_hbm, dtw_hbm, dtb_hbm, dec_hbm, skip_hbm, kv_hbm, idx_hbm, own_hbm,
    gb, yb, hf, kept_out,
    x_v, gate_v, cw_v, cb_v, low_v, bc_v, dtw_v, dtb_v, dec_v, skip_v, kv_v, idx_v, own_v, decs_v,
    halo, halo_out, halo_f, xs, act, part, rs_in, r0_in, ag_out, lr, dtb3, xb3, bcx, a2b, a2n, lb, sgb, skip_b,
    s_out, s_in, l_out, l_in, sx_out, sx_in, cum_out, cum_in, t_out, t_in, before, h_in, decay, reach,
    plane, carry_x,
    kz_out, kz_in, kx_out,
    in_sem, send_sem, recv_sem, here_sem,
):
    kx_in = kept_out
    me = lax.axis_index("ctx")
    mc = lax.axis_index("ch")
    mx = me // NZ
    mz = me % NZ
    mq = mz % 4

    loads = [
        (x_hbm, x_v), (cw_hbm, cw_v), (cb_hbm, cb_v), (idx_hbm, idx_v), (own_hbm, own_v), (kv_hbm, kv_v),
        (low_hbm, low_v), (bc_hbm, bc_v.at[pl.ds(0, 2 * ST), :]), (bc_hbm, bc_v.at[pl.ds(2 * ST, 2 * ST), :]),
        (dec_hbm, dec_v),
        (dec_hbm.at[:, pl.ds(pl.multiple_of(mq * 2 * LANES, 2 * LANES), 2 * LANES)], decs_v),
        (dtw_hbm, dtw_v), (dtb_hbm, dtb_v), (skip_hbm, skip_v), (gate_hbm, gate_v),
    ]
    loads = [pltpu.make_async_copy(s, d, in_sem.at[i]) for i, (s, d) in enumerate(loads)]
    (x_ld, cw_ld, cb_ld, idx_ld, own_ld, kv_ld, low_ld, bc_ld, bc2_ld, dec_ld, decs_ld, dtw_ld, dtb_ld, skip_ld, gate_ld) = loads

    for c in loads[:3]:
        c.start()

    def along_z(d):
        return {"ctx": mx * NZ + (mz + d + NZ) % NZ}

    def along_x(d):
        return {"ctx": ((mx + d) % NX) * NZ + mz}

    def along_xz(dx, dz):
        return {"ctx": ((mx + dx) % NX) * NZ + (mz + dz + NZ) % NZ}

    def along_ch(dy, dc):
        return {"ch": ((mc // 2 + dy) % (NC // 2)) * 2 + (mc + dc) % 2}

    far_z = (8, 7, 9, 6, 10, 5, 11, 4, 12, 3, 13, 2, 14, 1, 15)
    far_x = (2, 1, 3)
    far_ch = ((2, 0), (2, 1), (1, 0), (3, 0), (1, 1), (3, 1), (0, 1))
    right = {"ctx": (me + 1) % (NX * NZ)}
    left = {"ctx": (me + NX * NZ - 1) % (NX * NZ)}
    barrier = pltpu.get_barrier_semaphore()
    for d in far_ch:
        pl.semaphore_signal(barrier, inc=1, device_id=along_ch(*d))
    for d in (-1, 1):
        pl.semaphore_signal(barrier, inc=1, device_id=along_z(d))
    for d in far_x:
        pl.semaphore_signal(barrier, inc=1, device_id=along_x(d))

    @pl.when(mz == NZ - 1)
    def _():
        pl.semaphore_signal(barrier, inc=1, device_id=right)

    @pl.when(mz == 0)
    def _():
        pl.semaphore_signal(barrier, inc=1, device_id=left)

    for c in loads[3:]:
        c.start()

    def tell(i):
        for d in (-(1 << i), 1 << i):
            pl.semaphore_signal(here_sem.at[i], inc=1, device_id=along_z(d))

    def hear(i):
        pl.semaphore_wait(here_sem.at[i], 2)

    def tell_x():
        for d in far_x:
            pl.semaphore_signal(here_sem.at[3], inc=1, device_id=along_x(d))

    def hear_x():
        pl.semaphore_wait(here_sem.at[3], NX - 1)

    def remote(src, dst, k, peer):
        return pltpu.make_async_remote_copy(
            src_ref=src, dst_ref=dst, send_sem=send_sem.at[k], recv_sem=recv_sem.at[k], device_id=peer
        )

    def drain(ref, sem):
        pltpu.make_async_copy(ref, ref, sem).wait()

    HALO, RS, AG, KZ, KX, SZ, LZ, CZ, HZ, R0, CX, TX = (0, 1, 2, 3, 4, 5, 6, 7, 8, 9, 10, 13)

    bc_v[pl.ds(4 * ST, LANES - 4 * ST), :] = jnp.zeros((LANES - 4 * ST, CH), BF16)

    x_ld.wait()
    for j in range(TILES):
        halo_f[pl.ds(4 * j, 4), :] = x_v[pl.ds(TOK - 16, 16), pl.ds(j * LANES, LANES)].astype(F32)[12:, :]
    halo_out[...] = halo_f[...].astype(BF16)
    pl.semaphore_wait(barrier, NC - 1 + NX - 1 + 2 + jnp.where((mz == 0) | (mz == NZ - 1), 1, 0))

    remote(halo_out, halo, HALO, right).start()
    tell(0)

    def conv(first, rows):
        for j in range(TILES):
            cols = pl.ds(j * LANES, LANES)
            s = jnp.broadcast_to(cb_v[:, cols], (rows, LANES))
            for k in range(CONV):
                s = s + cw_v[pl.ds(k, 1), cols] * xs[pl.ds(first + 16 - (CONV - 1) + k, rows), cols]
            a = silu(s).astype(BF16)
            act[pl.ds(first, rows), cols] = a
            xb3[pl.ds(first * TILES + j, rows, stride=TILES), :] = a.astype(F32)

    def project(first, rows):
        a = act[pl.ds(first, rows), :]
        part[pl.ds(first, rows), pl.ds(0, RANK)] = dot(a, low_v[...]).astype(BF16)
        wide = lax.dot_general(a, bc_v[...], (((1,), (1,)), ((), ())), preferred_element_type=F32)
        high = wide.astype(BF16).astype(F32)
        low = jnp.where(iota((rows, LANES), 1) < 2 * ST, high, wide - high)
        part[pl.ds(first, rows), pl.ds(RANK, LANES)] = low.astype(BF16)

    def summed(ref):
        total = ref[pl.ds(0, 16), :].astype(F32)
        for i in range(1, NC):
            total = total + ref[pl.ds(16 * i, 16), :].astype(F32)
        wide = total[:, RANK:]
        return total[:, :RANK].astype(BF16), (wide + pltpu.roll(wide, LANES - 2 * ST, 1)).astype(BF16)

    def rows_of(i):
        return pl.ds(pl.multiple_of(i * 16, 16), 16)

    cw_ld.wait()
    cb_ld.wait()
    xs[pl.ds(16, TOK), :] = x_v[...].astype(F32)
    conv(16, TOK - 16)
    low_ld.wait()
    bc_ld.wait()
    bc2_ld.wait()
    project(16, TOK - 16)

    for d in far_ch:
        to = along_ch(*d)

        @pl.when(to["ch"] > 0)
        def _():
            remote(part.at[rows_of(to["ch"]), :], rs_in.at[rows_of(mc), :], RS, to).start()

    hear(0)
    tell(1)
    tell_x()
    drain(halo, recv_sem.at[HALO])
    halo_f[...] = halo[...].astype(F32)
    for j in range(TILES):
        xs[pl.ds(12, 4), pl.ds(j * LANES, LANES)] = jnp.where(me > 0, halo_f[pl.ds(4 * j, 4), :], 0.0)
    conv(0, 16)
    project(0, 16)
    for d in far_ch:
        remote(part.at[pl.ds(0, 16), :], r0_in.at[rows_of(mc), :], R0, along_ch(*d)).start()
    r0_in[rows_of(mc), :] = part[pl.ds(0, 16), :]

    idx_ld.wait()
    own_ld.wait()
    kv_ld.wait()
    own_row = own_v[...]
    eye = iota((KEEP, KEEP), 0) == iota((KEEP, KEEP), 1)
    own = jnp.sum(jnp.where(eye, own_row, 0), axis=1, keepdims=True)
    same = (own_row == own) & (iota((KEEP, KEEP), 1) < iota((KEEP, KEEP), 0))
    rank = jnp.sum(jnp.where(same, 1, 0), axis=1, keepdims=True)
    place = (own & (NZ - 1)) * 16 + (own >> 4) * 2 + rank
    src_t = (iota((TOK, KEEP), 0) == idx_v[...] - me * TOK).astype(F32).astype(BF16)
    picked = dot_rows(src_t, kv_v[...]).astype(BF16)
    slots = iota((KEEP, 256), 1)
    kz = dot_rows((slots == place).astype(F32).astype(BF16), picked[:, :LANES])
    kz = kz + dot_rows((slots == place + 8).astype(F32).astype(BF16), picked[:, LANES:])
    kz_out[...] = kz.astype(BF16)

    hear(1)
    tell(2)

    dec_ld.wait()
    decs_ld.wait()
    gate_ld.wait()
    for j in range(TILES):
        rate = -LOG2E * jnp.exp(dec_v[:, pl.ds(j * LANES, LANES)])
        a2n[pl.ds(j * ST, ST), :] = rate
        a2b[pl.ds(j, ST, stride=TILES), :] = rate
    a2s = [-LOG2E * jnp.exp(decs_v[:, pl.ds(jj * LANES, LANES)]) for jj in range(2)]
    skip_ld.wait()
    for j in range(TILES):
        cols = pl.ds(j * LANES, LANES)
        sgb[pl.ds(j, TOK, stride=TILES), :] = silu(gate_v[:, cols].astype(F32))
        skip_b[pl.ds(j, 1), :] = skip_v[:, cols]

    @pl.when(mc > 0)
    def _():
        rs_in[rows_of(mc), :] = part[rows_of(mc), :]
        drain(rs_in.at[pl.ds(0, TOK - 16), :], recv_sem.at[RS])
        low, coeff = summed(rs_in)
        ag_out[:, pl.ds(0, RANK)] = low
        ag_out[:, pl.ds(RANK, LANES)] = coeff
        for d in far_ch:
            remote(ag_out, lr.at[rows_of(mc), :], AG, along_ch(*d)).start()
        lr[rows_of(mc), :] = ag_out[...]

    hear(2)
    hear_x()
    for d in far_z:
        to = (mz + d) % NZ
        remote(kz_out.at[rows_of(to), :], kz_in.at[rows_of(mz), :], KZ, along_z(d)).start()
    kz_in[rows_of(mz), :] = kz_out[rows_of(mz), :]

    dtw_ld.wait()
    dtb_ld.wait()
    drain(r0_in.at[pl.ds(0, TOK - 16), :], recv_sem.at[R0])
    low, coeff = summed(r0_in)
    lr[pl.ds(0, 16), pl.ds(0, RANK)] = low
    lr[pl.ds(0, 16), pl.ds(RANK, LANES)] = coeff

    @pl.when(mc > 0)
    def _():
        drain(lr.at[pl.ds(0, TOK - 32), :], recv_sem.at[AG])

    @pl.when(mc == 0)
    def _():
        drain(lr.at[pl.ds(0, TOK - 16), :], recv_sem.at[AG])

    for j in range(TILES):
        cols = pl.ds(j * LANES, LANES)
        v = dot(lr[:, pl.ds(0, RANK)], dtw_v[:, cols]) + dtb_v[:, cols]
        v = jnp.maximum(v, 0.0) + jnp.log1p(jnp.exp(-jnp.abs(v)))
        dtb3[pl.ds(j, TOK, stride=TILES), :] = v
        s_out[j] = jnp.sum(v, axis=0, keepdims=True)
    coeff = lr[:, pl.ds(RANK, LANES)]

    def spread(i):
        rows = (iota((LANES, 4 * LANES), 1) >> 7) + 4 * i == iota((LANES, 4 * LANES), 0)
        wide = dot(coeff, rows.astype(F32).astype(BF16))
        bcx[:, :, pl.ds(i * 4 * LANES, 4 * LANES)] = wide.reshape(TOK // 8, 8, 4 * LANES)

    for i in range(4):
        spread(i)

    def token(g, u):
        return pl.ds(pl.multiple_of(g * 64, 64) + u * 8, 8)

    for d in far_z:
        to = (mz + d) % 4
        remote(s_out.at[pl.ds(2 * to, 2)], s_in.at[mz], SZ, along_z(d)).start()
    s_in[mz] = s_out[pl.ds(2 * mq, 2)]

    def end_step(g, state):
        state = list(state)
        for u in range(8):
            dt = dtb3[token(g, u), :]
            dx = dt * xb3[token(g, u), :]
            for n in range(ST):
                b = bcx[g, pl.ds(u, 1), pl.ds(n * LANES, LANES)]
                state[n] = jnp.exp2(dt * a2b[pl.ds(n * 8, 8), :]) * state[n] + dx * b
        return tuple(state)

    empty = tuple(jnp.zeros((TILES, LANES), F32) for _ in range(ST))
    state = lax.fori_loop(0, TOK // 8, end_step, empty)
    for n in range(ST):
        lb[pl.ds(n * 8, 8), :] = state[n]
    for j in range(TILES):
        l_out[pl.ds(j * ST, ST), :] = lb[pl.ds(j, ST, stride=TILES), :].astype(BF16)

    def block_of(i):
        return pl.ds(pl.multiple_of(i * 32, 32), 32)

    for d in far_z:
        to = (mz + d) % 4
        remote(l_out.at[block_of(to), :], l_in.at[block_of(mz), :], LZ, along_z(d)).start()
    l_in[block_of(mz), :] = l_out[block_of(mq), :]

    for i in range(4, 8):
        spread(i)

    def scan_step(g, state):
        state = list(state)
        for u in range(8):
            dt = dtb3[token(g, u), :]
            xt = xb3[token(g, u), :]
            dx = dt * xt
            y = [skip_b[...] * xt, None, None, None]
            for n in range(ST):
                b = bcx[g, pl.ds(u, 1), pl.ds(n * LANES, LANES)]
                c = bcx[g, pl.ds(u, 1), pl.ds((ST + n) * LANES, LANES)]
                state[n] = jnp.exp2(dt * a2b[pl.ds(n * 8, 8), :]) * state[n] + dx * b
                term = c * state[n]
                y[n % 4] = term if y[n % 4] is None else y[n % 4] + term
            yb[token(g, u), :] = ((y[0] + y[1]) + (y[2] + y[3])) * sgb[token(g, u), :]
        return tuple(state)

    lax.fori_loop(0, TOK // 8, scan_step, empty)

    def reach_step(g, cum):
        for u in range(8):
            cum = cum + dtb3[token(g, u), :]
            sgt = sgb[token(g, u), :]
            for n in range(ST):
                c = bcx[g, pl.ds(u, 1), pl.ds((ST + n) * LANES, LANES)]
                gb[pl.ds(pl.multiple_of(g * 1024, 1024) + u * 128 + n * 8, 8), :] = (c * sgt) * jnp.exp2(cum * a2b[pl.ds(n * 8, 8), :])
        return cum

    lax.fori_loop(0, TOK // 8, reach_step, jnp.zeros((TILES, LANES), F32))

    drain(kz_in.at[pl.ds(0, 240), :], recv_sem.at[KZ])
    row = iota((TOK, 256), 0)
    want = ((row >> 1) & (NZ - 1)) * 16 + (row >> 5) * 2 + (row & 1)
    for half in range(2):
        sel = (iota((TOK, 256), 1) == want + half * 8).astype(F32).astype(BF16)
        kx_out[:, pl.ds(half * LANES, LANES)] = dot(sel, kz_in[...]).astype(BF16)

    for d in far_x:
        to = (mx + d) % NX
        remote(kx_out.at[block_of(to), :], kx_in.at[block_of(mx), :], KX, along_x(d)).start()
    kx_in[block_of(mx), :] = kx_out[block_of(mx), :]

    drain(s_in.at[pl.ds(0, NZ - 1)], recv_sem.at[SZ])
    for jj in range(2):
        run = jnp.zeros((1, LANES), F32)
        for z in range(NZ):
            decay[pl.ds(z * 32 + jj * ST, ST), :] = jnp.exp2(a2s[jj] * s_in[z, jj])
            cum_out[z, jj] = run
            run = run + s_in[z, jj]
        sx_out[jj] = run

    def pair_of(i):
        return pl.ds(2 * i, 2)

    def to_planes(src, dst, k):
        for dx in (3, 2, 1):

            @pl.when(mx + dx < NX)
            def _():
                for dz in (-2, -1, 1, 0):
                    pltpu.make_async_remote_copy(
                        src_ref=src, dst_ref=dst, send_sem=send_sem.at[k + dx - 1], recv_sem=recv_sem.at[k + mx],
                        device_id=along_xz(dx, dz),
                    ).start()

    @pl.when(mx < NX - 1)
    def _():
        to_planes(sx_out, sx_in.at[mx, pair_of(mq)], CX)

    for dz in (-2, -1, 1):
        remote(cum_out.at[(mz + dz + NZ) % NZ], cum_in.at[pair_of(mq)], CZ, along_z(dz)).start()
    cum_in[pair_of(mq)] = cum_out[mz]

    drain(l_in.at[pl.ds(0, 480), :], recv_sem.at[LZ])
    for jj in range(2):
        carry = jnp.zeros((ST, LANES), F32)
        for z in range(NZ):
            rows = pl.ds(z * 32 + jj * ST, ST)
            before[rows, :] = carry.astype(BF16)
            carry = decay[rows, :] * carry + l_in[rows, :].astype(F32)
        t_out[pl.ds(jj * ST, ST), :] = carry.astype(BF16)

    @pl.when(mx < NX - 1)
    def _():
        to_planes(t_out, t_in.at[mx, block_of(mq)], TX)

    for dz in (-2, -1, 1):
        remote(before.at[block_of((mz + dz + NZ) % NZ), :], h_in.at[block_of(mq), :], HZ, along_z(dz)).start()
    h_in[block_of(mq), :] = before[block_of(mz), :]

    carry_x[...] = jnp.zeros_like(carry_x)
    for i in range(NX - 1):

        @pl.when(i < mx)
        def _():
            drain(sx_in.at[i], recv_sem.at[CX + i])
            for j in range(TILES):
                rows = pl.ds(j * ST, ST)
                plane[pl.ds(i * 128 + j * ST, ST), :] = jnp.exp2(a2n[rows, :] * sx_in[i, j])

    drain(cum_in.at[pl.ds(0, 6)], recv_sem.at[CZ])
    for j in range(TILES):
        rows = pl.ds(j * ST, ST)
        reach[rows, :] = jnp.exp2(a2n[rows, :] * cum_in[j])
    for i in range(NX - 1):

        @pl.when(i < mx)
        def _():
            drain(t_in.at[i], recv_sem.at[TX + i])
            carry_x[...] = plane[pl.ds(i * 128, 128), :] * carry_x[...] + t_in[i].astype(F32)

    drain(h_in.at[pl.ds(0, 96), :], recv_sem.at[HZ])
    hf[...] = h_in[...].astype(F32) + reach[...] * carry_x[...]

    drain(kx_in.at[pl.ds(0, 96), :], recv_sem.at[KX])

    drain(halo, send_sem.at[HALO])
    drain(r0_in.at[pl.ds(0, TOK - 16), :], send_sem.at[R0])

    @pl.when(mc > 0)
    def _():
        drain(rs_in.at[pl.ds(0, TOK - 32), :], send_sem.at[RS])
        drain(lr.at[pl.ds(0, TOK - 16), :], send_sem.at[AG])

    @pl.when(mc == 0)
    def _():
        drain(rs_in.at[pl.ds(0, TOK - 16), :], send_sem.at[RS])

    drain(kz_in.at[pl.ds(0, 240), :], send_sem.at[KZ])
    drain(kx_in.at[pl.ds(0, 96), :], send_sem.at[KX])
    drain(s_in.at[pl.ds(0, NZ - 1)], send_sem.at[SZ])
    drain(l_in.at[pl.ds(0, 480), :], send_sem.at[LZ])
    for dx in (1, 2, 3):

        @pl.when(mx + dx < NX)
        def _():
            drain(sx_in.at[0], send_sem.at[CX + dx - 1])
            drain(t_in.at[0], send_sem.at[TX + dx - 1])

    drain(cum_in.at[pl.ds(0, 6)], send_sem.at[CZ])
    drain(h_in.at[pl.ds(0, 96), :], send_sem.at[HZ])


def finish(gb, yb, hf, kept, gated_hbm, kept_hbm, ys, gated_v, sem):
    kept_copy = pltpu.make_async_copy(kept, kept_hbm.at[0], sem.at[PARTS])
    kept_copy.start()
    carried = [hf[pl.ds(n, TILES, stride=ST), :] for n in range(ST)]
    rows = TOK // PARTS
    copies = []
    for part in range(PARTS):

        def add_step(g, _):
            for u in range(8):
                at = pl.ds(pl.multiple_of(g * 64, 64) + u * 8, 8)
                y = [yb[at, :], None, None, None]
                for n in range(ST):
                    term = gb[pl.ds(pl.multiple_of(g * 1024, 1024) + u * 128 + n * 8, 8), :] * carried[n]
                    y[n % 4] = term if y[n % 4] is None else y[n % 4] + term
                ys[at, :] = (y[0] + y[1]) + (y[2] + y[3])
            return 0

        lax.fori_loop(part * rows // 8, (part + 1) * rows // 8, add_step, 0)
        here = pl.ds(part * rows, rows)
        for j in range(TILES):
            y = ys[pl.ds(part * rows * TILES + j, rows, stride=TILES), :]
            gated_v[here, pl.ds(j * LANES, LANES)] = y.astype(BF16)
        copies.append(pltpu.make_async_copy(gated_v.at[here, :], gated_hbm.at[here, :], sem.at[part]))
        copies[-1].start()
    for c in copies:
        c.wait()
    kept_copy.wait()


def local(
    x_in, gate_in, conv_weight, conv_bias, proj_low, proj_bc, dt_weight, dt_bias, decay_log, skip_gain, attn_kv,
    kept_index, kept_owner,
):
    V = pltpu.VMEM
    hbm = pl.BlockSpec(memory_space=pltpu.HBM)
    vmem = pl.BlockSpec(memory_space=pltpu.VMEM)
    pin = functools.partial(pltpu.with_memory_space_constraint, memory_space=pltpu.HBM)
    parts = pl.pallas_call(
        kernel,
        out_shape=(
            V((TOK * ST * TILES, LANES), F32), V((TOK * TILES, LANES), F32), V((128, LANES), F32), V((TOK, 2 * LANES), BF16),
        ),
        in_specs=[hbm] * 13,
        out_specs=(vmem,) * 4,
        scratch_shapes=[
            V((TOK, CH), BF16), V((TOK, CH), BF16), V((CONV, CH), F32), V((1, CH), F32), V((CH, RANK), BF16),
            V((LANES, CH), BF16), V((RANK, CH), BF16), V((1, CH), F32), V((ST, CH), F32), V((1, CH), F32),
            V((TOK, 2 * LANES), BF16), V((1, KEEP), jnp.int32), V((1, KEEP), jnp.int32), V((ST, 2 * LANES), F32),
            V((32, LANES), BF16), V((32, LANES), BF16), V((32, LANES), F32), V((TOK + 16, CH), F32), V((TOK, CH), BF16),
            V((TOK, RANK + LANES), BF16), V((TOK, RANK + LANES), BF16), V((TOK, RANK + LANES), BF16), V((16, RANK + LANES), BF16), V((TOK, RANK + LANES), BF16),
            V((TOK * TILES, LANES), F32), V((TOK * TILES, LANES), F32), V((TOK // 8, 8, 2 * ST * LANES), F32),
            V((ST * TILES, LANES), F32), V((ST * TILES, LANES), F32), V((ST * TILES, LANES), F32),
            V((TOK * TILES, LANES), F32), V((TILES, LANES), F32),
            V((TILES, 1, LANES), F32), V((NZ, 2, 1, LANES), F32), V((ST * TILES, LANES), BF16), V((NZ * 32, LANES), BF16),
            V((2, 1, LANES), F32), V((NX - 1, TILES, 1, LANES), F32), V((NZ, 2, 1, LANES), F32), V((TILES, 1, LANES), F32),
            V((32, LANES), BF16), V((NX - 1, 128, LANES), BF16), V((NZ * 32, LANES), BF16), V((128, LANES), BF16),
            V((NZ * 32, LANES), F32), V((128, LANES), F32), V(((NX - 1) * 128, LANES), F32),
            V((128, LANES), F32),
            V((256, LANES), BF16), V((256, LANES), BF16), V((TOK, 2 * LANES), BF16),
            pltpu.SemaphoreType.DMA((15,)),
            pltpu.SemaphoreType.DMA((16,)), pltpu.SemaphoreType.DMA((16,)),
            pltpu.SemaphoreType.REGULAR((4,)),
        ],
        compiler_params=pltpu.CompilerParams(
            collective_id=0, has_side_effects=True, vmem_limit_bytes=40_000_000
        ),
    )(*map(pin, (
        x_in, gate_in, conv_weight, conv_bias.reshape(1, CH), proj_low, proj_bc.T, dt_weight, dt_bias.reshape(1, CH),
        decay_log, skip_gain.reshape(1, CH), attn_kv, kept_index, kept_owner.reshape(1, KEEP),
    )))
    return pl.pallas_call(
        finish,
        out_shape=(jax.ShapeDtypeStruct((TOK, CH), BF16), jax.ShapeDtypeStruct((1, TOK, 2 * LANES), BF16)),
        in_specs=[vmem] * 4,
        out_specs=(hbm, hbm),
        scratch_shapes=[
            V((TOK * TILES, LANES), F32), V((TOK, CH), BF16), pltpu.SemaphoreType.DMA((PARTS + 1,)),
        ],
        compiler_params=pltpu.CompilerParams(vmem_limit_bytes=20_000_000),
    )(*parts)


def solution(mesh):
    return jax.shard_map(
        local,
        mesh=mesh,
        in_specs=(
            P("ctx", "ch"), P("ctx", "ch"), P(None, "ch"), P("ch"), P("ch", None), P("ch", None), P(None, "ch"),
            P("ch"), P(None, "ch"), P("ch"), P("ctx", "ch"), P("ch", "ctx"), P("ch", "ctx", None),
        ),
        out_specs=(P("ctx", "ch"), P("ch", "ctx", None)),
        check_vma=False,
    )
```

```python
import functools
import math

import jax
import jax.numpy as jnp
from jax import lax
from jax.experimental import pallas as pl
from jax.experimental.pallas import tpu as pltpu
from jax.sharding import PartitionSpec as P

MOST = 2
PARTS = 4
NZ = 16
NX = 4
NC = 8
TOK = 128
CH = 1024
ST = 16
CONV = 4
RANK = 256
LANES = 128
TILES = CH // LANES
KEEP = 32
F32 = jnp.float32
BF16 = jnp.bfloat16
LOG2E = math.log2(math.e)


def dot(a, b):
    return jnp.dot(a, b, preferred_element_type=F32)


def dot_rows(a, b):
    return lax.dot_general(a, b, (((0,), (0,)), ((), ())), preferred_element_type=F32)


def silu(v):
    return v / (1.0 + jnp.exp(-v))


def iota(shape, dim):
    return lax.broadcasted_iota(jnp.int32, shape, dim)


def kernel(
    x_hbm, gate_hbm, cw_hbm, cb_hbm, low_hbm, bc_hbm, dtw_hbm, dtb_hbm, dec_hbm, skip_hbm, kv_hbm, idx_hbm, own_hbm,
    gb, yb, hf, kept_out,
    x_v, gate_v, cw_v, cb_v, low_v, bc_v, dtw_v, dtb_v, dec_v, skip_v, kv_v, idx_v, own_v, decs_v,
    halo, halo_out, halo_f, xs, act, part, rs_in, r0_in, ag_out, lr, dtb3, xb3, bcx, a2b, a2n, lb, sgb, skip_b,
    s_out, s_in, l_out, l_in, sx_out, sx_in, cum_out, cum_in, t_out, t_in, before, h_in, decay, reach,
    plane, carry_x,
    kz_out, kz_in, kx_out,
    in_sem, send_sem, recv_sem, here_sem,
):
    kx_in = kept_out
    me = lax.axis_index("ctx")
    mc = lax.axis_index("ch")
    mx = me // NZ
    mz = me % NZ
    mq = mz % 4

    loads = [
        (x_hbm, x_v), (cw_hbm, cw_v), (cb_hbm, cb_v), (idx_hbm, idx_v), (own_hbm, own_v), (kv_hbm, kv_v),
        (low_hbm, low_v), (bc_hbm, bc_v.at[pl.ds(0, 2 * ST), :]), (bc_hbm, bc_v.at[pl.ds(2 * ST, 2 * ST), :]),
        (dec_hbm, dec_v),
        (dec_hbm.at[:, pl.ds(pl.multiple_of(mq * 2 * LANES, 2 * LANES), 2 * LANES)], decs_v),
        (dtw_hbm, dtw_v), (dtb_hbm, dtb_v), (skip_hbm, skip_v), (gate_hbm, gate_v),
    ]
    loads = [pltpu.make_async_copy(s, d, in_sem.at[i]) for i, (s, d) in enumerate(loads)]
    (x_ld, cw_ld, cb_ld, idx_ld, own_ld, kv_ld, low_ld, bc_ld, bc2_ld, dec_ld, decs_ld, dtw_ld, dtb_ld, skip_ld, gate_ld) = loads

    for c in loads[:3]:
        c.start()

    def along_z(d):
        return {"ctx": mx * NZ + (mz + d + NZ) % NZ}

    def along_x(d):
        return {"ctx": ((mx + d) % NX) * NZ + mz}

    def along_xz(dx, dz):
        return {"ctx": ((mx + dx) % NX) * NZ + (mz + dz + NZ) % NZ}

    def along_ch(dy, dc):
        return {"ch": ((mc // 2 + dy) % (NC // 2)) * 2 + (mc + dc) % 2}

    far_z = (8, 7, 9, 6, 10, 5, 11, 4, 12, 3, 13, 2, 14, 1, 15)
    far_x = (2, 1, 3)
    far_ch = ((2, 0), (2, 1), (1, 0), (3, 0), (1, 1), (3, 1), (0, 1))
    right = {"ctx": (me + 1) % (NX * NZ)}
    left = {"ctx": (me + NX * NZ - 1) % (NX * NZ)}
    barrier = pltpu.get_barrier_semaphore()
    for d in far_ch:
        pl.semaphore_signal(barrier, inc=1, device_id=along_ch(*d))
    for d in (-1, 1):
        pl.semaphore_signal(barrier, inc=1, device_id=along_z(d))
    for d in far_x:
        pl.semaphore_signal(barrier, inc=1, device_id=along_x(d))

    @pl.when(mz == NZ - 1)
    def _():
        pl.semaphore_signal(barrier, inc=1, device_id=right)

    @pl.when(mz == 0)
    def _():
        pl.semaphore_signal(barrier, inc=1, device_id=left)

    for c in loads[3:]:
        c.start()

    def tell(i):
        for d in (-(1 << i), 1 << i):
            pl.semaphore_signal(here_sem.at[i], inc=1, device_id=along_z(d))

    def hear(i):
        pl.semaphore_wait(here_sem.at[i], 2)

    def tell_x():
        for d in far_x:
            pl.semaphore_signal(here_sem.at[3], inc=1, device_id=along_x(d))

    def hear_x():
        pl.semaphore_wait(here_sem.at[3], NX - 1)

    def remote(src, dst, k, peer):
        return pltpu.make_async_remote_copy(
            src_ref=src, dst_ref=dst, send_sem=send_sem.at[k], recv_sem=recv_sem.at[k], device_id=peer
        )

    def drain(ref, sem):
        pltpu.make_async_copy(ref, ref, sem).wait()

    HALO, RS, AG, KZ, KX, SZ, LZ, CZ, HZ, R0, CX, TX = (0, 1, 2, 3, 4, 5, 6, 7, 8, 9, 10, 13)

    bc_v[pl.ds(4 * ST, LANES - 4 * ST), :] = jnp.zeros((LANES - 4 * ST, CH), BF16)

    x_ld.wait()
    for j in range(TILES):
        halo_f[pl.ds(4 * j, 4), :] = x_v[pl.ds(TOK - 16, 16), pl.ds(j * LANES, LANES)].astype(F32)[12:, :]
    halo_out[...] = halo_f[...].astype(BF16)
    pl.semaphore_wait(barrier, NC - 1 + NX - 1 + 2 + jnp.where((mz == 0) | (mz == NZ - 1), 1, 0))

    remote(halo_out, halo, HALO, right).start()
    tell(0)

    def conv(first, rows):
        for j in range(TILES):
            cols = pl.ds(j * LANES, LANES)
            s = jnp.broadcast_to(cb_v[:, cols], (rows, LANES))
            for k in range(CONV):
                s = s + cw_v[pl.ds(k, 1), cols] * xs[pl.ds(first + 16 - (CONV - 1) + k, rows), cols]
            a = silu(s).astype(BF16)
            act[pl.ds(first, rows), cols] = a
            xb3[pl.ds(first * TILES + j, rows, stride=TILES), :] = a.astype(F32)

    def project(first, rows):
        a = act[pl.ds(first, rows), :]
        part[pl.ds(first, rows), pl.ds(0, RANK)] = dot(a, low_v[...]).astype(BF16)
        wide = lax.dot_general(a, bc_v[...], (((1,), (1,)), ((), ())), preferred_element_type=F32)
        high = wide.astype(BF16).astype(F32)
        low = jnp.where(iota((rows, LANES), 1) < 2 * ST, high, wide - high)
        part[pl.ds(first, rows), pl.ds(RANK, LANES)] = low.astype(BF16)

    def summed(ref):
        total = ref[pl.ds(0, 16), :].astype(F32)
        for i in range(1, NC):
            total = total + ref[pl.ds(16 * i, 16), :].astype(F32)
        wide = total[:, RANK:]
        return total[:, :RANK].astype(BF16), (wide + pltpu.roll(wide, LANES - 2 * ST, 1)).astype(BF16)

    def rows_of(i):
        return pl.ds(pl.multiple_of(i * 16, 16), 16)

    cw_ld.wait()
    cb_ld.wait()
    xs[pl.ds(16, TOK), :] = x_v[...].astype(F32)
    conv(16, TOK - 16)
    low_ld.wait()
    bc_ld.wait()
    bc2_ld.wait()
    project(16, TOK - 16)

    for d in far_ch:
        to = along_ch(*d)

        @pl.when(to["ch"] > 0)
        def _():
            remote(part.at[rows_of(to["ch"]), :], rs_in.at[rows_of(mc), :], RS, to).start()

    hear(0)
    tell(1)
    tell_x()
    drain(halo, recv_sem.at[HALO])
    halo_f[...] = halo[...].astype(F32)
    for j in range(TILES):
        xs[pl.ds(12, 4), pl.ds(j * LANES, LANES)] = jnp.where(me > 0, halo_f[pl.ds(4 * j, 4), :], 0.0)
    conv(0, 16)
    project(0, 16)
    for d in far_ch:
        remote(part.at[pl.ds(0, 16), :], r0_in.at[rows_of(mc), :], R0, along_ch(*d)).start()
    r0_in[rows_of(mc), :] = part[pl.ds(0, 16), :]

    hear(1)
    tell(2)

    @pl.when(mc > 0)
    def _():
        rs_in[rows_of(mc), :] = part[rows_of(mc), :]
        drain(rs_in.at[pl.ds(0, TOK - 16), :], recv_sem.at[RS])
        low, coeff = summed(rs_in)
        ag_out[:, pl.ds(0, RANK)] = low
        ag_out[:, pl.ds(RANK, LANES)] = coeff
        for d in far_ch:
            remote(ag_out, lr.at[rows_of(mc), :], AG, along_ch(*d)).start()
        lr[rows_of(mc), :] = ag_out[...]

    idx_ld.wait()
    own_ld.wait()
    kv_ld.wait()
    own_row = own_v[...]
    eye = iota((KEEP, KEEP), 0) == iota((KEEP, KEEP), 1)
    own = jnp.sum(jnp.where(eye, own_row, 0), axis=1, keepdims=True)
    same = (own_row == own) & (iota((KEEP, KEEP), 1) < iota((KEEP, KEEP), 0))
    rank = jnp.sum(jnp.where(same, 1, 0), axis=1, keepdims=True)
    place = (own & (NZ - 1)) * 16 + (own >> 4) * 2 + rank
    src_t = (iota((TOK, KEEP), 0) == idx_v[...] - me * TOK).astype(F32).astype(BF16)
    picked = dot_rows(src_t, kv_v[...]).astype(BF16)
    slots = iota((KEEP, 256), 1)
    kz = dot_rows((slots == place).astype(F32).astype(BF16), picked[:, :LANES])
    kz = kz + dot_rows((slots == place + 8).astype(F32).astype(BF16), picked[:, LANES:])
    kz_out[...] = kz.astype(BF16)

    dec_ld.wait()
    decs_ld.wait()
    gate_ld.wait()
    for j in range(TILES):
        rate = -LOG2E * jnp.exp(dec_v[:, pl.ds(j * LANES, LANES)])
        a2n[pl.ds(j * ST, ST), :] = rate
        a2b[pl.ds(j, ST, stride=TILES), :] = rate
    a2s = [-LOG2E * jnp.exp(decs_v[:, pl.ds(jj * LANES, LANES)]) for jj in range(2)]
    skip_ld.wait()
    for j in range(TILES):
        cols = pl.ds(j * LANES, LANES)
        sgb[pl.ds(j, TOK, stride=TILES), :] = silu(gate_v[:, cols].astype(F32))
        skip_b[pl.ds(j, 1), :] = skip_v[:, cols]

    hear(2)
    hear_x()
    for d in far_z:
        to = (mz + d) % NZ
        remote(kz_out.at[rows_of(to), :], kz_in.at[rows_of(mz), :], KZ, along_z(d)).start()
    kz_in[rows_of(mz), :] = kz_out[rows_of(mz), :]

    dtw_ld.wait()
    dtb_ld.wait()
    drain(r0_in.at[pl.ds(0, TOK - 16), :], recv_sem.at[R0])
    low, coeff = summed(r0_in)
    lr[pl.ds(0, 16), pl.ds(0, RANK)] = low
    lr[pl.ds(0, 16), pl.ds(RANK, LANES)] = coeff

    @pl.when(mc > 0)
    def _():
        drain(lr.at[pl.ds(0, TOK - 32), :], recv_sem.at[AG])

    @pl.when(mc == 0)
    def _():
        drain(lr.at[pl.ds(0, TOK - 16), :], recv_sem.at[AG])

    for j in range(TILES):
        cols = pl.ds(j * LANES, LANES)
        v = dot(lr[:, pl.ds(0, RANK)], dtw_v[:, cols]) + dtb_v[:, cols]
        v = jnp.maximum(v, 0.0) + jnp.log1p(jnp.exp(-jnp.abs(v)))
        dtb3[pl.ds(j, TOK, stride=TILES), :] = v
        s_out[j] = jnp.sum(v, axis=0, keepdims=True)
    coeff = lr[:, pl.ds(RANK, LANES)]

    def spread(i):
        rows = (iota((LANES, 4 * LANES), 1) >> 7) + 4 * i == iota((LANES, 4 * LANES), 0)
        wide = dot(coeff, rows.astype(F32).astype(BF16))
        bcx[:, :, pl.ds(i * 4 * LANES, 4 * LANES)] = wide.reshape(TOK // 8, 8, 4 * LANES)

    for i in range(4):
        spread(i)

    def token(g, u):
        return pl.ds(pl.multiple_of(g * 64, 64) + u * 8, 8)

    for d in far_z:
        to = (mz + d) % 4
        remote(s_out.at[pl.ds(2 * to, 2)], s_in.at[mz], SZ, along_z(d)).start()
    s_in[mz] = s_out[pl.ds(2 * mq, 2)]

    def end_step(g, state):
        state = list(state)
        for u in range(8):
            dt = dtb3[token(g, u), :]
            dx = dt * xb3[token(g, u), :]
            for n in range(ST):
                b = bcx[g, pl.ds(u, 1), pl.ds(n * LANES, LANES)]
                state[n] = jnp.exp2(dt * a2b[pl.ds(n * 8, 8), :]) * state[n] + dx * b
        return tuple(state)

    empty = tuple(jnp.zeros((TILES, LANES), F32) for _ in range(ST))
    state = lax.fori_loop(0, TOK // 8, end_step, empty)
    for n in range(ST):
        lb[pl.ds(n * 8, 8), :] = state[n]
    for j in range(TILES):
        l_out[pl.ds(j * ST, ST), :] = lb[pl.ds(j, ST, stride=TILES), :].astype(BF16)

    def block_of(i):
        return pl.ds(pl.multiple_of(i * 32, 32), 32)

    for d in far_z:
        to = (mz + d) % 4
        remote(l_out.at[block_of(to), :], l_in.at[block_of(mz), :], LZ, along_z(d)).start()
    l_in[block_of(mz), :] = l_out[block_of(mq), :]

    for i in range(4, 8):
        spread(i)

    def scan_step(g, state):
        state = list(state)
        for u in range(8):
            dt = dtb3[token(g, u), :]
            xt = xb3[token(g, u), :]
            dx = dt * xt
            y = [skip_b[...] * xt, None, None, None]
            for n in range(ST):
                b = bcx[g, pl.ds(u, 1), pl.ds(n * LANES, LANES)]
                c = bcx[g, pl.ds(u, 1), pl.ds((ST + n) * LANES, LANES)]
                state[n] = jnp.exp2(dt * a2b[pl.ds(n * 8, 8), :]) * state[n] + dx * b
                term = c * state[n]
                y[n % 4] = term if y[n % 4] is None else y[n % 4] + term
            yb[token(g, u), :] = ((y[0] + y[1]) + (y[2] + y[3])) * sgb[token(g, u), :]
        return tuple(state)

    lax.fori_loop(0, TOK // 8, scan_step, empty)

    def reach_step(g, cum):
        for u in range(8):
            cum = cum + dtb3[token(g, u), :]
            sgt = sgb[token(g, u), :]
            for n in range(ST):
                c = bcx[g, pl.ds(u, 1), pl.ds((ST + n) * LANES, LANES)]
                gb[pl.ds(pl.multiple_of(g * 1024, 1024) + u * 128 + n * 8, 8), :] = (c * sgt) * jnp.exp2(cum * a2b[pl.ds(n * 8, 8), :])
        return cum

    lax.fori_loop(0, TOK // 8, reach_step, jnp.zeros((TILES, LANES), F32))

    drain(kz_in.at[pl.ds(0, 240), :], recv_sem.at[KZ])
    row = iota((TOK, 256), 0)
    want = ((row >> 1) & (NZ - 1)) * 16 + (row >> 5) * 2 + (row & 1)
    for half in range(2):
        sel = (iota((TOK, 256), 1) == want + half * 8).astype(F32).astype(BF16)
        kx_out[:, pl.ds(half * LANES, LANES)] = dot(sel, kz_in[...]).astype(BF16)

    for d in far_x:
        to = (mx + d) % NX
        remote(kx_out.at[block_of(to), :], kx_in.at[block_of(mx), :], KX, along_x(d)).start()
    kx_in[block_of(mx), :] = kx_out[block_of(mx), :]

    drain(s_in.at[pl.ds(0, NZ - 1)], recv_sem.at[SZ])
    for jj in range(2):
        run = jnp.zeros((1, LANES), F32)
        for z in range(NZ):
            decay[pl.ds(z * 32 + jj * ST, ST), :] = jnp.exp2(a2s[jj] * s_in[z, jj])
            cum_out[z, jj] = run
            run = run + s_in[z, jj]
        sx_out[jj] = run

    def pair_of(i):
        return pl.ds(2 * i, 2)

    def to_planes(src, dst, k):
        for dx in (3, 2, 1):

            @pl.when(mx + dx < NX)
            def _():
                for dz in (-2, -1, 1, 0):
                    pltpu.make_async_remote_copy(
                        src_ref=src, dst_ref=dst, send_sem=send_sem.at[k + dx - 1], recv_sem=recv_sem.at[k + mx],
                        device_id=along_xz(dx, dz),
                    ).start()

    @pl.when(mx < NX - 1)
    def _():
        to_planes(sx_out, sx_in.at[mx, pair_of(mq)], CX)

    for dz in (-2, -1, 1):
        remote(cum_out.at[(mz + dz + NZ) % NZ], cum_in.at[pair_of(mq)], CZ, along_z(dz)).start()
    cum_in[pair_of(mq)] = cum_out[mz]

    drain(l_in.at[pl.ds(0, 480), :], recv_sem.at[LZ])
    for jj in range(2):
        carry = jnp.zeros((ST, LANES), F32)
        for z in range(NZ):
            rows = pl.ds(z * 32 + jj * ST, ST)
            before[rows, :] = carry.astype(BF16)
            carry = decay[rows, :] * carry + l_in[rows, :].astype(F32)
        t_out[pl.ds(jj * ST, ST), :] = carry.astype(BF16)

    @pl.when(mx < NX - 1)
    def _():
        to_planes(t_out, t_in.at[mx, block_of(mq)], TX)

    for dz in (-2, -1, 1):
        remote(before.at[block_of((mz + dz + NZ) % NZ), :], h_in.at[block_of(mq), :], HZ, along_z(dz)).start()
    h_in[block_of(mq), :] = before[block_of(mz), :]

    carry_x[...] = jnp.zeros_like(carry_x)
    for i in range(NX - 1):

        @pl.when(i < mx)
        def _():
            drain(sx_in.at[i], recv_sem.at[CX + i])
            for j in range(TILES):
                rows = pl.ds(j * ST, ST)
                plane[pl.ds(i * 128 + j * ST, ST), :] = jnp.exp2(a2n[rows, :] * sx_in[i, j])

    drain(cum_in.at[pl.ds(0, 6)], recv_sem.at[CZ])
    for j in range(TILES):
        rows = pl.ds(j * ST, ST)
        reach[rows, :] = jnp.exp2(a2n[rows, :] * cum_in[j])
    for i in range(NX - 1):

        @pl.when(i < mx)
        def _():
            drain(t_in.at[i], recv_sem.at[TX + i])
            carry_x[...] = plane[pl.ds(i * 128, 128), :] * carry_x[...] + t_in[i].astype(F32)

    drain(h_in.at[pl.ds(0, 96), :], recv_sem.at[HZ])
    hf[...] = h_in[...].astype(F32) + reach[...] * carry_x[...]

    drain(kx_in.at[pl.ds(0, 96), :], recv_sem.at[KX])

    drain(halo, send_sem.at[HALO])
    drain(r0_in.at[pl.ds(0, TOK - 16), :], send_sem.at[R0])

    @pl.when(mc > 0)
    def _():
        drain(rs_in.at[pl.ds(0, TOK - 32), :], send_sem.at[RS])
        drain(lr.at[pl.ds(0, TOK - 16), :], send_sem.at[AG])

    @pl.when(mc == 0)
    def _():
        drain(rs_in.at[pl.ds(0, TOK - 16), :], send_sem.at[RS])

    drain(kz_in.at[pl.ds(0, 240), :], send_sem.at[KZ])
    drain(kx_in.at[pl.ds(0, 96), :], send_sem.at[KX])
    drain(s_in.at[pl.ds(0, NZ - 1)], send_sem.at[SZ])
    drain(l_in.at[pl.ds(0, 480), :], send_sem.at[LZ])
    for dx in (1, 2, 3):

        @pl.when(mx + dx < NX)
        def _():
            drain(sx_in.at[0], send_sem.at[CX + dx - 1])
            drain(t_in.at[0], send_sem.at[TX + dx - 1])

    drain(cum_in.at[pl.ds(0, 6)], send_sem.at[CZ])
    drain(h_in.at[pl.ds(0, 96), :], send_sem.at[HZ])


def finish(gb, yb, hf, kept, gated_hbm, kept_hbm, ys, gated_v, sem):
    kept_copy = pltpu.make_async_copy(kept, kept_hbm.at[0], sem.at[PARTS])
    kept_copy.start()
    carried = [hf[pl.ds(n, TILES, stride=ST), :] for n in range(ST)]
    rows = TOK // PARTS
    copies = []
    for part in range(PARTS):

        def add_step(g, _):
            for u in range(8):
                at = pl.ds(pl.multiple_of(g * 64, 64) + u * 8, 8)
                y = [yb[at, :], None, None, None]
                for n in range(ST):
                    term = gb[pl.ds(pl.multiple_of(g * 1024, 1024) + u * 128 + n * 8, 8), :] * carried[n]
                    y[n % 4] = term if y[n % 4] is None else y[n % 4] + term
                ys[at, :] = (y[0] + y[1]) + (y[2] + y[3])
            return 0

        lax.fori_loop(part * rows // 8, (part + 1) * rows // 8, add_step, 0)
        here = pl.ds(part * rows, rows)
        for j in range(TILES):
            y = ys[pl.ds(part * rows * TILES + j, rows, stride=TILES), :]
            gated_v[here, pl.ds(j * LANES, LANES)] = y.astype(BF16)
        copies.append(pltpu.make_async_copy(gated_v.at[here, :], gated_hbm.at[here, :], sem.at[part]))
        copies[-1].start()
    for c in copies:
        c.wait()
    kept_copy.wait()


def local(
    x_in, gate_in, conv_weight, conv_bias, proj_low, proj_bc, dt_weight, dt_bias, decay_log, skip_gain, attn_kv,
    kept_index, kept_owner,
):
    V = pltpu.VMEM
    hbm = pl.BlockSpec(memory_space=pltpu.HBM)
    vmem = pl.BlockSpec(memory_space=pltpu.VMEM)
    pin = functools.partial(pltpu.with_memory_space_constraint, memory_space=pltpu.HBM)
    parts = pl.pallas_call(
        kernel,
        out_shape=(
            V((TOK * ST * TILES, LANES), F32), V((TOK * TILES, LANES), F32), V((128, LANES), F32), V((TOK, 2 * LANES), BF16),
        ),
        in_specs=[hbm] * 13,
        out_specs=(vmem,) * 4,
        scratch_shapes=[
            V((TOK, CH), BF16), V((TOK, CH), BF16), V((CONV, CH), F32), V((1, CH), F32), V((CH, RANK), BF16),
            V((LANES, CH), BF16), V((RANK, CH), BF16), V((1, CH), F32), V((ST, CH), F32), V((1, CH), F32),
            V((TOK, 2 * LANES), BF16), V((1, KEEP), jnp.int32), V((1, KEEP), jnp.int32), V((ST, 2 * LANES), F32),
            V((32, LANES), BF16), V((32, LANES), BF16), V((32, LANES), F32), V((TOK + 16, CH), F32), V((TOK, CH), BF16),
            V((TOK, RANK + LANES), BF16), V((TOK, RANK + LANES), BF16), V((TOK, RANK + LANES), BF16), V((16, RANK + LANES), BF16), V((TOK, RANK + LANES), BF16),
            V((TOK * TILES, LANES), F32), V((TOK * TILES, LANES), F32), V((TOK // 8, 8, 2 * ST * LANES), F32),
            V((ST * TILES, LANES), F32), V((ST * TILES, LANES), F32), V((ST * TILES, LANES), F32),
            V((TOK * TILES, LANES), F32), V((TILES, LANES), F32),
            V((TILES, 1, LANES), F32), V((NZ, 2, 1, LANES), F32), V((ST * TILES, LANES), BF16), V((NZ * 32, LANES), BF16),
            V((2, 1, LANES), F32), V((NX - 1, TILES, 1, LANES), F32), V((NZ, 2, 1, LANES), F32), V((TILES, 1, LANES), F32),
            V((32, LANES), BF16), V((NX - 1, 128, LANES), BF16), V((NZ * 32, LANES), BF16), V((128, LANES), BF16),
            V((NZ * 32, LANES), F32), V((128, LANES), F32), V(((NX - 1) * 128, LANES), F32),
            V((128, LANES), F32),
            V((256, LANES), BF16), V((256, LANES), BF16), V((TOK, 2 * LANES), BF16),
            pltpu.SemaphoreType.DMA((15,)),
            pltpu.SemaphoreType.DMA((16,)), pltpu.SemaphoreType.DMA((16,)),
            pltpu.SemaphoreType.REGULAR((4,)),
        ],
        compiler_params=pltpu.CompilerParams(
            collective_id=0, has_side_effects=True, vmem_limit_bytes=40_000_000
        ),
    )(*map(pin, (
        x_in, gate_in, conv_weight, conv_bias.reshape(1, CH), proj_low, proj_bc.T, dt_weight, dt_bias.reshape(1, CH),
        decay_log, skip_gain.reshape(1, CH), attn_kv, kept_index, kept_owner.reshape(1, KEEP),
    )))
    return pl.pallas_call(
        finish,
        out_shape=(jax.ShapeDtypeStruct((TOK, CH), BF16), jax.ShapeDtypeStruct((1, TOK, 2 * LANES), BF16)),
        in_specs=[vmem] * 4,
        out_specs=(hbm, hbm),
        scratch_shapes=[
            V((TOK * TILES, LANES), F32), V((TOK, CH), BF16), pltpu.SemaphoreType.DMA((PARTS + 1,)),
        ],
        compiler_params=pltpu.CompilerParams(vmem_limit_bytes=20_000_000),
    )(*parts)


def solution(mesh):
    return jax.shard_map(
        local,
        mesh=mesh,
        in_specs=(
            P("ctx", "ch"), P("ctx", "ch"), P(None, "ch"), P("ch"), P("ch", None), P("ch", None), P(None, "ch"),
            P("ch"), P(None, "ch"), P("ch"), P("ctx", "ch"), P("ch", "ctx"), P("ch", "ctx", None),
        ),
        out_specs=(P("ctx", "ch"), P("ch", "ctx", None)),
        check_vma=False,
    )
```

```python
import functools
import math

import jax
import jax.numpy as jnp
from jax import lax
from jax.experimental import pallas as pl
from jax.experimental.pallas import tpu as pltpu
from jax.sharding import PartitionSpec as P

MOST = 2
PARTS = 4
NZ = 16
NX = 4
NC = 8
TOK = 128
CH = 1024
ST = 16
CONV = 4
RANK = 256
LANES = 128
TILES = CH // LANES
KEEP = 32
F32 = jnp.float32
BF16 = jnp.bfloat16
LOG2E = math.log2(math.e)


def dot(a, b):
    return jnp.dot(a, b, preferred_element_type=F32)


def dot_rows(a, b):
    return lax.dot_general(a, b, (((0,), (0,)), ((), ())), preferred_element_type=F32)


def silu(v):
    return v / (1.0 + jnp.exp(-v))


def iota(shape, dim):
    return lax.broadcasted_iota(jnp.int32, shape, dim)


def kernel(
    x_hbm, gate_hbm, cw_hbm, cb_hbm, low_hbm, bc_hbm, dtw_hbm, dtb_hbm, dec_hbm, skip_hbm, kv_hbm, idx_hbm, own_hbm,
    gb, yb, hf, kept_out,
    x_v, gate_v, cw_v, cb_v, low_v, bc_v, dtw_v, dtb_v, dec_v, skip_v, kv_v, idx_v, own_v, decs_v,
    halo, halo_out, halo_f, xs, act, part, rs_in, r0_in, ag_out, lr, dtb3, xb3, bcx, a2b, a2n, lb, sgb, skip_b,
    s_out, s_in, l_out, l_in, sx_out, sx_in, cum_out, cum_in, t_out, t_in, before, h_in, decay, reach,
    plane, carry_x,
    kz_out, kz_in, kx_out,
    in_sem, send_sem, recv_sem, here_sem,
):
    kx_in = kept_out
    me = lax.axis_index("ctx")
    mc = lax.axis_index("ch")
    mx = me // NZ
    mz = me % NZ
    mq = mz % 4

    loads = [
        (x_hbm, x_v), (cw_hbm, cw_v), (cb_hbm, cb_v), (idx_hbm, idx_v), (own_hbm, own_v), (kv_hbm, kv_v),
        (low_hbm, low_v), (bc_hbm, bc_v.at[pl.ds(0, 2 * ST), :]), (bc_hbm, bc_v.at[pl.ds(2 * ST, 2 * ST), :]),
        (dec_hbm, dec_v),
        (dec_hbm.at[:, pl.ds(pl.multiple_of(mq * 2 * LANES, 2 * LANES), 2 * LANES)], decs_v),
        (dtw_hbm, dtw_v), (dtb_hbm, dtb_v), (skip_hbm, skip_v), (gate_hbm, gate_v),
    ]
    loads = [pltpu.make_async_copy(s, d, in_sem.at[i]) for i, (s, d) in enumerate(loads)]
    (x_ld, cw_ld, cb_ld, idx_ld, own_ld, kv_ld, low_ld, bc_ld, bc2_ld, dec_ld, decs_ld, dtw_ld, dtb_ld, skip_ld, gate_ld) = loads

    for c in loads[:3]:
        c.start()

    def along_z(d):
        return {"ctx": mx * NZ + (mz + d + NZ) % NZ}

    def along_x(d):
        return {"ctx": ((mx + d) % NX) * NZ + mz}

    def along_xz(dx, dz):
        return {"ctx": ((mx + dx) % NX) * NZ + (mz + dz + NZ) % NZ}

    def along_ch(dy, dc):
        return {"ch": ((mc // 2 + dy) % (NC // 2)) * 2 + (mc + dc) % 2}

    far_z = (8, 7, 9, 6, 10, 5, 11, 4, 12, 3, 13, 2, 14, 1, 15)
    far_x = (2, 1, 3)
    far_ch = ((2, 0), (2, 1), (1, 0), (3, 0), (1, 1), (3, 1), (0, 1))
    right = {"ctx": (me + 1) % (NX * NZ)}
    left = {"ctx": (me + NX * NZ - 1) % (NX * NZ)}
    barrier = pltpu.get_barrier_semaphore()
    for d in far_ch:
        pl.semaphore_signal(barrier, inc=1, device_id=along_ch(*d))
    for d in (-1, 1):
        pl.semaphore_signal(barrier, inc=1, device_id=along_z(d))
    for d in far_x:
        pl.semaphore_signal(barrier, inc=1, device_id=along_x(d))

    @pl.when(mz == NZ - 1)
    def _():
        pl.semaphore_signal(barrier, inc=1, device_id=right)

    @pl.when(mz == 0)
    def _():
        pl.semaphore_signal(barrier, inc=1, device_id=left)

    for c in loads[3:]:
        c.start()

    def tell(i):
        for d in (-(1 << i), 1 << i):
            pl.semaphore_signal(here_sem.at[i], inc=1, device_id=along_z(d))

    def hear(i):
        pl.semaphore_wait(here_sem.at[i], 2)

    def tell_x():
        for d in far_x:
            pl.semaphore_signal(here_sem.at[3], inc=1, device_id=along_x(d))

    def hear_x():
        pl.semaphore_wait(here_sem.at[3], NX - 1)

    def remote(src, dst, k, peer):
        return pltpu.make_async_remote_copy(
            src_ref=src, dst_ref=dst, send_sem=send_sem.at[k], recv_sem=recv_sem.at[k], device_id=peer
        )

    def drain(ref, sem):
        pltpu.make_async_copy(ref, ref, sem).wait()

    HALO, RS, AG, KZ, KX, SZ, LZ, CZ, HZ, R0, CX, TX = (0, 1, 2, 3, 4, 5, 6, 7, 8, 9, 10, 13)

    bc_v[pl.ds(4 * ST, LANES - 4 * ST), :] = jnp.zeros((LANES - 4 * ST, CH), BF16)

    x_ld.wait()
    for j in range(TILES):
        halo_f[pl.ds(4 * j, 4), :] = x_v[pl.ds(TOK - 16, 16), pl.ds(j * LANES, LANES)].astype(F32)[12:, :]
    halo_out[...] = halo_f[...].astype(BF16)
    def conv(first, rows):
        for j in range(TILES):
            cols = pl.ds(j * LANES, LANES)
            s = jnp.broadcast_to(cb_v[:, cols], (rows, LANES))
            for k in range(CONV):
                s = s + cw_v[pl.ds(k, 1), cols] * xs[pl.ds(first + 16 - (CONV - 1) + k, rows), cols]
            a = silu(s).astype(BF16)
            act[pl.ds(first, rows), cols] = a
            xb3[pl.ds(first * TILES + j, rows, stride=TILES), :] = a.astype(F32)

    def project(first, rows):
        a = act[pl.ds(first, rows), :]
        part[pl.ds(first, rows), pl.ds(0, RANK)] = dot(a, low_v[...]).astype(BF16)
        wide = lax.dot_general(a, bc_v[...], (((1,), (1,)), ((), ())), preferred_element_type=F32)
        high = wide.astype(BF16).astype(F32)
        low = jnp.where(iota((rows, LANES), 1) < 2 * ST, high, wide - high)
        part[pl.ds(first, rows), pl.ds(RANK, LANES)] = low.astype(BF16)

    def summed(ref):
        total = ref[pl.ds(0, 16), :].astype(F32)
        for i in range(1, NC):
            total = total + ref[pl.ds(16 * i, 16), :].astype(F32)
        wide = total[:, RANK:]
        return total[:, :RANK].astype(BF16), (wide + pltpu.roll(wide, LANES - 2 * ST, 1)).astype(BF16)

    def rows_of(i):
        return pl.ds(pl.multiple_of(i * 16, 16), 16)

    cw_ld.wait()
    cb_ld.wait()
    xs[pl.ds(16, TOK), :] = x_v[...].astype(F32)
    conv(16, TOK - 16)
    low_ld.wait()
    bc_ld.wait()
    bc2_ld.wait()
    project(16, TOK - 16)

    pl.semaphore_wait(barrier, NC - 1 + NX - 1 + 2 + jnp.where((mz == 0) | (mz == NZ - 1), 1, 0))

    remote(halo_out, halo, HALO, right).start()
    tell(0)

    for d in far_ch:
        to = along_ch(*d)

        @pl.when(to["ch"] > 0)
        def _():
            remote(part.at[rows_of(to["ch"]), :], rs_in.at[rows_of(mc), :], RS, to).start()

    hear(0)
    tell(1)
    tell_x()
    drain(halo, recv_sem.at[HALO])
    halo_f[...] = halo[...].astype(F32)
    for j in range(TILES):
        xs[pl.ds(12, 4), pl.ds(j * LANES, LANES)] = jnp.where(me > 0, halo_f[pl.ds(4 * j, 4), :], 0.0)
    conv(0, 16)
    project(0, 16)
    for d in far_ch:
        remote(part.at[pl.ds(0, 16), :], r0_in.at[rows_of(mc), :], R0, along_ch(*d)).start()
    r0_in[rows_of(mc), :] = part[pl.ds(0, 16), :]

    idx_ld.wait()
    own_ld.wait()
    kv_ld.wait()
    own_row = own_v[...]
    eye = iota((KEEP, KEEP), 0) == iota((KEEP, KEEP), 1)
    own = jnp.sum(jnp.where(eye, own_row, 0), axis=1, keepdims=True)
    same = (own_row == own) & (iota((KEEP, KEEP), 1) < iota((KEEP, KEEP), 0))
    rank = jnp.sum(jnp.where(same, 1, 0), axis=1, keepdims=True)
    place = (own & (NZ - 1)) * 16 + (own >> 4) * 2 + rank
    src_t = (iota((TOK, KEEP), 0) == idx_v[...] - me * TOK).astype(F32).astype(BF16)
    picked = dot_rows(src_t, kv_v[...]).astype(BF16)
    slots = iota((KEEP, 256), 1)
    kz = dot_rows((slots == place).astype(F32).astype(BF16), picked[:, :LANES])
    kz = kz + dot_rows((slots == place + 8).astype(F32).astype(BF16), picked[:, LANES:])
    kz_out[...] = kz.astype(BF16)

    hear(1)
    tell(2)

    dec_ld.wait()
    decs_ld.wait()
    gate_ld.wait()
    for j in range(TILES):
        rate = -LOG2E * jnp.exp(dec_v[:, pl.ds(j * LANES, LANES)])
        a2n[pl.ds(j * ST, ST), :] = rate
        a2b[pl.ds(j, ST, stride=TILES), :] = rate
    a2s = [-LOG2E * jnp.exp(decs_v[:, pl.ds(jj * LANES, LANES)]) for jj in range(2)]
    skip_ld.wait()
    for j in range(TILES):
        cols = pl.ds(j * LANES, LANES)
        sgb[pl.ds(j, TOK, stride=TILES), :] = silu(gate_v[:, cols].astype(F32))
        skip_b[pl.ds(j, 1), :] = skip_v[:, cols]

    @pl.when(mc > 0)
    def _():
        rs_in[rows_of(mc), :] = part[rows_of(mc), :]
        drain(rs_in.at[pl.ds(0, TOK - 16), :], recv_sem.at[RS])
        low, coeff = summed(rs_in)
        ag_out[:, pl.ds(0, RANK)] = low
        ag_out[:, pl.ds(RANK, LANES)] = coeff
        for d in far_ch:
            remote(ag_out, lr.at[rows_of(mc), :], AG, along_ch(*d)).start()
        lr[rows_of(mc), :] = ag_out[...]

    hear(2)
    hear_x()
    for d in far_z:
        to = (mz + d) % NZ
        remote(kz_out.at[rows_of(to), :], kz_in.at[rows_of(mz), :], KZ, along_z(d)).start()
    kz_in[rows_of(mz), :] = kz_out[rows_of(mz), :]

    dtw_ld.wait()
    dtb_ld.wait()
    drain(r0_in.at[pl.ds(0, TOK - 16), :], recv_sem.at[R0])
    low, coeff = summed(r0_in)
    lr[pl.ds(0, 16), pl.ds(0, RANK)] = low
    lr[pl.ds(0, 16), pl.ds(RANK, LANES)] = coeff

    @pl.when(mc > 0)
    def _():
        drain(lr.at[pl.ds(0, TOK - 32), :], recv_sem.at[AG])

    @pl.when(mc == 0)
    def _():
        drain(lr.at[pl.ds(0, TOK - 16), :], recv_sem.at[AG])

    for j in range(TILES):
        cols = pl.ds(j * LANES, LANES)
        v = dot(lr[:, pl.ds(0, RANK)], dtw_v[:, cols]) + dtb_v[:, cols]
        v = jnp.maximum(v, 0.0) + jnp.log1p(jnp.exp(-jnp.abs(v)))
        dtb3[pl.ds(j, TOK, stride=TILES), :] = v
        s_out[j] = jnp.sum(v, axis=0, keepdims=True)
    coeff = lr[:, pl.ds(RANK, LANES)]

    def spread(i):
        rows = (iota((LANES, 4 * LANES), 1) >> 7) + 4 * i == iota((LANES, 4 * LANES), 0)
        wide = dot(coeff, rows.astype(F32).astype(BF16))
        bcx[:, :, pl.ds(i * 4 * LANES, 4 * LANES)] = wide.reshape(TOK // 8, 8, 4 * LANES)

    for i in range(4):
        spread(i)

    def token(g, u):
        return pl.ds(pl.multiple_of(g * 64, 64) + u * 8, 8)

    for d in far_z:
        to = (mz + d) % 4
        remote(s_out.at[pl.ds(2 * to, 2)], s_in.at[mz], SZ, along_z(d)).start()
    s_in[mz] = s_out[pl.ds(2 * mq, 2)]

    def end_step(g, state):
        state = list(state)
        for u in range(8):
            dt = dtb3[token(g, u), :]
            dx = dt * xb3[token(g, u), :]
            for n in range(ST):
                b = bcx[g, pl.ds(u, 1), pl.ds(n * LANES, LANES)]
                state[n] = jnp.exp2(dt * a2b[pl.ds(n * 8, 8), :]) * state[n] + dx * b
        return tuple(state)

    empty = tuple(jnp.zeros((TILES, LANES), F32) for _ in range(ST))
    state = lax.fori_loop(0, TOK // 8, end_step, empty)
    for n in range(ST):
        lb[pl.ds(n * 8, 8), :] = state[n]
    for j in range(TILES):
        l_out[pl.ds(j * ST, ST), :] = lb[pl.ds(j, ST, stride=TILES), :].astype(BF16)

    def block_of(i):
        return pl.ds(pl.multiple_of(i * 32, 32), 32)

    for d in far_z:
        to = (mz + d) % 4
        remote(l_out.at[block_of(to), :], l_in.at[block_of(mz), :], LZ, along_z(d)).start()
    l_in[block_of(mz), :] = l_out[block_of(mq), :]

    for i in range(4, 8):
        spread(i)

    def scan_step(g, state):
        state = list(state)
        for u in range(8):
            dt = dtb3[token(g, u), :]
            xt = xb3[token(g, u), :]
            dx = dt * xt
            y = [skip_b[...] * xt, None, None, None]
            for n in range(ST):
                b = bcx[g, pl.ds(u, 1), pl.ds(n * LANES, LANES)]
                c = bcx[g, pl.ds(u, 1), pl.ds((ST + n) * LANES, LANES)]
                state[n] = jnp.exp2(dt * a2b[pl.ds(n * 8, 8), :]) * state[n] + dx * b
                term = c * state[n]
                y[n % 4] = term if y[n % 4] is None else y[n % 4] + term
            yb[token(g, u), :] = ((y[0] + y[1]) + (y[2] + y[3])) * sgb[token(g, u), :]
        return tuple(state)

    lax.fori_loop(0, TOK // 8, scan_step, empty)

    def reach_step(g, cum):
        for u in range(8):
            cum = cum + dtb3[token(g, u), :]
            sgt = sgb[token(g, u), :]
            for n in range(ST):
                c = bcx[g, pl.ds(u, 1), pl.ds((ST + n) * LANES, LANES)]
                gb[pl.ds(pl.multiple_of(g * 1024, 1024) + u * 128 + n * 8, 8), :] = (c * sgt) * jnp.exp2(cum * a2b[pl.ds(n * 8, 8), :])
        return cum

    lax.fori_loop(0, TOK // 8, reach_step, jnp.zeros((TILES, LANES), F32))

    drain(kz_in.at[pl.ds(0, 240), :], recv_sem.at[KZ])
    row = iota((TOK, 256), 0)
    want = ((row >> 1) & (NZ - 1)) * 16 + (row >> 5) * 2 + (row & 1)
    for half in range(2):
        sel = (iota((TOK, 256), 1) == want + half * 8).astype(F32).astype(BF16)
        kx_out[:, pl.ds(half * LANES, LANES)] = dot(sel, kz_in[...]).astype(BF16)

    for d in far_x:
        to = (mx + d) % NX
        remote(kx_out.at[block_of(to), :], kx_in.at[block_of(mx), :], KX, along_x(d)).start()
    kx_in[block_of(mx), :] = kx_out[block_of(mx), :]

    drain(s_in.at[pl.ds(0, NZ - 1)], recv_sem.at[SZ])
    for jj in range(2):
        run = jnp.zeros((1, LANES), F32)
        for z in range(NZ):
            decay[pl.ds(z * 32 + jj * ST, ST), :] = jnp.exp2(a2s[jj] * s_in[z, jj])
            cum_out[z, jj] = run
            run = run + s_in[z, jj]
        sx_out[jj] = run

    def pair_of(i):
        return pl.ds(2 * i, 2)

    def to_planes(src, dst, k):
        for dx in (3, 2, 1):

            @pl.when(mx + dx < NX)
            def _():
                for dz in (-2, -1, 1, 0):
                    pltpu.make_async_remote_copy(
                        src_ref=src, dst_ref=dst, send_sem=send_sem.at[k + dx - 1], recv_sem=recv_sem.at[k + mx],
                        device_id=along_xz(dx, dz),
                    ).start()

    @pl.when(mx < NX - 1)
    def _():
        to_planes(sx_out, sx_in.at[mx, pair_of(mq)], CX)

    for dz in (-2, -1, 1):
        remote(cum_out.at[(mz + dz + NZ) % NZ], cum_in.at[pair_of(mq)], CZ, along_z(dz)).start()
    cum_in[pair_of(mq)] = cum_out[mz]

    drain(l_in.at[pl.ds(0, 480), :], recv_sem.at[LZ])
    for jj in range(2):
        carry = jnp.zeros((ST, LANES), F32)
        for z in range(NZ):
            rows = pl.ds(z * 32 + jj * ST, ST)
            before[rows, :] = carry.astype(BF16)
            carry = decay[rows, :] * carry + l_in[rows, :].astype(F32)
        t_out[pl.ds(jj * ST, ST), :] = carry.astype(BF16)

    @pl.when(mx < NX - 1)
    def _():
        to_planes(t_out, t_in.at[mx, block_of(mq)], TX)

    for dz in (-2, -1, 1):
        remote(before.at[block_of((mz + dz + NZ) % NZ), :], h_in.at[block_of(mq), :], HZ, along_z(dz)).start()
    h_in[block_of(mq), :] = before[block_of(mz), :]

    carry_x[...] = jnp.zeros_like(carry_x)
    for i in range(NX - 1):

        @pl.when(i < mx)
        def _():
            drain(sx_in.at[i], recv_sem.at[CX + i])
            for j in range(TILES):
                rows = pl.ds(j * ST, ST)
                plane[pl.ds(i * 128 + j * ST, ST), :] = jnp.exp2(a2n[rows, :] * sx_in[i, j])

    drain(cum_in.at[pl.ds(0, 6)], recv_sem.at[CZ])
    for j in range(TILES):
        rows = pl.ds(j * ST, ST)
        reach[rows, :] = jnp.exp2(a2n[rows, :] * cum_in[j])
    for i in range(NX - 1):

        @pl.when(i < mx)
        def _():
            drain(t_in.at[i], recv_sem.at[TX + i])
            carry_x[...] = plane[pl.ds(i * 128, 128), :] * carry_x[...] + t_in[i].astype(F32)

    drain(h_in.at[pl.ds(0, 96), :], recv_sem.at[HZ])
    hf[...] = h_in[...].astype(F32) + reach[...] * carry_x[...]

    drain(kx_in.at[pl.ds(0, 96), :], recv_sem.at[KX])

    drain(halo, send_sem.at[HALO])
    drain(r0_in.at[pl.ds(0, TOK - 16), :], send_sem.at[R0])

    @pl.when(mc > 0)
    def _():
        drain(rs_in.at[pl.ds(0, TOK - 32), :], send_sem.at[RS])
        drain(lr.at[pl.ds(0, TOK - 16), :], send_sem.at[AG])

    @pl.when(mc == 0)
    def _():
        drain(rs_in.at[pl.ds(0, TOK - 16), :], send_sem.at[RS])

    drain(kz_in.at[pl.ds(0, 240), :], send_sem.at[KZ])
    drain(kx_in.at[pl.ds(0, 96), :], send_sem.at[KX])
    drain(s_in.at[pl.ds(0, NZ - 1)], send_sem.at[SZ])
    drain(l_in.at[pl.ds(0, 480), :], send_sem.at[LZ])
    for dx in (1, 2, 3):

        @pl.when(mx + dx < NX)
        def _():
            drain(sx_in.at[0], send_sem.at[CX + dx - 1])
            drain(t_in.at[0], send_sem.at[TX + dx - 1])

    drain(cum_in.at[pl.ds(0, 6)], send_sem.at[CZ])
    drain(h_in.at[pl.ds(0, 96), :], send_sem.at[HZ])


def finish(gb, yb, hf, kept, gated_hbm, kept_hbm, ys, gated_v, sem):
    kept_copy = pltpu.make_async_copy(kept, kept_hbm.at[0], sem.at[PARTS])
    kept_copy.start()
    carried = [hf[pl.ds(n, TILES, stride=ST), :] for n in range(ST)]
    rows = TOK // PARTS
    copies = []
    for part in range(PARTS):

        def add_step(g, _):
            for u in range(8):
                at = pl.ds(pl.multiple_of(g * 64, 64) + u * 8, 8)
                y = [yb[at, :], None, None, None]
                for n in range(ST):
                    term = gb[pl.ds(pl.multiple_of(g * 1024, 1024) + u * 128 + n * 8, 8), :] * carried[n]
                    y[n % 4] = term if y[n % 4] is None else y[n % 4] + term
                ys[at, :] = (y[0] + y[1]) + (y[2] + y[3])
            return 0

        lax.fori_loop(part * rows // 8, (part + 1) * rows // 8, add_step, 0)
        here = pl.ds(part * rows, rows)
        for j in range(TILES):
            y = ys[pl.ds(part * rows * TILES + j, rows, stride=TILES), :]
            gated_v[here, pl.ds(j * LANES, LANES)] = y.astype(BF16)
        copies.append(pltpu.make_async_copy(gated_v.at[here, :], gated_hbm.at[here, :], sem.at[part]))
        copies[-1].start()
    for c in copies:
        c.wait()
    kept_copy.wait()


def local(
    x_in, gate_in, conv_weight, conv_bias, proj_low, proj_bc, dt_weight, dt_bias, decay_log, skip_gain, attn_kv,
    kept_index, kept_owner,
):
    V = pltpu.VMEM
    hbm = pl.BlockSpec(memory_space=pltpu.HBM)
    vmem = pl.BlockSpec(memory_space=pltpu.VMEM)
    pin = functools.partial(pltpu.with_memory_space_constraint, memory_space=pltpu.HBM)
    parts = pl.pallas_call(
        kernel,
        out_shape=(
            V((TOK * ST * TILES, LANES), F32), V((TOK * TILES, LANES), F32), V((128, LANES), F32), V((TOK, 2 * LANES), BF16),
        ),
        in_specs=[hbm] * 13,
        out_specs=(vmem,) * 4,
        scratch_shapes=[
            V((TOK, CH), BF16), V((TOK, CH), BF16), V((CONV, CH), F32), V((1, CH), F32), V((CH, RANK), BF16),
            V((LANES, CH), BF16), V((RANK, CH), BF16), V((1, CH), F32), V((ST, CH), F32), V((1, CH), F32),
            V((TOK, 2 * LANES), BF16), V((1, KEEP), jnp.int32), V((1, KEEP), jnp.int32), V((ST, 2 * LANES), F32),
            V((32, LANES), BF16), V((32, LANES), BF16), V((32, LANES), F32), V((TOK + 16, CH), F32), V((TOK, CH), BF16),
            V((TOK, RANK + LANES), BF16), V((TOK, RANK + LANES), BF16), V((TOK, RANK + LANES), BF16), V((16, RANK + LANES), BF16), V((TOK, RANK + LANES), BF16),
            V((TOK * TILES, LANES), F32), V((TOK * TILES, LANES), F32), V((TOK // 8, 8, 2 * ST * LANES), F32),
            V((ST * TILES, LANES), F32), V((ST * TILES, LANES), F32), V((ST * TILES, LANES), F32),
            V((TOK * TILES, LANES), F32), V((TILES, LANES), F32),
            V((TILES, 1, LANES), F32), V((NZ, 2, 1, LANES), F32), V((ST * TILES, LANES), BF16), V((NZ * 32, LANES), BF16),
            V((2, 1, LANES), F32), V((NX - 1, TILES, 1, LANES), F32), V((NZ, 2, 1, LANES), F32), V((TILES, 1, LANES), F32),
            V((32, LANES), BF16), V((NX - 1, 128, LANES), BF16), V((NZ * 32, LANES), BF16), V((128, LANES), BF16),
            V((NZ * 32, LANES), F32), V((128, LANES), F32), V(((NX - 1) * 128, LANES), F32),
            V((128, LANES), F32),
            V((256, LANES), BF16), V((256, LANES), BF16), V((TOK, 2 * LANES), BF16),
            pltpu.SemaphoreType.DMA((15,)),
            pltpu.SemaphoreType.DMA((16,)), pltpu.SemaphoreType.DMA((16,)),
            pltpu.SemaphoreType.REGULAR((4,)),
        ],
        compiler_params=pltpu.CompilerParams(
            collective_id=0, has_side_effects=True, vmem_limit_bytes=40_000_000
        ),
    )(*map(pin, (
        x_in, gate_in, conv_weight, conv_bias.reshape(1, CH), proj_low, proj_bc.T, dt_weight, dt_bias.reshape(1, CH),
        decay_log, skip_gain.reshape(1, CH), attn_kv, kept_index, kept_owner.reshape(1, KEEP),
    )))
    return pl.pallas_call(
        finish,
        out_shape=(jax.ShapeDtypeStruct((TOK, CH), BF16), jax.ShapeDtypeStruct((1, TOK, 2 * LANES), BF16)),
        in_specs=[vmem] * 4,
        out_specs=(hbm, hbm),
        scratch_shapes=[
            V((TOK * TILES, LANES), F32), V((TOK, CH), BF16), pltpu.SemaphoreType.DMA((PARTS + 1,)),
        ],
        compiler_params=pltpu.CompilerParams(vmem_limit_bytes=20_000_000),
    )(*parts)


def solution(mesh):
    return jax.shard_map(
        local,
        mesh=mesh,
        in_specs=(
            P("ctx", "ch"), P("ctx", "ch"), P(None, "ch"), P("ch"), P("ch", None), P("ch", None), P(None, "ch"),
            P("ch"), P(None, "ch"), P("ch"), P("ctx", "ch"), P("ch", "ctx"), P("ch", "ctx", None),
        ),
        out_specs=(P("ctx", "ch"), P("ch", "ctx", None)),
        check_vma=False,
    )
```
